32 devices in a mesh: dp: 2 (over x), expert: 16 (over z, y, core).
Axes of the slice: x: 2, y: 2, z: 4, core: 2. Of those that a mesh axis runs over, the one named last changes fastest.
Arguments:
- hidden_in: bfloat16 [4096, 1536], P(('dp', 'expert')), may hold values from -6 to 6
- cotangent: bfloat16 [4096, 1536], P(('dp', 'expert')), may hold values from -6 to 6
- routes: int32 [4096, 6], P(('dp', 'expert')), may hold values from 0 to 63, all different within a row; in each aligned block of 128 rows (0 to 127, 128 to 255, ...) at most 24 rows name the same one
- route_gates: float32 [4096, 6], P(('dp', 'expert')), may hold values from 0.1 to 0.3
- lengths: int32 [32, 3], P(('dp', 'expert')), may hold values from 1 to 64, 128 in all within a row
- in_proj: bfloat16 [1536, 6448], P(('dp', 'expert')), may hold values from -0.15625 to 0.15625
- out_proj: bfloat16 [3072, 1536], P(('dp', 'expert')), may hold values from -0.109375 to 0.109375
- conv_weight: bfloat16 [3328, 4], P(('dp', 'expert')), may hold values from -3 to 3
- conv_bias: bfloat16 [3328], P(('dp', 'expert')), may hold values from -0.5 to 0.5
- norm_gain: bfloat16 [1536], P(('dp', 'expert')), may hold values from 0.5 to 1.5
- mix_gain: bfloat16 [3072], P(('dp', 'expert')), may hold values from 0.5 to 1.5
- ffn_gain: bfloat16 [1536], P(('dp', 'expert')), may hold values from 0.5 to 1.5
- shared_gate: bfloat16 [1536, 1024], P(('dp', 'expert')), may hold values from -0.15625 to 0.15625
- shared_up: bfloat16 [1536, 1024], P(('dp', 'expert')), may hold values from -0.15625 to 0.15625
- shared_down: bfloat16 [1024, 1536], P(('dp', 'expert')), may hold values from -0.1875 to 0.1875
- expert_gate: bfloat16 [64, 1536, 512], P('expert', 'dp'), may hold values from -0.15625 to 0.15625
- expert_up: bfloat16 [64, 1536, 512], P('expert', 'dp'), may hold values from -0.15625 to 0.15625
- expert_down: bfloat16 [64, 512, 1536], P('expert', 'dp'), may hold values from -0.25 to 0.25
- decay_log: float32 [48], replicated, may hold values from 0 to 2.77
- step_bias: float32 [48], replicated, may hold values from -5 to -1
- skip_gain: float32 [48], replicated, may hold values from 0.5 to 1.5
Outputs:
- output: bfloat16 [4096, 1536], P(('dp', 'expert'))
- grad_input: float32 [4096, 1536], P(('dp', 'expert'))
- grad_in_proj: float32 [1536, 6448], P(('dp', 'expert'))
- grad_out_proj: float32 [3072, 1536], P(('dp', 'expert'))
- grad_conv_weight: float32 [3328, 4], P(('dp', 'expert'))
- grad_conv_bias: float32 [3328], P(('dp', 'expert'))
- grad_norm_gain: float32 [1536], P(('dp', 'expert'))
- grad_mix_gain: float32 [3072], P(('dp', 'expert'))
- grad_ffn_gain: float32 [1536], P(('dp', 'expert'))
- grad_shared_gate: float32 [1536, 1024], P(('dp', 'expert'))
- grad_shared_up: float32 [1536, 1024], P(('dp', 'expert'))
- grad_shared_down: float32 [1024, 1536], P(('dp', 'expert'))
- grad_expert_gate: float32 [64, 1536, 512], P('expert', 'dp')
- grad_expert_up: float32 [64, 1536, 512], P('expert', 'dp')
- grad_expert_down: float32 [64, 512, 1536], P('expert', 'dp')
- grad_decay_log: float32 [48], replicated
- grad_step_bias: float32 [48], replicated
- grad_skip_gain: float32 [48], replicated
The draws below stay inside these ranges and needn't reach their ends.
Inputs may be any that keep to these rules, and one draw needn't show every extreme that they name: `routes`: within the rows of one device (128 tokens), no expert is named more than 24 times, a bound that some block reaches; a token's 6 experts differ. `lengths`: each device's row sums to 128; the last entry is the unused tail.
All inputs are finite; a program needn't handle non-finite values.
Results may differ from the reference program's by a relative error of at most 0.0091.
Values may be sent and summed in bfloat16 or wider, within the bound.
No kernel may reach another device: no remote copies, remote signals or barrier semaphores. Data moves between devices by JAX's collectives and lax.ppermute only.
A program may use at most 448 MiB of HBM per device.

```python
import math
import jax
import jax.numpy as jnp
import numpy as np
from jax import lax

D = 1536
HEADS = 48
HEAD_DIM = 64
STATE = 128
KERNEL = 4
SH = 1024
FF_E = 512
TOPK = 6
SEQ_SLOTS = 3
TOK_DEV = 128
INNER = 3072
CONV_CH = 3328
PROJ = 6448
EXPERTS = 64
CAP = 24
TOKENS = 4096
DEVICES = 32


def levels(rng, shape, shards, low, high):
    factor_of = 1.0
    for dim, shards_of in shards:
        draws = jax.random.uniform(jax.random.fold_in(jax.random.fold_in(rng, 6), dim), (shards_of,), jnp.float32, low / len(shards), high / len(shards))
        factor_of = factor_of * jnp.repeat(jnp.exp(draws), shape[dim] // shards_of).reshape((-1,) + (1,) * (len(shape) - 1 - dim))
    return factor_of


def split_up(amount, total, bound, skew):
    portions = [(1 << 20) // math.isqrt(standing ** skew) + 1 for standing in range(2, amount + 1)]
    spare, holding = total - bound - (amount - 1), [1] * (amount - 1)
    while spare > 0:
        movable = [i for i in range(amount - 1) if holding[i] < bound]
        pool, budget = sum([portions[i] for i in movable]), spare
        for i in movable:
            addition = min(bound - holding[i], max(1, budget * portions[i] // pool), spare)
            holding[i] = holding[i] + addition
            spare = spare - addition
    return np.array([bound] + holding)


def uneven_parts(key, amount, total, limit, lean):
    if amount == 2:
        one = jax.random.randint(key, (), max(1, total - limit), min(limit, total - 1) + 1)
        return jnp.stack([one, total - one])
    tallies = jnp.asarray(split_up(amount, total, limit, lean), jnp.int32)
    twos = (amount - 1) // 2
    source_of, receiver = tallies[1:1 + 2 * twos:2], tallies[2:2 + 2 * twos:2]
    room = jnp.minimum(source_of - 1, limit - receiver)
    moved = jax.random.randint(jax.random.fold_in(key, 1), (twos,), 0, 1 << 20) % (room + 1)
    tallies = tallies.at[1:1 + 2 * twos:2].set(source_of - moved).at[2:2 + 2 * twos:2].set(receiver + moved)
    return tallies[jax.random.permutation(jax.random.fold_in(key, 2), amount)]


def routed_block(rng, own, number, rows, count, top, limit, skew):
    ranking = jax.random.permutation(rng, count)
    heavy_load, common = shares(count, rows * top, limit, skew, True), shares(count, rows * top, limit, skew, False)
    places = jnp.arange(count)

    def named(tallies, rotation):
        used = int((tallies > 0).sum())
        fixed = max(1, used // 4)
        passed = fixed + (places - fixed + rotation * (used - fixed)) % max(1, count - fixed)
        return jnp.zeros((count,), jnp.int32).at[ranking[jnp.where(places < fixed, places, passed)]].set(jnp.asarray(tallies, jnp.int32))

    tallies = jnp.where(number % 4 == 0, named(heavy_load, number // 4), named(common, number - number // 4 - 1))
    mixed = jax.random.permutation(jax.random.fold_in(own, 3), count)
    giver, receiver = mixed[0:count // 2 * 2:2], mixed[1:count // 2 * 2:2]
    slack = jnp.minimum(tallies[giver] - 1, limit - tallies[receiver]) // 2
    slack = jnp.where((giver == ranking[0]) | (receiver == ranking[0]) | (tallies[receiver] == 0), 0, jnp.maximum(slack, 0))
    passed = jax.random.randint(jax.random.fold_in(own, 4), (count // 2,), 0, 1 << 20) % (slack + 1)
    tallies = tallies.at[giver].add(-passed).at[receiver].add(passed)
    members = jnp.searchsorted(jnp.cumsum(tallies), jnp.arange(rows * top), side="right").astype(jnp.int32)
    listing = members.reshape(top, rows).T
    listing = listing[jax.random.permutation(jax.random.fold_in(own, 1), rows)]
    rotation = jax.random.randint(jax.random.fold_in(own, 2), (rows, 1), 0, top)
    return jnp.take_along_axis(listing, (jnp.arange(top)[None, :] + rotation) % top, axis=1)


def shares(amount, total, bound, slope, full):
    portions = [(1 << 20) // math.isqrt(grade ** slope) + 1 for grade in range(1, amount + 1)]
    largest = bound if full else min(bound, max(-(-total // amount), total * portions[0] // sum(portions)))
    least = 1 if total - largest >= amount - 1 else 0
    given, rest = [largest] + [least] * (amount - 1), total - largest - least * (amount - 1)
    while rest > 0:
        movable = [i for i in range(1, amount) if given[i] < largest] or [i for i in range(1, amount) if given[i] < bound]
        mass, budget = sum([portions[i] for i in movable]), rest
        for i in movable:
            addition = min(bound - given[i], max(1, budget * portions[i] // mass), rest)
            given[i] = given[i] + addition
            rest = rest - addition
    return np.array(given)


def gaussian(rng, dims, deviation, bound, shards=(), held_as=jnp.bfloat16):
    values = deviation * jax.random.normal(rng, dims, jnp.float32)
    if shards:
        values = values * levels(rng, dims, shards, -0.22, 0.18)
    return jnp.clip(values, -bound, bound).astype(held_as)


def setup_inputs(seed: int = 0) -> dict:
    splits = jax.random.split(jax.random.key(seed), 22)
    hidden_in = gaussian(splits[0], (TOKENS, D), 1.0, 6.0, ((0, 32),))
    cotangent = gaussian(splits[1], (TOKENS, D), 1.0, 6.0, ((0, 32),))
    routes_keys = jax.random.split(jax.random.fold_in(splits[2], 1), TOKENS // TOK_DEV)
    routes_turns = jax.random.permutation(jax.random.fold_in(splits[2], 3), TOKENS // TOK_DEV)
    routes = jax.vmap(lambda own, number: routed_block(jax.random.fold_in(splits[2], 2), own, number, TOK_DEV, EXPERTS, TOPK, CAP, 2))(routes_keys, routes_turns).reshape((TOKENS, TOPK))
    route_gates = jnp.clip(jnp.exp(math.log(0.3) - 1.0986123 * jax.random.uniform(splits[3], (TOKENS, TOPK), jnp.float32) ** levels(splits[3], (TOKENS, TOPK), ((0, 32),), -0.2, 0.2)), 0.1, 0.3)
    lengths = jax.vmap(lambda own: uneven_parts(own, SEQ_SLOTS, TOK_DEV, TOK_DEV // 2, 2))(jax.random.split(splits[4], DEVICES)).reshape((DEVICES, SEQ_SLOTS)).astype(jnp.int32)
    in_proj = gaussian(splits[5], (D, PROJ), D ** -0.5, 0.15625, ((0, 32),))
    out_proj = gaussian(splits[6], (INNER, D), INNER ** -0.5, 0.109375, ((0, 32),))
    conv_weight = gaussian(splits[7], (CONV_CH, KERNEL), KERNEL ** -0.5, 3.0, ((0, 32),))
    conv_bias = jnp.clip(jax.random.uniform(splits[8], (CONV_CH,), jnp.float32, -0.5, 0.5) * levels(splits[8], (CONV_CH,), ((0, 32),), -0.4, 0.0), -0.5, 0.5).astype(jnp.bfloat16)
    norm_gain = jnp.clip(1.0 + 0.1 * jax.random.normal(splits[9], (D,), jnp.float32), 0.5, 1.5).astype(jnp.bfloat16)
    mix_gain = jnp.clip(1.0 + 0.1 * jax.random.normal(splits[10], (INNER,), jnp.float32), 0.5, 1.5).astype(jnp.bfloat16)
    ffn_gain = jnp.clip(1.0 + 0.1 * jax.random.normal(splits[11], (D,), jnp.float32), 0.5, 1.5).astype(jnp.bfloat16)
    shared_gate = gaussian(splits[12], (D, SH), D ** -0.5, 0.15625, ((0, 32),))
    shared_up = gaussian(splits[13], (D, SH), D ** -0.5, 0.15625, ((0, 32),))
    shared_down = gaussian(splits[14], (SH, D), SH ** -0.5, 0.1875, ((0, 32),))
    expert_gate = gaussian(splits[15], (EXPERTS, D, FF_E), D ** -0.5, 0.15625, ((0, 16), (1, 2)))
    expert_up = gaussian(splits[16], (EXPERTS, D, FF_E), D ** -0.5, 0.15625, ((0, 16), (1, 2)))
    expert_down = gaussian(splits[17], (EXPERTS, FF_E, D), FF_E ** -0.5, 0.25, ((0, 16), (1, 2)))
    decay_log = jnp.clip(jax.random.uniform(splits[18], (HEADS,), jnp.float32, 0.0, 2.77), 0.0, 2.77)
    step_bias = jnp.clip(jax.random.uniform(splits[19], (HEADS,), jnp.float32, -5.0, -1.0), -5.0, -1.0)
    skip_gain = jnp.clip(jax.random.uniform(splits[20], (HEADS,), jnp.float32, 0.5, 1.5), 0.5, 1.5)
    return {"hidden_in": hidden_in, "cotangent": cotangent, "routes": routes, "route_gates": route_gates, "lengths": lengths, "in_proj": in_proj, "out_proj": out_proj, "conv_weight": conv_weight, "conv_bias": conv_bias, "norm_gain": norm_gain, "mix_gain": mix_gain, "ffn_gain": ffn_gain, "shared_gate": shared_gate, "shared_up": shared_up, "shared_down": shared_down, "expert_gate": expert_gate, "expert_up": expert_up, "expert_down": expert_down, "decay_log": decay_log, "step_bias": step_bias, "skip_gain": skip_gain}


@jax.custom_vjp
def low(v):
    return lax.optimization_barrier(v.astype(jnp.bfloat16)).astype(jnp.float32)

@jax.custom_vjp
def low_back(v):
    return v

def low_keep(v):
    return (low(v), None)

def low_pass(kept, grad):
    return (grad,)

def back_keep(v):
    return (v, None)

def back_low(kept, grad):
    return (low(grad),)
low.defvjp(low_keep, low_pass)
low_back.defvjp(back_keep, back_low)
epsilon = 1e-05

def matmul(left, right):
    return jnp.dot(left, right, precision=lax.Precision.HIGHEST, preferred_element_type=jnp.float32)

def rms_norm(value_entries, gain):
    return value_entries * lax.rsqrt(lax.optimization_barrier(jnp.mean(value_entries * value_entries, axis=-1, keepdims=True)) + epsilon) * gain

def segment_ids(lengths_row, count):
    bounds = jnp.cumsum(lengths_row).astype(jnp.int32)
    position = jnp.arange(count, dtype=jnp.int32)
    return lax.optimization_barrier(jnp.sum((position[:, None] >= bounds[None, :SEQ_SLOTS - 1]).astype(jnp.int32), axis=1)).astype(jnp.int32)

def mixer_core(projected, segment, conv_weight, conv_bias, step_bias, decay_log, skip_gain, mix_gain):
    count = projected.shape[0]
    gate_z = projected[:, :INNER]
    conv_in = projected[:, INNER:INNER + CONV_CH]
    step_raw = projected[:, INNER + CONV_CH:]
    total = conv_bias[None, :] + conv_weight[:, KERNEL - 1][None, :] * conv_in
    for offset in range(1, KERNEL):
        shifted = jnp.concatenate([jnp.zeros((offset, CONV_CH), conv_in.dtype), conv_in[:count - offset]], axis=0)
        earlier = jnp.concatenate([jnp.full((offset,), -1, jnp.int32), segment[:count - offset]], axis=0)
        same_run = (earlier == segment).astype(conv_in.dtype)
        total = total + conv_weight[:, KERNEL - 1 - offset][None, :] * shifted * same_run[:, None]
    conv_out = jax.nn.silu(total)
    value_entries = conv_out[:, :INNER].reshape(count, HEADS, HEAD_DIM)
    state_in = conv_out[:, INNER:INNER + STATE]
    state_out = conv_out[:, INNER + STATE:]
    step_size = jax.nn.softplus(step_raw + step_bias[None, :])
    decay_rate = -jnp.exp(decay_log)
    cumul = jnp.cumsum(step_size * decay_rate[None, :], axis=0)
    position = jnp.arange(count, dtype=jnp.int32)
    causal = (position[:, None] >= position[None, :]) & (segment[:, None] == segment[None, :])
    spread = cumul.T[:, :, None] - cumul.T[:, None, :]
    decay = jnp.exp(jnp.where(causal[None, :, :], spread, -jnp.inf))
    scores = matmul(state_out, state_in.T)
    mixing = decay * scores[None, :, :] * step_size.T[:, None, :]
    scan_out = jnp.einsum('hij,jhp->ihp', mixing, value_entries, precision=lax.Precision.HIGHEST)
    scan_out = scan_out + skip_gain[None, :, None] * value_entries
    gated = scan_out.reshape(count, INNER) * jax.nn.silu(gate_z)
    return rms_norm(gated, mix_gain)

def reference(hidden_in, cotangent, routes, route_gates, lengths, in_proj, out_proj, conv_weight, conv_bias, norm_gain, mix_gain, ffn_gain, shared_gate, shared_up, shared_down, expert_gate, expert_up, expert_down, decay_log, step_bias, skip_gain):
    segments = jax.vmap(lambda lengths_row: segment_ids(lengths_row, TOK_DEV))(lengths)
    live = (segments < SEQ_SLOTS - 1).astype(jnp.float32).reshape(TOKENS, 1)
    flat_routes = routes.reshape(DEVICES, TOK_DEV * TOPK).astype(jnp.int32)
    onehot = (flat_routes[:, :, None] == jnp.arange(EXPERTS, dtype=jnp.int32)[None, None, :]).astype(jnp.int32)
    ranks = lax.optimization_barrier(jnp.sum((jnp.cumsum(onehot, axis=1) - 1) * onehot, axis=2)).astype(jnp.int32)
    anchor = jnp.arange(DEVICES, dtype=jnp.int32)[:, None]
    slots = (flat_routes * (DEVICES * CAP) + anchor * CAP + ranks).reshape(-1).astype(jnp.int32)
    owners = (jnp.arange(TOKENS * TOPK, dtype=jnp.int32) // TOPK).astype(jnp.int32)
    expert_slot_rows = jnp.zeros((EXPERTS * DEVICES * CAP,), jnp.int32).at[slots].set(owners).reshape(EXPERTS, DEVICES * CAP)
    gate_values = route_gates.astype(jnp.float32)

    def forward_pass_fn(input_rows, input_projection_weight, output_projection_weight, convolution_weight_matrix, convolution_bias_vector, final_norm_weight, mixer_norm_weight, feedforward_norm_weight, shared_gate_weight, shared_up_weight, shared_down_weight, expert_gate_weight, expert_raise_weight, expert_down_weight, decay_parameter, step_parameter, skip_parameter):
        normed = low(rms_norm(input_rows, final_norm_weight))
        projected = low_back(matmul(normed, input_projection_weight))

        def one_block(pair):
            return mixer_core(pair[0], pair[1], convolution_weight_matrix, convolution_bias_vector, step_parameter, decay_parameter, skip_parameter, mixer_norm_weight)
        mixed = lax.map(jax.checkpoint(one_block), (projected.reshape(DEVICES, TOK_DEV, PROJ), segments))
        mixed = low(mixed.reshape(TOKENS, INNER))
        mixer_out = low_back(matmul(mixed, output_projection_weight))
        resid = input_rows + live * mixer_out
        ffn_in = low(rms_norm(resid, feedforward_norm_weight))
        shared_g = low_back(matmul(ffn_in, shared_gate_weight))
        shared_u = low_back(matmul(ffn_in, shared_up_weight))
        shared_out = low_back(matmul(low(jax.nn.silu(shared_g) * shared_u), shared_down_weight))

        def single_expert_apply(items):
            picked, gate_w, up_w, down_w = items
            taken = low_back(ffn_in[picked])
            hidden_g = low_back(matmul(taken, gate_w))
            hidden_u = low_back(matmul(taken, up_w))
            return low_back(low(matmul(low(jax.nn.silu(hidden_g) * hidden_u), down_w)))
        produced_rows = lax.map(jax.checkpoint(single_expert_apply), (expert_slot_rows, expert_gate_weight, expert_raise_weight, expert_down_weight))
        routed_rows = produced_rows.reshape(EXPERTS * DEVICES * CAP, D)[slots].reshape(TOKENS, TOPK, D)
        routed = lax.optimization_barrier(jnp.sum(routed_rows * gate_values[:, :, None], axis=1))
        return resid + live * (shared_out + routed)
    primals = (hidden_in, in_proj, out_proj, conv_weight, conv_bias, norm_gain, mix_gain, ffn_gain, shared_gate, shared_up, shared_down, expert_gate, expert_up, expert_down, decay_log, step_bias, skip_gain)
    primals = tuple((item.astype(jnp.float32) for item in primals))
    result, pullback = jax.vjp(forward_pass_fn, *primals)
    grads = pullback(cotangent.astype(jnp.float32))
    return (result.astype(jnp.bfloat16), grads[0], grads[1], grads[2], grads[3], grads[4], grads[5], grads[6], grads[7], grads[8], grads[9], grads[10], grads[11], grads[12], grads[13], grads[14], grads[15], grads[16])
```

```python
import jax
import jax.numpy as jnp
from jax import lax
from jax.sharding import Mesh, PartitionSpec as P

HEADS = 48
HEAD_DIM = 64
STATE = 128
KERNEL = 4
SEQ_SLOTS = 3
INNER = 3072
CONV_CH = 3328
EXTRA = 128

epsilon = 1e-05
bf16 = jnp.bfloat16
f32 = jnp.float32
GROUP = ("z", "y", "core")
ALL = ("dp", "z", "y", "core")


def matmul(left, right, dims=None, precision=None):
    if dims is None:
        dims = (((left.ndim - 1,), (0,)), ((), ()))
    return lax.dot_general(left, right, dims, precision=precision, preferred_element_type=f32)


def swap(value, axis):
    return lax.ppermute(value, axis, [(0, 1), (1, 0)])


def ring(value):
    size = lax.axis_size("z")
    return lax.ppermute(value, "z", [(k, (k + 1) % size) for k in range(size)])


def split_three(value):
    high = lax.reduce_precision(value, 8, 7)
    rest = value - high
    middle = lax.reduce_precision(rest, 8, 7)
    return high.astype(bf16), middle.astype(bf16), (rest - middle).astype(bf16)


def join_three(parts):
    return parts[0].astype(f32) + parts[1].astype(f32) + parts[2].astype(f32)


def group_gather(block):
    size = lax.axis_size("z")
    current = block
    out = []
    for step in range(size):
        if step < size - 1:
            following, beside = lax.optimization_barrier((ring(current), swap(current, "y")))
        else:
            following, beside = None, swap(current, "y")
        out += [current, beside, swap(current, "core"), swap(beside, "core")]
        current = following
    return jnp.concatenate(out, axis=0)


def add_low(left, right):
    return (left.astype(f32) + right.astype(f32)).astype(bf16)


def group_scatter(parts):
    size = lax.axis_size("z")
    parts = parts.reshape((size, 2, 2, parts.shape[0] // (4 * size)) + parts.shape[1:])
    summed = {}
    for step in list(range(1, size)) + [0]:
        pair = add_low(parts[step, 0], swap(parts[step, 1], "core"))
        summed[step] = (pair[0], swap(pair[1], "y"))
    total = add_low(*summed[1])
    for step in range(2, size):
        total = add_low(ring(total), add_low(*summed[step]))
    own = summed[0]
    return ring(total).astype(f32) + own[0].astype(f32) + own[1].astype(f32)


def dp_gather_rows(value, axis):
    if lax.axis_size("dp") != 2:
        return lax.all_gather(value, "dp", axis=axis, tiled=True)
    other = swap(value, "dp")
    first = lax.axis_index("dp") == 0
    return jnp.concatenate(
        [jnp.where(first, value, other), jnp.where(first, other, value)], axis=axis
    )


def dp_scatter_rows(value, axis):
    count = lax.axis_size("dp")
    if count != 2:
        return lax.psum_scatter(value.astype(bf16), "dp", scatter_dimension=axis, tiled=True).astype(f32)
    place = lax.axis_index("dp")
    extent = value.shape[axis] // count
    sent = lax.dynamic_slice_in_dim(value, (1 - place) * extent, extent, axis).astype(bf16)
    kept = lax.dynamic_slice_in_dim(value, place * extent, extent, axis)
    return kept + swap(sent, "dp").astype(f32)


def mixer_core(proj, segment, conv_w, conv_b, step_bias, decay_log, skip_gain):
    blocks, count = segment.shape
    heads = step_bias.shape[0]
    own = heads * HEAD_DIM
    gate_z = proj[:, :own]
    conv_in = proj[:, own : 2 * own + 2 * STATE].reshape(blocks, count, own + 2 * STATE)
    step_raw = proj[:, 2 * own + 2 * STATE : 2 * own + 2 * STATE + heads]
    total = conv_b + conv_w[KERNEL - 1] * conv_in
    for offset in range(1, KERNEL):
        shifted = jnp.pad(conv_in[:, : count - offset], ((0, 0), (offset, 0), (0, 0)))
        earlier = jnp.pad(segment[:, : count - offset], ((0, 0), (offset, 0)), constant_values=-1)
        same = (earlier == segment).astype(f32)[:, :, None]
        total = total + conv_w[KERNEL - 1 - offset] * (shifted * same)
    conv_out = jax.nn.silu(total)
    values = conv_out[:, :, :own].reshape(blocks, count, heads, HEAD_DIM).transpose(0, 2, 1, 3)
    state_in = conv_out[:, :, own : own + STATE]
    state_out = conv_out[:, :, own + STATE :]
    step = jax.nn.softplus(step_raw + step_bias).reshape(blocks, count, heads).transpose(0, 2, 1)
    rate = -jnp.exp(decay_log)
    cumul = jnp.cumsum(step * rate[None, :, None], axis=2)
    position = jnp.arange(count, dtype=jnp.int32)
    causal = (position[:, None] >= position[None, :]) & (segment[:, :, None] == segment[:, None, :])
    spread = cumul[:, :, :, None] - cumul[:, :, None, :]
    decay = jnp.exp(jnp.where(causal[:, None], spread, -jnp.inf))
    high = lax.Precision.HIGHEST
    scores = jnp.einsum("bin,bjn->bij", state_out, state_in, precision=high)
    mixing = decay * scores[:, None] * step[:, :, None, :]
    scan = jnp.einsum("bhij,bhjp->bhip", mixing, values, precision=high)
    scan = scan + skip_gain[None, :, None, None] * values
    scan = scan.transpose(0, 2, 1, 3).reshape(blocks * count, own)
    return scan * jax.nn.silu(gate_z)


def local(
    hidden_in,
    cotangent,
    routes,
    route_gates,
    lengths,
    in_proj,
    out_proj,
    conv_weight,
    conv_bias,
    norm_gain,
    mix_gain,
    ffn_gain,
    shared_gate,
    shared_up,
    shared_down,
    expert_gate,
    expert_up,
    expert_down,
    decay_log,
    step_bias,
    skip_gain,
):
    tokens, width = hidden_in.shape
    top = routes.shape[1]
    replicas = lax.axis_size("dp")
    groups = lax.axis_size("z") * 4
    devices = replicas * groups
    core = lax.axis_index("core")
    column = lax.axis_index("z") * 2 + lax.axis_index("y")
    place = column * 2 + core
    heads = HEADS // groups
    own = heads * HEAD_DIM
    half = groups // 2
    rows_in = in_proj.shape[0]
    hidden_units = shared_gate.shape[1]
    unit = hidden_units // devices
    units = hidden_units // groups
    local_experts = expert_gate.shape[0]
    capacity = 2 * tokens * top // (local_experts * groups)
    first_head = core * (HEADS // 2) + column * heads
    first_channel = first_head * HEAD_DIM

    small = (conv_weight.reshape(-1), conv_bias, norm_gain, mix_gain, ffn_gain)
    small_sizes = [entry.shape[0] for entry in small]
    small_lanes = -(-sum(small_sizes) // rows_in)
    small_flat = jnp.concatenate(small)
    small_flat = jnp.pad(small_flat, (0, small_lanes * rows_in - small_flat.shape[0]))

    def by_place(block):
        block = block.reshape(rows_in, 2, half, own).transpose(2, 1, 0, 3)
        return block.reshape(groups, rows_in, own)

    def by_unit(block):
        block = block.reshape(rows_in, replicas, groups, unit).transpose(2, 0, 1, 3)
        return block.reshape(groups, rows_in, units)

    def to_all(block):
        return jnp.broadcast_to(block[None], (groups,) + block.shape)

    step_columns = in_proj[:, INNER + CONV_CH :].reshape(rows_in, 2, half, heads).transpose(2, 1, 0, 3)
    step_columns = step_columns.reshape(groups, rows_in, heads)
    spare = EXTRA - heads - small_lanes
    pack = jnp.concatenate(
        [
            by_place(in_proj[:, :INNER]),
            by_place(in_proj[:, INNER : 2 * INNER]),
            to_all(in_proj[:, 2 * INNER : INNER + CONV_CH]),
            step_columns,
            to_all(small_flat.reshape(rows_in, small_lanes)),
            jnp.zeros((groups, rows_in, spare), bf16),
            by_unit(shared_gate),
            by_unit(shared_up),
        ],
        axis=2,
    )
    proj_lanes = 2 * own + 2 * STATE + EXTRA
    pack = lax.all_to_all(pack, GROUP, split_axis=0, concat_axis=0, tiled=True)
    pack = dp_gather_rows(pack.reshape(1, groups * rows_in, pack.shape[2]), 0)
    pack = pack.reshape(devices * rows_in, pack.shape[2])
    small_at = 2 * own + 2 * STATE + heads
    small_all = pack[:, small_at : small_at + small_lanes].reshape(devices, rows_in * small_lanes)
    pieces = []
    start = 0
    for size in small_sizes:
        pieces.append(small_all[:, start : start + size].reshape(-1).astype(f32))
        start += size
    conv_w_all = pieces[0].reshape(CONV_CH, KERNEL).T
    conv_b_all, norm_gain_all, mix_gain_all, ffn_gain_all = pieces[1:]
    lane = jnp.arange(proj_lanes)
    w_in = jnp.where(lane < small_at, pack[:, :proj_lanes], jnp.zeros((), bf16))
    w_shared = pack[:, proj_lanes:]

    def own_channels(rows):
        return lax.dynamic_slice_in_dim(rows, first_channel, own, rows.ndim - 1)

    conv_w = jnp.concatenate([own_channels(conv_w_all), conv_w_all[:, INNER:]], axis=1)
    conv_b = jnp.concatenate([own_channels(conv_b_all), conv_b_all[INNER:]])
    own_mix_gain = own_channels(mix_gain_all)

    def own_heads(row):
        return lax.dynamic_slice_in_dim(row, first_head, heads, 0)

    if replicas == 2:
        both = swap(out_proj, "core")
        both = jnp.concatenate(
            [jnp.where(core == 0, out_proj, both), jnp.where(core == 0, both, out_proj)]
        )
        w_out = jnp.where(lax.axis_index("dp") == core, both, swap(both, "dp"))
    else:
        w_out = lax.dynamic_slice_in_dim(
            lax.all_gather(out_proj, ALL, axis=0, tiled=True), first_channel, own, 0
        )
    w_shared_down = dp_gather_rows(shared_down[None], 0).reshape(units, width)

    bounds = jnp.cumsum(lengths[0])
    slot = jnp.arange(tokens, dtype=jnp.int32)
    run = jnp.sum((slot[:, None] >= bounds[None, : SEQ_SLOTS - 1]).astype(jnp.int32), axis=1)
    live = (run < SEQ_SLOTS - 1).astype(f32)[:, None]
    beside = [run.astype(bf16)[:, None], routes.astype(bf16), *split_three(route_gates)]
    beside = jnp.concatenate(beside, axis=1)
    beside = jnp.pad(beside, ((0, 0), (0, EXTRA - beside.shape[1])))
    gathered = group_gather(jnp.concatenate([hidden_in, beside], axis=1))
    hidden_all = gathered[:, :width]
    segment = gathered[:, width].astype(jnp.int32).reshape(groups, tokens)
    at = width + 1
    routes_all = gathered[:, at : at + top].astype(jnp.int32)
    gates_all = join_three([gathered[:, at + k * top : at + (k + 1) * top] for k in (1, 2, 3)])

    w_gate = dp_gather_rows(expert_gate, 1)
    w_up = dp_gather_rows(expert_up, 1)
    w_down = dp_gather_rows(expert_down, 1)

    rows = hidden_all.astype(f32)
    normed = rows * lax.rsqrt(jnp.mean(rows * rows, axis=1, keepdims=True) + epsilon) * norm_gain_all
    normed = normed.astype(bf16)
    proj = matmul(normed, w_in)
    gated, core_back = jax.vjp(
        lambda *args: mixer_core(args[0], segment, *args[1:]),
        proj,
        conv_w,
        conv_b,
        own_heads(step_bias),
        own_heads(decay_log),
        own_heads(skip_gain),
    )
    scaled = (gated * own_mix_gain).astype(bf16)
    squares = (gated * gated).astype(bf16)
    fold = (jnp.arange(own)[:, None] % EXTRA == jnp.arange(EXTRA)[None, :]).astype(bf16)
    w_out_fold = jnp.concatenate(
        [jnp.pad(w_out, ((0, 0), (0, EXTRA))), jnp.pad(fold, ((0, 0), (width, 0)))], axis=0
    )
    mixed_part = matmul(jnp.concatenate([scaled, squares], axis=1), w_out_fold).astype(bf16)
    mixed_sum = group_scatter(mixed_part)
    mix_rms = lax.rsqrt(jnp.sum(mixed_sum[:, width:], axis=1, keepdims=True) / INNER + epsilon)
    mixer_out = mixed_sum[:, :width] * mix_rms
    input_rows = hidden_in.astype(f32)
    resid = input_rows + live * mixer_out
    ffn_rms = lax.rsqrt(jnp.mean(resid * resid, axis=1, keepdims=True) + epsilon)
    ffn_hat = resid * ffn_rms
    ffn_all = group_gather((ffn_hat * ffn_gain_all).astype(bf16))
    grad_out = cotangent.astype(f32)
    branch = (grad_out * live).astype(bf16)
    branch_all = group_gather(branch)

    shared_gu = matmul(ffn_all, w_shared)

    def swiglu(both):
        extent = both.shape[-1] // 2
        return jax.nn.silu(both[..., :extent]) * both[..., extent:]

    shared_act, shared_back = jax.vjp(swiglu, shared_gu)
    shared_low = shared_act.astype(bf16)
    grad_shared_down = matmul(shared_low, branch_all, (((0,), (0,)), ((), ())))
    (grad_shared_gu,) = shared_back(matmul(branch_all, w_shared_down, (((1,), (1,)), ((), ()))))
    shared_gu_low = grad_shared_gu.astype(bf16)
    grad_shared_w = matmul(ffn_all, shared_gu_low, (((0,), (0,)), ((), ())))

    pairs = groups // 2
    pair_tokens = 2 * tokens
    pair_slots = 2 * capacity
    lanes = pairs * pair_slots
    numbers = place * local_experts + jnp.arange(local_experts, dtype=jnp.int32)
    named = routes_all[:, None, :] == numbers[None, :, None]
    member = jnp.any(named, axis=2).T.reshape(local_experts, pairs, pair_tokens)
    weight = jnp.sum(jnp.where(named, gates_all[:, None, :], 0.0), axis=2).T
    weight = weight.reshape(local_experts, pairs, pair_tokens)
    below = jnp.triu(jnp.ones((pair_tokens, pair_tokens), bf16))
    rank = matmul(member.astype(bf16), below)
    rank = jnp.where(member, rank.astype(jnp.int32) - 1, -1)
    chosen = rank[:, :, None, :] == jnp.arange(pair_slots, dtype=jnp.int32)[None, None, :, None]
    slot_weight = jnp.sum(jnp.where(chosen, weight[:, :, None, :], 0.0), axis=3)
    slot_weight = slot_weight.reshape(local_experts, lanes, 1)
    select = chosen.astype(bf16)

    def dispatch(values):
        values = values.reshape(pairs, pair_tokens, width)
        return jnp.einsum("ebrt,btd->ebrd", select, values, preferred_element_type=f32).reshape(
            local_experts, lanes, width
        )

    def combine(values):
        values = values.reshape(local_experts, pairs, pair_slots, width)
        return jnp.einsum("ebrt,ebrd->btd", select, values, preferred_element_type=f32).reshape(
            groups * tokens, width
        )

    batch = ((0,), (0,))
    expert_in = dispatch(ffn_all).astype(bf16)
    d_row = (dispatch(branch_all) * slot_weight).astype(bf16)
    hidden_g = matmul(expert_in, w_gate, (((2,), (1,)), batch))
    hidden_u = matmul(expert_in, w_up, (((2,), (1,)), batch))
    expert_act, expert_back = jax.vjp(lambda g, u: jax.nn.silu(g) * u, hidden_g, hidden_u)
    act_low = expert_act.astype(bf16)
    grad_g, grad_u = expert_back(matmul(d_row, w_down, (((2,), (2,)), batch)))
    g_low = grad_g.astype(bf16)
    u_low = grad_u.astype(bf16)
    d_in_row = matmul(g_low, w_gate, (((2,), (2,)), batch)) + matmul(
        u_low, w_up, (((2,), (2,)), batch)
    )
    grad_ffn_part = combine(d_in_row.astype(bf16)) + matmul(
        shared_gu_low, w_shared, (((1,), (1,)), ((), ()))
    )
    grad_ffn = group_scatter(grad_ffn_part.astype(bf16))
    grad_gate = matmul(expert_in, g_low, (((1,), (1,)), batch))
    grad_up = matmul(expert_in, u_low, (((1,), (1,)), batch))
    grad_down = matmul(act_low, d_row, (((1,), (1,)), batch))
    expert_row = (matmul(act_low, w_down, (((2,), (1,)), batch)) * slot_weight).astype(bf16)
    branch_part = combine(expert_row) + matmul(shared_low, w_shared_down)
    branch_sum = group_scatter(branch_part.astype(bf16))
    output = (resid + live * branch_sum).astype(bf16)
    grad_gate = dp_scatter_rows(grad_gate, 1)
    grad_up = dp_scatter_rows(grad_up, 1)
    grad_down = dp_scatter_rows(grad_down, 1)

    grad_ffn_gain = jnp.sum(grad_ffn * ffn_hat, axis=0)
    scaled_ffn = grad_ffn * ffn_gain_all
    grad_resid = grad_out + ffn_rms * (
        scaled_ffn - ffn_hat * jnp.mean(scaled_ffn * ffn_hat, axis=1, keepdims=True)
    )
    d_mixer = (grad_resid * live).astype(bf16).astype(f32)
    inner_term = jnp.sum(d_mixer * mixer_out, axis=1, keepdims=True) * mix_rms * mix_rms / INNER
    inner_pack = jnp.pad(jnp.concatenate(split_three(inner_term), axis=1), ((0, 0), (0, EXTRA - 3)))
    d_mixer_all = group_gather(jnp.concatenate([(d_mixer * mix_rms).astype(bf16), inner_pack], axis=1))
    inner_all = join_three([d_mixer_all[:, width + k : width + k + 1] for k in range(3)])
    d_mixer_all = d_mixer_all[:, :width]
    grad_mixed = matmul(d_mixer_all, w_out, (((1,), (1,)), ((), ())))
    grad_out_rows = matmul(scaled, d_mixer_all, (((0,), (0,)), ((), ())))
    grad_proj, grad_conv_w, grad_conv_b, grad_stepb, grad_decay, grad_skip = core_back(
        grad_mixed * own_mix_gain - gated * inner_all
    )
    proj_low = grad_proj.astype(bf16)
    grad_normed_part = matmul(proj_low, w_in, (((1,), (1,)), ((), ())))
    grad_normed = group_scatter(grad_normed_part.astype(bf16))
    grad_w_in = matmul(normed, proj_low, (((0,), (0,)), ((), ())))

    grad_pack = jnp.concatenate([grad_w_in, grad_shared_w], axis=1)
    grad_pack = dp_scatter_rows(grad_pack, 0).astype(bf16).reshape(groups, rows_in, -1)
    grad_pack = lax.all_to_all(grad_pack, GROUP, split_axis=0, concat_axis=0, tiled=True).astype(f32)

    def from_place(block):
        block = block.reshape(half, 2, rows_in, block.shape[2]).transpose(2, 1, 0, 3)
        return block.reshape(rows_in, -1)

    def from_unit(block):
        block = block.reshape(groups, rows_in, replicas, unit).transpose(1, 2, 0, 3)
        return block.reshape(rows_in, hidden_units)

    both_at = 2 * own + 2 * STATE
    grad_in_proj = jnp.concatenate(
        [
            from_place(grad_pack[:, :, :own]),
            from_place(grad_pack[:, :, own : 2 * own]),
            jnp.sum(grad_pack[:, :, 2 * own : both_at], axis=0),
            from_place(grad_pack[:, :, both_at : both_at + heads]),
        ],
        axis=1,
    )
    grad_shared_gate = from_unit(grad_pack[:, :, proj_lanes : proj_lanes + units])
    grad_shared_up = from_unit(grad_pack[:, :, proj_lanes + units :])
    grad_shared_down = dp_scatter_rows(grad_shared_down.reshape(replicas, unit, width), 0)[0]
    if replicas == 2:
        mine = lax.axis_index("dp") == core
        received = swap(grad_out_rows.astype(bf16), "dp").astype(f32)
        total = (grad_out_rows + received).reshape(2, own // 2, width)
        passed = swap(lax.dynamic_index_in_dim(total, 1 - core, 0, keepdims=False), "core")
        grad_out_proj = jnp.where(mine, lax.dynamic_index_in_dim(total, core, 0, keepdims=False), passed)
    else:
        full = jnp.zeros((INNER, width), f32)
        full = lax.dynamic_update_slice_in_dim(full, grad_out_rows, first_channel, 0)
        grad_out_proj = lax.psum_scatter(full, ALL, scatter_dimension=0, tiled=True)
    grad_mix_gain = jnp.sum(grad_out_proj * out_proj.astype(f32), axis=1) / mix_gain.astype(f32)
    grad_norm_gain = jnp.sum(grad_in_proj * in_proj.astype(f32), axis=1) / norm_gain.astype(f32)

    def to_owner(part):
        rows_part = jnp.zeros((part.shape[0], CONV_CH), f32)
        rows_part = lax.dynamic_update_slice_in_dim(rows_part, part[:, :own], first_channel, 1)
        rows_part = lax.dynamic_update_slice_in_dim(rows_part, part[:, own:], INNER, 1)
        return rows_part.reshape(part.shape[0], devices, -1).transpose(1, 0, 2).reshape(devices, -1)

    def head_row(part):
        return lax.dynamic_update_slice_in_dim(jnp.zeros((HEADS,), f32), part, first_head, 0)

    head_rows = jnp.concatenate([head_row(grad_decay), head_row(grad_stepb), head_row(grad_skip)])
    sums = jnp.concatenate(
        [
            to_owner(grad_conv_w),
            to_owner(grad_conv_b[None]),
            grad_ffn_gain.reshape(devices, -1),
            jnp.broadcast_to(head_rows[None], (devices, 3 * HEADS)),
        ],
        axis=1,
    )
    sums = lax.all_to_all(sums, ALL, split_axis=0, concat_axis=0, tiled=True)
    sums = jnp.sum(sums, axis=0)
    channels = CONV_CH // devices
    grad_conv_weight = sums[: KERNEL * channels].reshape(KERNEL, channels).T
    grad_conv_bias = sums[KERNEL * channels : (KERNEL + 1) * channels]
    at = (KERNEL + 1) * channels
    grad_ffn_gain = sums[at : at + rows_in]
    at += rows_in
    grad_decay, grad_stepb, grad_skip = (sums[at + k * HEADS : at + (k + 1) * HEADS] for k in range(3))

    in_rms = lax.rsqrt(jnp.mean(input_rows * input_rows, axis=1, keepdims=True) + epsilon)
    in_hat = input_rows * in_rms
    scaled_in = grad_normed * norm_gain_all
    grad_input = grad_resid + in_rms * (
        scaled_in - in_hat * jnp.mean(scaled_in * in_hat, axis=1, keepdims=True)
    )
    return (
        output,
        grad_input,
        grad_in_proj,
        grad_out_proj,
        grad_conv_weight,
        grad_conv_bias,
        grad_norm_gain,
        grad_mix_gain,
        grad_ffn_gain,
        grad_shared_gate,
        grad_shared_up,
        grad_shared_down,
        grad_gate,
        grad_up,
        grad_down,
        grad_decay,
        grad_stepb,
        grad_skip,
    )


def solution(mesh):
    replicas, groups = mesh.shape["dp"], mesh.shape["expert"]
    inner = Mesh(mesh.devices.reshape(replicas, groups // 4, 2, 2), ALL)
    flat = P(ALL)
    expert = P(GROUP, "dp", None)
    return jax.shard_map(
        local,
        mesh=inner,
        in_specs=(flat,) * 15 + (expert,) * 3 + (P(),) * 3,
        out_specs=(flat,) * 12 + (expert,) * 3 + (P(),) * 3,
        check_vma=False,
    )
```

```python
import jax
import jax.numpy as jnp
from jax import lax
from jax.experimental import pallas as pl
from jax.experimental.pallas import tpu as pltpu
from jax.sharding import Mesh, PartitionSpec as P

HEADS = 48
HEAD_DIM = 64
STATE = 128
KERNEL = 4
SEQ_SLOTS = 3
INNER = 3072
CONV_CH = 3328
EXTRA = 128

epsilon = 1e-05
bf16 = jnp.bfloat16
f32 = jnp.float32
GROUP = ("z", "y", "core")
ALL = ("dp", "z", "y", "core")


def matmul(left, right, dims=None, precision=None):
    if dims is None:
        dims = (((left.ndim - 1,), (0,)), ((), ()))
    return lax.dot_general(left, right, dims, precision=precision, preferred_element_type=f32)


def swap(value, axis):
    return lax.ppermute(value, axis, [(0, 1), (1, 0)])


def ring(value):
    size = lax.axis_size("z")
    return lax.ppermute(value, "z", [(k, (k + 1) % size) for k in range(size)])


def after(value, *earlier):
    return lax.optimization_barrier((value, earlier))[0]


def split_three(value):
    high = lax.reduce_precision(value, 8, 7)
    rest = value - high
    middle = lax.reduce_precision(rest, 8, 7)
    return high.astype(bf16), middle.astype(bf16), (rest - middle).astype(bf16)


def join_three(parts):
    return parts[0].astype(f32) + parts[1].astype(f32) + parts[2].astype(f32)


def gather(block, *joined):
    size = lax.axis_size("z")
    blocks = []
    for step in range(size - 1):
        following, beside = ring(block), swap(block, "y")
        blocks += [block, beside]
        if step == size - 2 and joined:
            block, _, joined = lax.optimization_barrier((following, beside, joined))
        else:
            block, _ = lax.optimization_barrier((following, beside))
    blocks += [block, swap(block, "y")]
    near = jnp.concatenate(blocks, axis=0)
    everything = jnp.concatenate([near, swap(near, "core")], axis=0)
    return (everything, *joined) if joined else everything


def add_low(left, right):
    return (left.astype(f32) + right.astype(f32)).astype(bf16)


def scatter(parts):
    size = lax.axis_size("z")
    parts = parts.reshape((2, size, 2, parts.shape[0] // (4 * size)) + parts.shape[1:])
    pairs = add_low(parts[0], swap(parts[1], "core"))
    there = [swap(pairs[step, 1], "y") for step in list(range(1, size)) + [0]]
    total = add_low(pairs[1, 0], there[0])
    for step in range(2, size):
        total = add_low(ring(total), add_low(pairs[step, 0], there[step - 1]))
    return ring(total).astype(f32) + pairs[0, 0].astype(f32) + there[-1].astype(f32)


def dp_gather_rows(value, axis):
    if lax.axis_size("dp") != 2:
        return lax.all_gather(value, "dp", axis=axis, tiled=True)
    other = swap(value, "dp")
    first = lax.axis_index("dp") == 0
    return jnp.concatenate(
        [jnp.where(first, value, other), jnp.where(first, other, value)], axis=axis
    )


def dp_scatter_rows(value, axis):
    count = lax.axis_size("dp")
    if count != 2:
        return lax.psum_scatter(value.astype(bf16), "dp", scatter_dimension=axis, tiled=True).astype(f32)
    place = lax.axis_index("dp")
    extent = value.shape[axis] // count
    sent = lax.dynamic_slice_in_dim(value, (1 - place) * extent, extent, axis).astype(bf16)
    kept = lax.dynamic_slice_in_dim(value, place * extent, extent, axis)
    return kept + swap(sent, "dp").astype(f32)


def params(steps=1):
    return pltpu.CompilerParams(
        dimension_semantics=("arbitrary",) * steps, vmem_limit_bytes=56 * 1024 * 1024
    )


def whole(array):
    return pl.BlockSpec(array.shape, lambda step: (0,) * array.ndim)


def sigmoid(value):
    return 1.0 / (1.0 + jnp.exp(-value))


def exact(left, right, dims):
    return lax.dot_general(
        left, right, (dims, ((), ())), precision=lax.Precision.HIGHEST, preferred_element_type=f32
    )


def rows_of(array, index):
    return array[index : index + 1]


WIDE = 256
CONV_LANES = 2 * STATE + WIDE
PROJ_LANES = CONV_LANES + WIDE + EXTRA


def triangle(count):
    row = lax.broadcasted_iota(jnp.int32, (count, count), 0)
    column = lax.broadcasted_iota(jnp.int32, (count, count), 1)
    return row - column


def block_scan(proj, place, conv, head):
    heads = HEADS // 16
    count = proj.shape[0]
    taps = [proj[:, :CONV_LANES]]
    total = rows_of(conv, KERNEL) + rows_of(conv, KERNEL - 1) * taps[0]
    for offset in range(1, KERNEL):
        inside = (place >= offset).astype(f32)
        taps.append(pltpu.roll(taps[0], offset, 0) * inside)
        total = total + rows_of(conv, KERNEL - 1 - offset) * taps[offset]
    conv_sig = sigmoid(total)
    conv_out = total * conv_sig
    b_part, c_part = conv_out[:, :STATE], conv_out[:, STATE : 2 * STATE]
    raw = proj[:, CONV_LANES + WIDE :] + rows_of(head, 0)[:, :EXTRA]
    step = jnp.maximum(raw, 0.0) + jnp.log1p(jnp.exp(-jnp.abs(raw)))
    distance = triangle(count)
    lower = (distance >= 0).astype(f32)
    cumul = exact(lower, step * rows_of(head, 1)[:, :EXTRA], ((1,), (0,)))
    cumul_rows = cumul.T
    step_rows = step.T
    scores = exact(c_part, b_part, ((1,), (1,)))
    reach = jnp.logical_and(distance >= 0, distance.astype(f32) <= place)
    lane = lax.broadcasted_iota(jnp.int32, (1, 2 * HEAD_DIM), 1)
    decays, values, scan = [], [], [None] * (WIDE // EXTRA)
    for index in range(heads):
        tile = index // 2
        spread = cumul[:, index : index + 1] - rows_of(cumul_rows, index)
        decay = jnp.exp(jnp.where(reach, spread, -1e30))
        mine = (lane // HEAD_DIM == index % 2).astype(f32)
        at = 2 * STATE + tile * EXTRA
        value = conv_out[:, at : at + EXTRA] * mine
        mixing = decay * scores * rows_of(step_rows, index)
        part = exact(mixing, value, ((1,), (0,)))
        scan[tile] = part if scan[tile] is None else scan[tile] + part
        decays.append((decay, mixing))
        values.append((value, mine))
    scan = jnp.concatenate(scan, axis=1) + rows_of(head, 2) * conv_out[:, 2 * STATE :]
    gate = proj[:, CONV_LANES : CONV_LANES + WIDE]
    gate_sig = sigmoid(gate)
    gated = scan * (gate * gate_sig)
    return dict(
        taps=taps, total=total, conv_sig=conv_sig, conv_out=conv_out, raw=raw, step_rows=step_rows,
        scores=scores, decays=decays, values=values, scan=scan, gate=gate, gate_sig=gate_sig,
        gated=gated, lower=lower,
    )


def mixer_forward_kernel(
    count, tokens_ref, beside_ref, gain_ref, w_in_ref, w_out_ref, conv_ref, head_ref,
    normed_ref, proj_ref, part_ref, scaled_ref,
):
    rows = tokens_ref[...].astype(f32)
    normed = rows * lax.rsqrt(jnp.mean(rows * rows, axis=1, keepdims=True) + epsilon) * gain_ref[...]
    normed = normed.astype(bf16)
    normed_ref[...] = normed
    proj_ref[...] = jnp.dot(normed, w_in_ref[...], preferred_element_type=f32)
    conv, head = conv_ref[...], head_ref[...]
    width = tokens_ref.shape[1]
    for index in range(tokens_ref.shape[0] // count):
        part = pl.ds(index * count, count)
        place = beside_ref[part, :].astype(f32)[:, 1:2]
        found = block_scan(proj_ref[part, :], place, conv, head)
        gated = found["gated"]
        scaled_ref[part, :] = (gated * rows_of(head, 3)).astype(bf16)
        square = gated * gated
        square = square[:, :EXTRA] + square[:, EXTRA:]
        part_ref[part, width:] = square.astype(bf16)
    part_ref[:, :width] = jnp.dot(
        scaled_ref[...], w_out_ref[...], preferred_element_type=f32
    ).astype(bf16)


def mixer_forward(gathered, width, count, gain, w_in, w_out, conv, head):
    total = gathered.shape[0]
    rows = 4 * count
    lanes = width // EXTRA

    def rows_spec(extent, column=0):
        return pl.BlockSpec((rows, extent), lambda step: (step, column))

    return pl.pallas_call(
        lambda *refs: mixer_forward_kernel(count, *refs),
        grid=(total // rows,),
        in_specs=[rows_spec(width), rows_spec(EXTRA, lanes)]
        + [whole(entry) for entry in (gain, w_in, w_out, conv, head)],
        out_specs=[rows_spec(width), rows_spec(PROJ_LANES), rows_spec(width + EXTRA), rows_spec(WIDE)],
        out_shape=[
            jax.ShapeDtypeStruct((total, width), bf16),
            jax.ShapeDtypeStruct((total, PROJ_LANES), f32),
            jax.ShapeDtypeStruct((total, width + EXTRA), bf16),
            jax.ShapeDtypeStruct((total, WIDE), bf16),
        ],
        compiler_params=params(),
        name="mixer_forward",
    )(gathered, gathered, gain, w_in, w_out, conv, head)


def mixer_backward_kernel(
    count, grad_ref, inner_ref, beside_ref, proj_ref, w_in_ref, w_out_ref, conv_ref, head_ref, rate_ref,
    normed_ref, proj_grad_ref, conv_grad_ref, head_grad_ref,
):
    heads = HEADS // 16
    conv, head = conv_ref[...], head_ref[...]

    @pl.when(pl.program_id(0) == 0)
    def _():
        conv_grad_ref[...] = jnp.zeros_like(conv_grad_ref)
        head_grad_ref[...] = jnp.zeros_like(head_grad_ref)

    grad_mixed = lax.dot_general(
        grad_ref[...], w_out_ref[...], (((1,), (1,)), ((), ())), preferred_element_type=f32
    )
    lane = lax.broadcasted_iota(jnp.int32, (1, EXTRA), 1)
    for index in range(grad_ref.shape[0] // count):
        part = pl.ds(index * count, count)
        place = beside_ref[part, :].astype(f32)[:, 1:2]
        found = block_scan(proj_ref[part, :], place, conv, head)
        inner = inner_ref[part, :].astype(f32)
        inner = inner[:, 0:1] + inner[:, 1:2] + inner[:, 2:3]
        gate, gate_sig, scan = found["gate"], found["gate_sig"], found["scan"]
        d_gated = grad_mixed[index * count : (index + 1) * count] * rows_of(head, 3) - found["gated"] * inner
        d_scan = d_gated * (gate * gate_sig)
        d_gate = d_gated * scan * (gate_sig * (1.0 + gate * (1.0 - gate_sig)))
        conv_out = found["conv_out"]
        d_values = [None] * (WIDE // EXTRA)
        d_scores = jnp.zeros((count, count), f32)
        column_sums = jnp.zeros((count, EXTRA), f32)
        direct, taken = [], []
        for number in range(heads):
            tile = number // 2
            decay, mixing = found["decays"][number]
            value, mine = found["values"][number]
            d_part = d_scan[:, tile * EXTRA : (tile + 1) * EXTRA]
            back = exact(mixing, d_part, ((0,), (0,))) * mine
            d_values[tile] = back if d_values[tile] is None else d_values[tile] + back
            d_mixing = exact(d_part, value, ((1,), (1,)))
            d_decayed = d_mixing * decay
            d_scores = d_scores + d_decayed * rows_of(found["step_rows"], number)
            d_spread = d_mixing * mixing
            direct.append(jnp.sum(d_decayed * found["scores"], axis=0, keepdims=True))
            taken.append(jnp.sum(d_spread, axis=0, keepdims=True))
            sums = jnp.sum(d_spread, axis=1, keepdims=True)
            column_sums = column_sums + jnp.where(lane == number, sums, 0.0)
            head_grad_ref[16 + number : 17 + number, :] += jnp.sum(d_part * value, axis=0, keepdims=True)
        d_values = jnp.concatenate(d_values, axis=1) + rows_of(head, 2) * d_scan
        empty = jnp.zeros((8 - heads, count), f32)
        d_cumul = column_sums.T[:8] - jnp.concatenate(taken + [empty], axis=0)
        d_rated = exact(d_cumul, found["lower"], ((1,), (0,)))
        step_rows = found["step_rows"][:8]
        d_step = jnp.concatenate(direct + [empty], axis=0) + d_rated * rate_ref[...]
        d_raw = d_step * sigmoid(found["raw"]).T[:8]
        head_grad_ref[0:8, :] += d_rated * step_rows
        head_grad_ref[8:16, :] += d_raw
        d_raw = jnp.concatenate([d_raw, jnp.zeros((EXTRA - 8, count), f32)], axis=0).T
        d_b = exact(d_scores, conv_out[:, STATE : 2 * STATE], ((0,), (0,)))
        d_c = exact(d_scores, conv_out[:, :STATE], ((1,), (0,)))
        d_out = jnp.concatenate([d_b, d_c, d_values], axis=1)
        conv_sig = found["conv_sig"]
        d_total = d_out * (conv_sig * (1.0 + found["total"] * (1.0 - conv_sig)))
        conv_grad_ref[KERNEL : KERNEL + 1, :] += jnp.sum(d_total, axis=0, keepdims=True)
        d_conv = rows_of(conv, KERNEL - 1) * d_total
        for offset in range(KERNEL):
            row = KERNEL - 1 - offset
            conv_grad_ref[row : row + 1, :] += jnp.sum(d_total * found["taps"][offset], axis=0, keepdims=True)
            if offset:
                kept = d_total * (place >= offset).astype(f32)
                d_conv = d_conv + rows_of(conv, row) * pltpu.roll(kept, count - offset, 0)
        proj_grad_ref[part, :] = jnp.concatenate([d_conv, d_gate, d_raw], axis=1).astype(bf16)
    normed_ref[...] = lax.dot_general(
        proj_grad_ref[...], w_in_ref[...], (((1,), (1,)), ((), ())), preferred_element_type=f32
    ).astype(bf16)


def mixer_backward(grads, gathered, proj, width, count, w_in, w_out, conv, head, rate):
    total = grads.shape[0]
    rows = 4 * count
    lanes = width // EXTRA

    def rows_spec(extent, column=0):
        return pl.BlockSpec((rows, extent), lambda step: (step, column))

    conv_shape = jax.ShapeDtypeStruct(conv.shape, f32)
    head_shape = jax.ShapeDtypeStruct((24, EXTRA), f32)
    return pl.pallas_call(
        lambda *refs: mixer_backward_kernel(count, *refs),
        grid=(total // rows,),
        in_specs=[rows_spec(width), rows_spec(EXTRA, lanes), rows_spec(EXTRA, lanes), rows_spec(PROJ_LANES)]
        + [whole(entry) for entry in (w_in, w_out, conv, head, rate)],
        out_specs=[rows_spec(width), rows_spec(PROJ_LANES), whole(conv_shape), whole(head_shape)],
        out_shape=[
            jax.ShapeDtypeStruct((total, width), bf16),
            jax.ShapeDtypeStruct((total, PROJ_LANES), bf16),
            conv_shape,
            head_shape,
        ],
        compiler_params=params(),
        name="mixer_backward",
    )(grads, grads, gathered, proj, w_in, w_out, conv, head, rate)


def selection(rank_ref, experts, slots):
    number = lax.broadcasted_iota(jnp.int32, (slots, rank_ref.shape[2]), 0)
    return [rank_ref[0, k : k + 1, :] == number for k in range(experts)]


def dispatch_kernel(experts, slots, weigh, rank_ref, weight_ref, values_ref, out_ref, *weights_ref):
    chosen = selection(rank_ref, experts, slots)
    select = jnp.concatenate([entry.astype(f32) for entry in chosen], axis=0).astype(bf16)
    rows = jnp.dot(select, values_ref[...], preferred_element_type=f32)
    for k in range(experts):
        part = rows[k * slots : (k + 1) * slots]
        if weigh:
            own = jnp.where(chosen[k], weight_ref[0, k : k + 1, :], 0.0)
            own = jnp.sum(own, axis=1, keepdims=True)
            part = part * own
            weights_ref[0][k] = jnp.broadcast_to(own, (slots, EXTRA))
        out_ref[k] = part.astype(bf16)


def dispatch(values, rank, weight, experts, slots, weigh):
    pairs, _, tokens = rank.shape
    width = values.shape[1]
    rank_spec = pl.BlockSpec((1,) + rank.shape[1:], lambda step: (step, 0, 0))
    specs = [pl.BlockSpec((experts, slots, width), lambda step: (0, step, 0))]
    shapes = [jax.ShapeDtypeStruct((experts, pairs * slots, width), bf16)]
    if weigh:
        specs.append(pl.BlockSpec((experts, slots, EXTRA), lambda step: (0, step, 0)))
        shapes.append(jax.ShapeDtypeStruct((experts, pairs * slots, EXTRA), f32))
    return pl.pallas_call(
        lambda *refs: dispatch_kernel(experts, slots, weigh, *refs),
        grid=(pairs,),
        in_specs=[rank_spec, rank_spec, pl.BlockSpec((tokens, width), lambda step: (step, 0))],
        out_specs=specs,
        out_shape=shapes,
        compiler_params=params(),
        name="dispatch",
    )(rank, weight, values)


def combine_kernel(experts, slots, turned, rank_ref, rows_ref, left_ref, right_ref, out_ref):
    chosen = selection(rank_ref, experts, slots)
    select = jnp.concatenate([entry.astype(f32) for entry in chosen], axis=0).astype(bf16)
    rows = jnp.concatenate([rows_ref[k] for k in range(experts)], axis=0)
    total = lax.dot_general(select, rows, (((0,), (0,)), ((), ())), preferred_element_type=f32)
    dims = ((1,), (1,)) if turned else ((1,), (0,))
    total = total + lax.dot_general(
        left_ref[...], right_ref[...], (dims, ((), ())), preferred_element_type=f32
    )
    out_ref[...] = total.astype(bf16)


def combine(rows, rank, left, right, slots, turned):
    pairs, _, tokens = rank.shape
    experts, _, width = rows.shape
    return pl.pallas_call(
        lambda *refs: combine_kernel(experts, slots, turned, *refs),
        grid=(pairs,),
        in_specs=[
            pl.BlockSpec((1,) + rank.shape[1:], lambda step: (step, 0, 0)),
            pl.BlockSpec((experts, slots, width), lambda step: (0, step, 0)),
            pl.BlockSpec((tokens, left.shape[1]), lambda step: (step, 0)),
            whole(right),
        ],
        out_specs=pl.BlockSpec((tokens, width), lambda step: (step, 0)),
        out_shape=jax.ShapeDtypeStruct((pairs * tokens, width), bf16),
        compiler_params=params(),
        name="combine",
    )(rank, rows, left, right)


def expert_kernel(
    rows_ref, grad_ref, weight_ref, gate_ref, up_ref, down_ref, act_ref, g_ref, u_ref, back_ref, out_ref
):
    rows, gate_w, up_w, down_w = rows_ref[0], gate_ref[0], up_ref[0], down_ref[0]
    turned = (((1,), (1,)), ((), ()))
    gate = jnp.dot(rows, gate_w, preferred_element_type=f32)
    up = jnp.dot(rows, up_w, preferred_element_type=f32)
    sig = sigmoid(gate)
    silu = gate * sig
    act = (silu * up).astype(bf16)
    d_act = lax.dot_general(grad_ref[0], down_w, turned, preferred_element_type=f32)
    d_gate = (d_act * up * (sig * (1.0 + gate * (1.0 - sig)))).astype(bf16)
    d_up = (d_act * silu).astype(bf16)
    act_ref[0], g_ref[0], u_ref[0] = act, d_gate, d_up
    back = lax.dot_general(d_gate, gate_w, turned, preferred_element_type=f32)
    back = back + lax.dot_general(d_up, up_w, turned, preferred_element_type=f32)
    back_ref[0] = back.astype(bf16)
    out = jnp.dot(act, down_w, preferred_element_type=f32) * weight_ref[0][:, :1]
    out_ref[0] = out.astype(bf16)


def expert_pass(rows, grads, weights, gate, up, down):
    experts, lanes, width = rows.shape
    hidden = gate.shape[2]

    def each(entry):
        return pl.BlockSpec((1,) + entry.shape[1:], lambda step: (step, 0, 0))

    inputs = (rows, grads, weights, gate, up, down)
    small = jax.ShapeDtypeStruct((experts, lanes, hidden), bf16)
    large = jax.ShapeDtypeStruct((experts, lanes, width), bf16)
    outputs = [small] * 3 + [large] * 2
    return pl.pallas_call(
        expert_kernel,
        grid=(experts,),
        in_specs=[each(entry) for entry in inputs],
        out_specs=[each(entry) for entry in outputs],
        out_shape=outputs,
        compiler_params=params(),
        name="expert_pass",
    )(*inputs)


def local(
    hidden_in,
    cotangent,
    routes,
    route_gates,
    lengths,
    in_proj,
    out_proj,
    conv_weight,
    conv_bias,
    norm_gain,
    mix_gain,
    ffn_gain,
    shared_gate,
    shared_up,
    shared_down,
    expert_gate,
    expert_up,
    expert_down,
    decay_log,
    step_bias,
    skip_gain,
):
    tokens, width = hidden_in.shape
    top = routes.shape[1]
    replicas = lax.axis_size("dp")
    groups = lax.axis_size("z") * 4
    devices = replicas * groups
    core = lax.axis_index("core")
    column = lax.axis_index("z") * 2 + lax.axis_index("y")
    place = column * 2 + core
    heads = HEADS // groups
    own = heads * HEAD_DIM
    half = groups // 2
    rows_in = in_proj.shape[0]
    hidden_units = shared_gate.shape[1]
    unit = hidden_units // devices
    units = hidden_units // groups
    local_experts = expert_gate.shape[0]
    capacity = 2 * tokens * top // (local_experts * groups)
    first_head = core * (HEADS // 2) + column * heads
    first_channel = first_head * HEAD_DIM

    small = (conv_weight.reshape(-1), conv_bias, norm_gain, mix_gain, ffn_gain)
    small_sizes = [entry.shape[0] for entry in small]
    small_lanes = -(-sum(small_sizes) // rows_in)
    small_flat = jnp.concatenate(small)
    small_flat = jnp.pad(small_flat, (0, small_lanes * rows_in - small_flat.shape[0]))

    def by_place(block):
        block = block.reshape(rows_in, 2, half, own).transpose(2, 1, 0, 3)
        return block.reshape(groups, rows_in, own)

    def by_unit(block):
        block = block.reshape(rows_in, replicas, groups, unit).transpose(2, 0, 1, 3)
        return block.reshape(groups, rows_in, units)

    pack = jnp.concatenate(
        [
            by_place(in_proj[:, :INNER]),
            by_place(in_proj[:, INNER : 2 * INNER]),
            by_unit(shared_gate),
            by_unit(shared_up),
        ],
        axis=2,
    )
    pack = lax.all_to_all(pack, GROUP, split_axis=0, concat_axis=0, tiled=True)
    pack = dp_gather_rows(pack.reshape(1, groups * rows_in, pack.shape[2]), 0)
    pack = pack.reshape(devices * rows_in, pack.shape[2])

    spread = jnp.concatenate([in_proj[:, 2 * INNER :], small_flat.reshape(rows_in, small_lanes)], axis=1)
    spread = jnp.pad(spread, ((0, 0), (0, -spread.shape[1] % EXTRA)))
    spread = dp_gather_rows(spread[None], 0).reshape(replicas * rows_in, -1)

    if replicas == 2:
        both = swap(out_proj, "core")
        both = jnp.concatenate(
            [jnp.where(core == 0, out_proj, both), jnp.where(core == 0, both, out_proj)]
        )
        w_out = jnp.where(lax.axis_index("dp") == core, both, swap(both, "dp"))
    else:
        w_out = lax.dynamic_slice_in_dim(
            lax.all_gather(out_proj, ALL, axis=0, tiled=True), first_channel, own, 0
        )
    w_shared_down = dp_gather_rows(shared_down[None], 0).reshape(units, width)

    bounds = jnp.cumsum(lengths[0])
    slot = jnp.arange(tokens, dtype=jnp.int32)
    runs = jnp.sum((slot[:, None] >= bounds[None, : SEQ_SLOTS - 1]).astype(jnp.int32), axis=1)
    live = (runs < SEQ_SLOTS - 1).astype(f32)[:, None]
    starts = jnp.concatenate([jnp.zeros((1,), jnp.int32), bounds[: SEQ_SLOTS - 1].astype(jnp.int32)])
    place_in_run = slot - jnp.sum(jnp.where(runs[:, None] == jnp.arange(SEQ_SLOTS), starts, 0), axis=1)
    beside = [runs.astype(bf16)[:, None], place_in_run.astype(bf16)[:, None], routes.astype(bf16), *split_three(route_gates)]
    beside = jnp.concatenate(beside, axis=1)
    beside = jnp.pad(beside, ((0, 0), (0, EXTRA - beside.shape[1])))
    w_gate, w_up, w_down = (
        lax.all_gather(entry, "dp", axis=1, tiled=True)
        for entry in (expert_gate, expert_up, expert_down)
    )
    spread = jnp.pad(spread, ((0, tokens - spread.shape[0]), (0, 0)))
    gathered = gather(jnp.concatenate([hidden_in, beside, spread], axis=1))
    at = width + 2
    routes_all = gathered[:, at : at + top].astype(jnp.int32)
    gates_all = join_three([gathered[:, at + k * top : at + (k + 1) * top] for k in (1, 2, 3)])

    number = jnp.arange(groups, dtype=jnp.int32)
    back_z = (lax.axis_index("z") - number // 4) % (groups // 4)
    other_y = (number // 2) % 2 != lax.axis_index("y")
    other_core = number % 2 != core
    order = other_core * half + back_z * 2 + other_y
    spread = gathered[:, width + EXTRA :].reshape(groups, tokens, -1)[:, : replicas * rows_in]
    spread = spread[order].reshape(groups, replicas, rows_in, -1).transpose(1, 0, 2, 3)
    spread = spread.reshape(devices, rows_in, -1)
    small_at = 2 * STATE + HEADS
    small_all = spread[:, :, small_at : small_at + small_lanes].reshape(devices, -1)
    pieces = []
    start = 0
    for size in small_sizes:
        pieces.append(small_all[:, start : start + size].reshape(-1).astype(f32))
        start += size
    conv_w_all = pieces[0].reshape(CONV_CH, KERNEL).T
    conv_b_all, norm_gain_all, mix_gain_all, ffn_gain_all = pieces[1:]
    spread = spread.reshape(devices * rows_in, -1)
    w_step = lax.dynamic_slice_in_dim(spread, 2 * STATE + first_head, heads, 1)
    w_step = jnp.pad(w_step, ((0, 0), (0, EXTRA - heads)))
    widen = ((0, 0), (0, WIDE - own))
    w_in = [spread[:, : 2 * STATE], jnp.pad(pack[:, own : 2 * own], widen), jnp.pad(pack[:, :own], widen), w_step]
    w_in = jnp.concatenate(w_in, axis=1)
    w_shared = pack[:, 2 * own :]

    def own_channels(rows):
        return lax.dynamic_slice_in_dim(rows, first_channel, own, rows.ndim - 1)

    conv = jnp.concatenate([conv_w_all, conv_b_all[None]], axis=0)
    conv = jnp.concatenate([conv[:, INNER:], own_channels(conv)], axis=1)
    conv = jnp.pad(conv, ((0, 8 - conv.shape[0]), (0, CONV_LANES - conv.shape[1])))

    def own_heads(row):
        return lax.dynamic_slice_in_dim(row, first_head, heads, 0)

    def lanes_of(row):
        return jnp.pad(row, (0, WIDE - row.shape[0]))

    rate = -jnp.exp(own_heads(decay_log))
    head = [
        lanes_of(own_heads(step_bias)),
        lanes_of(rate),
        lanes_of(jnp.repeat(own_heads(skip_gain), HEAD_DIM)),
        lanes_of(own_channels(mix_gain_all)),
    ]
    head = jnp.pad(jnp.stack(head), ((0, 4), (0, 0)))
    rate_rows = jnp.broadcast_to(jnp.pad(rate, (0, 8 - heads))[:, None], (8, EXTRA))
    w_out = jnp.pad(w_out, ((0, WIDE - own), (0, 0)))

    normed, proj, mixed_part, scaled = mixer_forward(
        gathered, width, tokens, norm_gain_all[None], w_in, w_out, conv, head
    )
    grad_out = cotangent.astype(f32)
    branch = (grad_out * live).astype(bf16)
    branch_all = gather(after(branch, gathered))
    mixed_part, branch_all = lax.optimization_barrier((mixed_part, branch_all))
    mixed_sum = scatter(mixed_part)
    mix_rms = lax.rsqrt(jnp.sum(mixed_sum[:, width:], axis=1, keepdims=True) / INNER + epsilon)
    mixer_out = mixed_sum[:, :width] * mix_rms
    input_rows = hidden_in.astype(f32)
    resid = input_rows + live * mixer_out
    ffn_rms = lax.rsqrt(jnp.mean(resid * resid, axis=1, keepdims=True) + epsilon)
    ffn_hat = resid * ffn_rms
    ffn_low = (ffn_hat * ffn_gain_all).astype(bf16)

    ffn_all = gather(ffn_low)

    shared_gu = matmul(ffn_all, w_shared)

    def swiglu(both):
        extent = both.shape[-1] // 2
        return jax.nn.silu(both[..., :extent]) * both[..., extent:]

    shared_act, shared_back = jax.vjp(swiglu, shared_gu)
    shared_low = shared_act.astype(bf16)
    (grad_shared_gu,) = shared_back(matmul(branch_all, w_shared_down, (((1,), (1,)), ((), ()))))
    shared_gu_low = grad_shared_gu.astype(bf16)

    pairs = groups // 2
    pair_tokens = 2 * tokens
    pair_slots = 2 * capacity
    lanes = pairs * pair_slots
    numbers = place * local_experts + jnp.arange(local_experts, dtype=jnp.int32)
    named = routes_all[:, None, :] == numbers[None, :, None]
    member = jnp.any(named, axis=2).T.reshape(local_experts, pairs, pair_tokens)
    weight = jnp.sum(jnp.where(named, gates_all[:, None, :], 0.0), axis=2).T
    weight = weight.reshape(local_experts, pairs, pair_tokens)
    below = jnp.triu(jnp.ones((pair_tokens, pair_tokens), bf16))
    rank = matmul(member.astype(bf16), below)
    rank = jnp.where(member, rank.astype(jnp.int32) - 1, -1).transpose(1, 0, 2)
    rank = jnp.pad(rank, ((0, 0), (0, 8 - local_experts), (0, 0)), constant_values=-1)
    weight = jnp.pad(weight.transpose(1, 0, 2), ((0, 0), (0, 8 - local_experts), (0, 0)))
    d_row, slot_weight = dispatch(branch_all, rank, weight, local_experts, pair_slots, True)
    (expert_in,) = dispatch(ffn_all, rank, weight, local_experts, pair_slots, False)
    act_low, g_low, u_low, d_in_row, expert_row = expert_pass(
        expert_in, d_row, slot_weight, w_gate, w_up, w_down
    )
    half_grad = (((1,), (1,)), ((0,), (0,)))

    def expert_grad(left, right):
        total = matmul(left, right, half_grad).astype(bf16)
        return lax.psum_scatter(total, "dp", scatter_dimension=1, tiled=True).astype(f32)

    grad_ffn_part = combine(d_in_row, rank, shared_gu_low, w_shared, pair_slots, True)
    grad_ffn = scatter(grad_ffn_part)
    (expert_in, expert_row, act_low, shared_low, ffn_all) = after(
        (expert_in, expert_row, act_low, shared_low, ffn_all), grad_ffn_part
    )
    grad_down = expert_grad(act_low, d_row)
    grad_gate = expert_grad(expert_in, g_low)
    grad_up = expert_grad(expert_in, u_low)
    branch_part = combine(expert_row, rank, shared_low, w_shared_down, pair_slots, False)

    grad_ffn_gain = jnp.sum(grad_ffn * ffn_hat, axis=0)
    scaled_ffn = grad_ffn * ffn_gain_all
    grad_resid = grad_out + ffn_rms * (
        scaled_ffn - ffn_hat * jnp.mean(scaled_ffn * ffn_hat, axis=1, keepdims=True)
    )
    d_mixer = (grad_resid * live).astype(bf16).astype(f32)
    inner_term = jnp.sum(d_mixer * mixer_out, axis=1, keepdims=True) * mix_rms * mix_rms / INNER
    inner_pack = jnp.pad(jnp.concatenate(split_three(inner_term), axis=1), ((0, 0), (0, EXTRA - 3)))
    d_mixer_pack = jnp.concatenate([(d_mixer * mix_rms).astype(bf16), inner_pack], axis=1)
    d_mixer_all = gather(d_mixer_pack)
    output = (resid + live * scatter(after(branch_part, d_mixer_all))).astype(bf16)
    grad_normed_part, proj_low, conv_grads, head_grads = mixer_backward(
        d_mixer_all, gathered, proj, width, tokens, w_in, w_out, conv, head, rate_rows
    )
    grad_normed_part, output = lax.optimization_barrier((grad_normed_part, output))
    grad_normed = scatter(grad_normed_part)
    normed, scaled = after((normed, scaled), grad_normed_part)
    grad_w_in = matmul(normed, proj_low, (((0,), (0,)), ((), ())))
    grad_out_rows = matmul(scaled, d_mixer_all[:, :width], (((0,), (0,)), ((), ())))[:own]
    shared_low, ffn_all = after((shared_low, ffn_all), d_mixer_all)
    grad_shared_down = matmul(shared_low, branch_all, (((0,), (0,)), ((), ())))
    grad_shared_w = matmul(ffn_all, shared_gu_low, (((0,), (0,)), ((), ())))

    value_at, gate_at = 2 * STATE, CONV_LANES
    grad_pack = jnp.concatenate(
        [
            grad_w_in[:, gate_at : gate_at + own],
            grad_w_in[:, value_at : value_at + own],
            grad_w_in[:, : 2 * STATE],
            grad_w_in[:, CONV_LANES + WIDE :],
            grad_shared_w,
        ],
        axis=1,
    )
    proj_lanes = 2 * own + 2 * STATE + EXTRA
    grad_pack = dp_scatter_rows(grad_pack, 0).astype(bf16).reshape(groups, rows_in, -1)
    grad_pack = lax.all_to_all(grad_pack, GROUP, split_axis=0, concat_axis=0, tiled=True).astype(f32)

    def from_place(block):
        block = block.reshape(half, 2, rows_in, block.shape[2]).transpose(2, 1, 0, 3)
        return block.reshape(rows_in, -1)

    def from_unit(block):
        block = block.reshape(groups, rows_in, replicas, unit).transpose(1, 2, 0, 3)
        return block.reshape(rows_in, hidden_units)

    both_at = 2 * own + 2 * STATE
    grad_in_proj = jnp.concatenate(
        [
            from_place(grad_pack[:, :, :own]),
            from_place(grad_pack[:, :, own : 2 * own]),
            jnp.sum(grad_pack[:, :, 2 * own : both_at], axis=0),
            from_place(grad_pack[:, :, both_at : both_at + heads]),
        ],
        axis=1,
    )
    grad_shared_gate = from_unit(grad_pack[:, :, proj_lanes : proj_lanes + units])
    grad_shared_up = from_unit(grad_pack[:, :, proj_lanes + units :])
    grad_shared_down = dp_scatter_rows(grad_shared_down.reshape(replicas, unit, width), 0)[0]
    if replicas == 2:
        mine = lax.axis_index("dp") == core
        received = swap(grad_out_rows.astype(bf16), "dp").astype(f32)
        total = (grad_out_rows + received).reshape(2, own // 2, width)
        passed = swap(lax.dynamic_index_in_dim(total, 1 - core, 0, keepdims=False), "core")
        grad_out_proj = jnp.where(mine, lax.dynamic_index_in_dim(total, core, 0, keepdims=False), passed)
    else:
        full = jnp.zeros((INNER, width), f32)
        full = lax.dynamic_update_slice_in_dim(full, grad_out_rows, first_channel, 0)
        grad_out_proj = lax.psum_scatter(full, ALL, scatter_dimension=0, tiled=True)
    grad_mix_gain = jnp.sum(grad_out_proj * out_proj.astype(f32), axis=1) / mix_gain.astype(f32)
    grad_norm_gain = jnp.sum(grad_in_proj * in_proj.astype(f32), axis=1) / norm_gain.astype(f32)

    def to_owner(part):
        rows_part = jnp.zeros((part.shape[0], CONV_CH), f32)
        values = part[:, 2 * STATE : 2 * STATE + own]
        rows_part = lax.dynamic_update_slice_in_dim(rows_part, values, first_channel, 1)
        rows_part = lax.dynamic_update_slice_in_dim(rows_part, part[:, : 2 * STATE], INNER, 1)
        return rows_part.reshape(part.shape[0], devices, -1).transpose(1, 0, 2).reshape(devices, -1)

    def head_row(part):
        return lax.dynamic_update_slice_in_dim(jnp.zeros((HEADS,), f32), part, first_head, 0)

    head_grads = jnp.sum(head_grads.reshape(3, 8, EXTRA)[:, :heads], axis=2)
    head_rows = jnp.concatenate([head_row(entry) for entry in (head_grads[0] * rate, *head_grads[1:])])
    sums = jnp.concatenate(
        [
            to_owner(conv_grads[: KERNEL + 1]),
            grad_ffn_gain.reshape(devices, -1),
            jnp.broadcast_to(head_rows[None], (devices, 3 * HEADS)),
        ],
        axis=1,
    )
    sums = lax.all_to_all(sums, ALL, split_axis=0, concat_axis=0, tiled=True)
    sums = jnp.sum(sums, axis=0)
    channels = CONV_CH // devices
    grad_conv_weight = sums[: KERNEL * channels].reshape(KERNEL, channels).T
    grad_conv_bias = sums[KERNEL * channels : (KERNEL + 1) * channels]
    at = (KERNEL + 1) * channels
    grad_ffn_gain = sums[at : at + rows_in]
    at += rows_in
    grad_decay, grad_stepb, grad_skip = (sums[at + k * HEADS : at + (k + 1) * HEADS] for k in range(3))

    in_rms = lax.rsqrt(jnp.mean(input_rows * input_rows, axis=1, keepdims=True) + epsilon)
    in_hat = input_rows * in_rms
    scaled_in = grad_normed * norm_gain_all
    grad_input = grad_resid + in_rms * (
        scaled_in - in_hat * jnp.mean(scaled_in * in_hat, axis=1, keepdims=True)
    )
    return (
        output,
        grad_input,
        grad_in_proj,
        grad_out_proj,
        grad_conv_weight,
        grad_conv_bias,
        grad_norm_gain,
        grad_mix_gain,
        grad_ffn_gain,
        grad_shared_gate,
        grad_shared_up,
        grad_shared_down,
        grad_gate,
        grad_up,
        grad_down,
        grad_decay,
        grad_stepb,
        grad_skip,
    )


def solution(mesh):
    replicas, groups = mesh.shape["dp"], mesh.shape["expert"]
    inner = Mesh(mesh.devices.reshape(replicas, groups // 4, 2, 2), ALL)
    flat = P(ALL)
    expert = P(GROUP, "dp", None)
    return jax.shard_map(
        local,
        mesh=inner,
        in_specs=(flat,) * 15 + (expert,) * 3 + (P(),) * 3,
        out_specs=(flat,) * 12 + (expert,) * 3 + (P(),) * 3,
        check_vma=False,
    )
```

```python
import jax
import jax.numpy as jnp
from jax import lax
from jax.experimental import pallas as pl
from jax.experimental.pallas import tpu as pltpu
from jax.sharding import Mesh, PartitionSpec as P

HEADS = 48
HEAD_DIM = 64
STATE = 128
KERNEL = 4
SEQ_SLOTS = 3
INNER = 3072
CONV_CH = 3328
EXTRA = 128

epsilon = 1e-05
bf16 = jnp.bfloat16
f32 = jnp.float32
GROUP = ("z", "y", "core")
ALL = ("dp", "z", "y", "core")


def matmul(left, right, dims=None, precision=None):
    if dims is None:
        dims = (((left.ndim - 1,), (0,)), ((), ()))
    return lax.dot_general(left, right, dims, precision=precision, preferred_element_type=f32)


def swap(value, axis):
    return lax.ppermute(value, axis, [(0, 1), (1, 0)])


def ring(value):
    size = lax.axis_size("z")
    return lax.ppermute(value, "z", [(k, (k + 1) % size) for k in range(size)])


def after(value, *earlier):
    return lax.optimization_barrier((value, earlier))[0]


def split_three(value):
    high = lax.reduce_precision(value, 8, 7)
    rest = value - high
    middle = lax.reduce_precision(rest, 8, 7)
    return high.astype(bf16), middle.astype(bf16), (rest - middle).astype(bf16)


def join_three(parts):
    return parts[0].astype(f32) + parts[1].astype(f32) + parts[2].astype(f32)


def tie(value, *others):
    return lax.optimization_barrier((value, *others))


def work_of(entry, token):
    return entry(token) if callable(entry) else entry


def gather(block, beside_work=()):
    size = lax.axis_size("z")
    beside_work = (list(beside_work) + [()] * size)[:size]
    blocks = []
    for step in range(size):
        following = ring(block) if step < size - 1 else ()
        near = swap(block, "y")
        work = work_of(beside_work[step], block)
        following, near, beside_work[step] = tie(following, near, work)
        blocks += [block, near]
        block = following
    own = jnp.concatenate(blocks, axis=0)
    return own, swap(own, "core"), beside_work


def add_low(left, right):
    return (left.astype(f32) + right.astype(f32)).astype(bf16)


def scatter_first(near, mate, moved=None):
    size = lax.axis_size("z")
    shape = (size, 2, near.shape[0] // (2 * size), near.shape[1])
    there = (swap(mate, "core") if moved is None else moved).reshape(shape)
    near = near.reshape(shape)
    pairs = [add_low(near[step], there[step]) for step in range(size)]
    return pairs


def scatter_beside(pairs):
    size = len(pairs)
    order = list(range(1, size)) + [0]
    there = {step: swap(pairs[step][1], "y") for step in order}
    return [there[step] for step in range(size)]


def ring_step(total, pairs, there, step):
    at = (step + 1) % len(pairs)
    total = ring(total).astype(f32) + (pairs[at][0].astype(f32) + there[at].astype(f32))
    return total.astype(bf16) if at else total


def scatter_last(pairs, beside_work=(), there=None):
    size = len(pairs)
    beside_work = (list(beside_work) + [()] * size)[:size]
    there = there or scatter_beside(pairs)
    total = add_low(pairs[1][0], there[1])
    token = pairs
    for step in range(1, size):
        total, beside_work[step - 1] = tie(total, work_of(beside_work[step - 1], token))
        token = total
        total = ring_step(total, pairs, there, step)
    total, beside_work[-1] = tie(total, work_of(beside_work[-1], token))
    return total, beside_work


def dp_gather_rows(value, axis):
    if lax.axis_size("dp") != 2:
        return lax.all_gather(value, "dp", axis=axis, tiled=True)
    other = swap(value, "dp")
    first = lax.axis_index("dp") == 0
    return jnp.concatenate(
        [jnp.where(first, value, other), jnp.where(first, other, value)], axis=axis
    )


def dp_scatter_rows(value, axis, hold=()):
    count = lax.axis_size("dp")
    if count != 2:
        return lax.psum_scatter(value.astype(bf16), "dp", scatter_dimension=axis, tiled=True).astype(f32)
    place = lax.axis_index("dp")
    extent = value.shape[axis] // count
    sent = lax.dynamic_slice_in_dim(value, (1 - place) * extent, extent, axis).astype(bf16)
    kept = lax.dynamic_slice_in_dim(value, place * extent, extent, axis)
    received, kept, hold = tie(swap(sent, "dp"), kept, hold)
    return kept + received.astype(f32)


def params(steps=1):
    return pltpu.CompilerParams(
        dimension_semantics=("arbitrary",) * steps, vmem_limit_bytes=56 * 1024 * 1024
    )


def cost(micros):
    return pl.CostEstimate(
        flops=int(micros * 1.1e9), bytes_accessed=int(micros * 3.5e6), transcendentals=0
    )


def whole(array):
    return pl.BlockSpec(array.shape, lambda step: (0,) * array.ndim)


def sigmoid(value):
    return 1.0 / (1.0 + jnp.exp(-value))


def exact(left, right, dims):
    return lax.dot_general(
        left, right, (dims, ((), ())), precision=lax.Precision.HIGHEST, preferred_element_type=f32
    )


def rows_of(array, index):
    return array[index : index + 1]


WIDE = 256
CONV_LANES = 2 * STATE + WIDE
PROJ_LANES = CONV_LANES + WIDE + EXTRA


def triangle(count):
    row = lax.broadcasted_iota(jnp.int32, (count, count), 0)
    column = lax.broadcasted_iota(jnp.int32, (count, count), 1)
    return row - column


def block_scan(proj, place, conv, head):
    heads = HEADS // 16
    count = proj.shape[0]
    taps = [proj[:, :CONV_LANES]]
    total = rows_of(conv, KERNEL) + rows_of(conv, KERNEL - 1) * taps[0]
    for offset in range(1, KERNEL):
        inside = (place >= offset).astype(f32)
        taps.append(pltpu.roll(taps[0], offset, 0) * inside)
        total = total + rows_of(conv, KERNEL - 1 - offset) * taps[offset]
    conv_sig = sigmoid(total)
    conv_out = total * conv_sig
    b_part, c_part = conv_out[:, :STATE], conv_out[:, STATE : 2 * STATE]
    raw = proj[:, CONV_LANES + WIDE :] + rows_of(head, 0)[:, :EXTRA]
    step = jnp.maximum(raw, 0.0) + jnp.log1p(jnp.exp(-jnp.abs(raw)))
    distance = triangle(count)
    lower = (distance >= 0).astype(f32)
    cumul = exact(lower, step * rows_of(head, 1)[:, :EXTRA], ((1,), (0,)))
    cumul_rows = cumul.T
    step_rows = step.T
    scores = exact(c_part, b_part, ((1,), (1,)))
    reach = jnp.logical_and(distance >= 0, distance.astype(f32) <= place)
    lane = lax.broadcasted_iota(jnp.int32, (1, 2 * HEAD_DIM), 1)
    decays, values, scan = [], [], [None] * (WIDE // EXTRA)
    for index in range(heads):
        tile = index // 2
        spread = cumul[:, index : index + 1] - rows_of(cumul_rows, index)
        decay = jnp.exp(jnp.where(reach, spread, -1e30))
        mine = (lane // HEAD_DIM == index % 2).astype(f32)
        at = 2 * STATE + tile * EXTRA
        value = conv_out[:, at : at + EXTRA] * mine
        mixing = decay * scores * rows_of(step_rows, index)
        part = exact(mixing, value, ((1,), (0,)))
        scan[tile] = part if scan[tile] is None else scan[tile] + part
        decays.append((decay, mixing))
        values.append((value, mine))
    scan = jnp.concatenate(scan, axis=1) + rows_of(head, 2) * conv_out[:, 2 * STATE :]
    gate = proj[:, CONV_LANES : CONV_LANES + WIDE]
    gate_sig = sigmoid(gate)
    gated = scan * (gate * gate_sig)
    return dict(
        taps=taps, total=total, conv_sig=conv_sig, conv_out=conv_out, raw=raw, step_rows=step_rows,
        scores=scores, decays=decays, values=values, scan=scan, gate=gate, gate_sig=gate_sig,
        gated=gated, lower=lower,
    )


def mixer_forward_kernel(
    count, tokens_ref, beside_ref, gain_ref, w_in_ref, w_out_ref, conv_ref, head_ref,
    normed_ref, proj_ref, part_ref, scaled_ref,
):
    rows = tokens_ref[...].astype(f32)
    normed = rows * lax.rsqrt(jnp.mean(rows * rows, axis=1, keepdims=True) + epsilon) * gain_ref[...]
    normed = normed.astype(bf16)
    normed_ref[...] = normed
    proj_ref[...] = jnp.dot(normed, w_in_ref[...], preferred_element_type=f32)
    conv, head = conv_ref[...], head_ref[...]
    width = tokens_ref.shape[1]
    for index in range(tokens_ref.shape[0] // count):
        part = pl.ds(index * count, count)
        place = beside_ref[part, :].astype(f32)[:, 1:2]
        found = block_scan(proj_ref[part, :], place, conv, head)
        gated = found["gated"]
        scaled_ref[part, :] = (gated * rows_of(head, 3)).astype(bf16)
        square = gated * gated
        square = square[:, :EXTRA] + square[:, EXTRA:]
        part_ref[part, width:] = square.astype(bf16)
    part_ref[:, :width] = jnp.dot(
        scaled_ref[...], w_out_ref[...], preferred_element_type=f32
    ).astype(bf16)


def mixer_forward(gathered, width, count, gain, w_in, w_out, conv, head):
    total = gathered.shape[0]
    rows = 4 * count
    lanes = width // EXTRA

    def rows_spec(extent, column=0):
        return pl.BlockSpec((rows, extent), lambda step: (step, column))

    return pl.pallas_call(
        lambda *refs: mixer_forward_kernel(count, *refs),
        grid=(total // rows,),
        in_specs=[rows_spec(width), rows_spec(EXTRA, lanes)]
        + [whole(entry) for entry in (gain, w_in, w_out, conv, head)],
        out_specs=[rows_spec(width), rows_spec(PROJ_LANES), rows_spec(width + EXTRA), rows_spec(WIDE)],
        out_shape=[
            jax.ShapeDtypeStruct((total, width), bf16),
            jax.ShapeDtypeStruct((total, PROJ_LANES), f32),
            jax.ShapeDtypeStruct((total, width + EXTRA), bf16),
            jax.ShapeDtypeStruct((total, WIDE), bf16),
        ],
        compiler_params=params(),
        cost_estimate=cost(total / 80),
        name="mixer_forward",
    )(gathered, gathered, gain, w_in, w_out, conv, head)


def mixer_backward_kernel(
    count, grad_ref, inner_ref, beside_ref, proj_ref, w_in_ref, w_out_ref, conv_ref, head_ref, rate_ref,
    normed_ref, proj_grad_ref, conv_grad_ref, head_grad_ref,
):
    heads = HEADS // 16
    conv, head = conv_ref[...], head_ref[...]

    @pl.when(pl.program_id(0) == 0)
    def _():
        conv_grad_ref[...] = jnp.zeros_like(conv_grad_ref)
        head_grad_ref[...] = jnp.zeros_like(head_grad_ref)

    grad_mixed = lax.dot_general(
        grad_ref[...], w_out_ref[...], (((1,), (1,)), ((), ())), preferred_element_type=f32
    )
    lane = lax.broadcasted_iota(jnp.int32, (1, EXTRA), 1)
    for index in range(grad_ref.shape[0] // count):
        part = pl.ds(index * count, count)
        place = beside_ref[part, :].astype(f32)[:, 1:2]
        found = block_scan(proj_ref[part, :], place, conv, head)
        inner = inner_ref[part, :].astype(f32)
        inner = inner[:, 0:1] + inner[:, 1:2] + inner[:, 2:3]
        gate, gate_sig, scan = found["gate"], found["gate_sig"], found["scan"]
        d_gated = grad_mixed[index * count : (index + 1) * count] * rows_of(head, 3) - found["gated"] * inner
        d_scan = d_gated * (gate * gate_sig)
        d_gate = d_gated * scan * (gate_sig * (1.0 + gate * (1.0 - gate_sig)))
        conv_out = found["conv_out"]
        d_values = [None] * (WIDE // EXTRA)
        d_scores = jnp.zeros((count, count), f32)
        column_sums = jnp.zeros((count, EXTRA), f32)
        direct, taken = [], []
        for number in range(heads):
            tile = number // 2
            decay, mixing = found["decays"][number]
            value, mine = found["values"][number]
            d_part = d_scan[:, tile * EXTRA : (tile + 1) * EXTRA]
            back = exact(mixing, d_part, ((0,), (0,))) * mine
            d_values[tile] = back if d_values[tile] is None else d_values[tile] + back
            d_mixing = exact(d_part, value, ((1,), (1,)))
            d_decayed = d_mixing * decay
            d_scores = d_scores + d_decayed * rows_of(found["step_rows"], number)
            d_spread = d_mixing * mixing
            direct.append(jnp.sum(d_decayed * found["scores"], axis=0, keepdims=True))
            taken.append(jnp.sum(d_spread, axis=0, keepdims=True))
            sums = jnp.sum(d_spread, axis=1, keepdims=True)
            column_sums = column_sums + jnp.where(lane == number, sums, 0.0)
            head_grad_ref[16 + number : 17 + number, :] += jnp.sum(d_part * value, axis=0, keepdims=True)
        d_values = jnp.concatenate(d_values, axis=1) + rows_of(head, 2) * d_scan
        empty = jnp.zeros((8 - heads, count), f32)
        d_cumul = column_sums.T[:8] - jnp.concatenate(taken + [empty], axis=0)
        d_rated = exact(d_cumul, found["lower"], ((1,), (0,)))
        step_rows = found["step_rows"][:8]
        d_step = jnp.concatenate(direct + [empty], axis=0) + d_rated * rate_ref[...]
        d_raw = d_step * sigmoid(found["raw"]).T[:8]
        head_grad_ref[0:8, :] += d_rated * step_rows
        head_grad_ref[8:16, :] += d_raw
        d_raw = jnp.concatenate([d_raw, jnp.zeros((EXTRA - 8, count), f32)], axis=0).T
        d_b = exact(d_scores, conv_out[:, STATE : 2 * STATE], ((0,), (0,)))
        d_c = exact(d_scores, conv_out[:, :STATE], ((1,), (0,)))
        d_out = jnp.concatenate([d_b, d_c, d_values], axis=1)
        conv_sig = found["conv_sig"]
        d_total = d_out * (conv_sig * (1.0 + found["total"] * (1.0 - conv_sig)))
        conv_grad_ref[KERNEL : KERNEL + 1, :] += jnp.sum(d_total, axis=0, keepdims=True)
        d_conv = rows_of(conv, KERNEL - 1) * d_total
        for offset in range(KERNEL):
            row = KERNEL - 1 - offset
            conv_grad_ref[row : row + 1, :] += jnp.sum(d_total * found["taps"][offset], axis=0, keepdims=True)
            if offset:
                kept = d_total * (place >= offset).astype(f32)
                d_conv = d_conv + rows_of(conv, row) * pltpu.roll(kept, count - offset, 0)
        proj_grad_ref[part, :] = jnp.concatenate([d_conv, d_gate, d_raw], axis=1).astype(bf16)
    normed_ref[...] = lax.dot_general(
        proj_grad_ref[...], w_in_ref[...], (((1,), (1,)), ((), ())), preferred_element_type=f32
    ).astype(bf16)


def mixer_backward(grads, gathered, proj, width, count, w_in, w_out, conv, head, rate):
    total = grads.shape[0]
    rows = 4 * count
    lanes = width // EXTRA

    def rows_spec(extent, column=0):
        return pl.BlockSpec((rows, extent), lambda step: (step, column))

    conv_shape = jax.ShapeDtypeStruct(conv.shape, f32)
    head_shape = jax.ShapeDtypeStruct((24, EXTRA), f32)
    return pl.pallas_call(
        lambda *refs: mixer_backward_kernel(count, *refs),
        grid=(total // rows,),
        in_specs=[rows_spec(width), rows_spec(EXTRA, lanes), rows_spec(EXTRA, lanes), rows_spec(PROJ_LANES)]
        + [whole(entry) for entry in (w_in, w_out, conv, head, rate)],
        out_specs=[rows_spec(width), rows_spec(PROJ_LANES), whole(conv_shape), whole(head_shape)],
        out_shape=[
            jax.ShapeDtypeStruct((total, width), bf16),
            jax.ShapeDtypeStruct((total, PROJ_LANES), bf16),
            conv_shape,
            head_shape,
        ],
        compiler_params=params(),
        cost_estimate=cost(total / 46),
        name="mixer_backward",
    )(grads, grads, gathered, proj, w_in, w_out, conv, head, rate)


def selection(rank_ref, experts, slots):
    number = lax.broadcasted_iota(jnp.int32, (slots, rank_ref.shape[2]), 0)
    return [rank_ref[0, k : k + 1, :] == number for k in range(experts)]


def dispatch_kernel(experts, slots, grads, rank_ref, weight_ref, values_ref, *refs):
    chosen = selection(rank_ref, experts, slots)
    select = jnp.concatenate([entry.astype(f32) for entry in chosen], axis=0).astype(bf16)
    values = values_ref[...]
    rows = jnp.dot(select, values, preferred_element_type=f32)
    if grads:
        down_ref = refs[0]
        out_ref, weights_ref, act_grad_ref = refs[-3:]
        act_grad_ref[...] = lax.dot_general(
            values, down_ref[...], (((1,), (1,)), ((), ())), preferred_element_type=f32
        )
    else:
        act_grad_ref, gate_ref, up_ref = refs[:3]
        out_ref, act_ref, g_ref, u_ref = refs[-4:]
        gate = jnp.dot(values, gate_ref[...], preferred_element_type=f32)
        up = jnp.dot(values, up_ref[...], preferred_element_type=f32)
        sig = sigmoid(gate)
        silu = gate * sig
        d_act = act_grad_ref[...]
        act_ref[...] = (silu * up).astype(bf16)
        g_ref[...] = (d_act * up * (sig * (1.0 + gate * (1.0 - sig)))).astype(bf16)
        u_ref[...] = (d_act * silu).astype(bf16)
    for k in range(experts):
        part = rows[k * slots : (k + 1) * slots]
        if grads:
            own = jnp.where(chosen[k], weight_ref[0, k : k + 1, :], 0.0)
            own = jnp.sum(own, axis=1, keepdims=True)
            part = part * own
            weights_ref[k] = jnp.broadcast_to(own, (slots, EXTRA))
        out_ref[k] = part.astype(bf16)


def dispatch(values, rank, weight, experts, slots, first, shared, into=None):
    pairs, _, tokens = rank.shape
    count = values.shape[0] // tokens
    width = values.shape[1]
    grads = len(shared) == 1
    hidden = shared[0].shape[0] if grads else shared[0].shape[1]

    def slots_spec(extent):
        return pl.BlockSpec((experts, slots, extent), lambda step: (0, first + step, 0))

    def rows_spec(extent):
        return pl.BlockSpec((tokens, extent), lambda step: (step, 0))

    rank_spec = pl.BlockSpec((1,) + rank.shape[1:], lambda step: (first + step, 0, 0))
    in_specs = [rank_spec, rank_spec, rows_spec(width)]
    out_specs = [slots_spec(width)]
    shapes = [jax.ShapeDtypeStruct((experts, pairs * slots, width), bf16)]
    small = (values.shape[0], hidden)
    if grads:
        in_specs += [whole(shared[0])]
        out_specs += [slots_spec(EXTRA), rows_spec(hidden)]
        shapes += [
            jax.ShapeDtypeStruct((experts, pairs * slots, EXTRA), f32),
            jax.ShapeDtypeStruct(small, f32),
        ]
    else:
        in_specs += [rows_spec(hidden), whole(shared[1]), whole(shared[2])]
        out_specs += [rows_spec(hidden)] * 3
        shapes += [jax.ShapeDtypeStruct(small, bf16)] * 3
    aliases = {}
    into = () if into is None else tuple(into)
    for index, entry in enumerate(into):
        aliases[len(in_specs)] = index
        in_specs.append(pl.BlockSpec(memory_space=pl.ANY))
    return pl.pallas_call(
        lambda *refs: dispatch_kernel(experts, slots, grads, *refs),
        grid=(count,),
        in_specs=in_specs,
        out_specs=out_specs,
        out_shape=shapes,
        input_output_aliases=aliases,
        compiler_params=params(),
        cost_estimate=cost(5),
        name="dispatch",
    )(rank, weight, values, *shared, *into)


def combine_kernel(experts, slots, terms, turned, rank_ref, rows_ref, *refs):
    out_ref = refs[-1]
    chosen = selection(rank_ref, experts, slots)
    select = jnp.concatenate([entry.astype(f32) for entry in chosen], axis=0).astype(bf16)
    rows = jnp.concatenate([rows_ref[k] for k in range(experts)], axis=0)
    total = lax.dot_general(select, rows, (((0,), (0,)), ((), ())), preferred_element_type=f32)
    dims = ((1,), (1,)) if turned else ((1,), (0,))
    for k in range(terms):
        total = total + lax.dot_general(
            refs[2 * k][...], refs[2 * k + 1][...], (dims, ((), ())), preferred_element_type=f32
        )
    out_ref[...] = total.astype(bf16)


def combine(rows, rank, terms, slots, first, turned):
    pairs, _, tokens = rank.shape
    experts, _, width = rows.shape
    count = terms[0][0].shape[0] // tokens
    specs, operands = [], []
    for left, right in terms:
        specs += [pl.BlockSpec((tokens, left.shape[1]), lambda step: (step, 0)), whole(right)]
        operands += [left, right]
    return pl.pallas_call(
        lambda *refs: combine_kernel(experts, slots, len(terms), turned, *refs),
        grid=(count,),
        in_specs=[
            pl.BlockSpec((1,) + rank.shape[1:], lambda step: (first + step, 0, 0)),
            pl.BlockSpec((experts, slots, width), lambda step: (0, first + step, 0)),
        ]
        + specs,
        out_specs=pl.BlockSpec((tokens, width), lambda step: (step, 0)),
        out_shape=jax.ShapeDtypeStruct((count * tokens, width), bf16),
        compiler_params=params(),
        cost_estimate=cost(5),
        name="combine",
    )(rank, rows, *operands)


def expert_kernel(
    rows_ref, grad_ref, weight_ref, gate_ref, up_ref, down_ref, act_ref, g_ref, u_ref, back_ref, out_ref
):
    rows, gate_w, up_w, down_w = rows_ref[0], gate_ref[0], up_ref[0], down_ref[0]
    turned = (((1,), (1,)), ((), ()))
    gate = jnp.dot(rows, gate_w, preferred_element_type=f32)
    up = jnp.dot(rows, up_w, preferred_element_type=f32)
    sig = sigmoid(gate)
    silu = gate * sig
    act = (silu * up).astype(bf16)
    d_act = lax.dot_general(grad_ref[0], down_w, turned, preferred_element_type=f32)
    d_gate = (d_act * up * (sig * (1.0 + gate * (1.0 - sig)))).astype(bf16)
    d_up = (d_act * silu).astype(bf16)
    act_ref[0], g_ref[0], u_ref[0] = act, d_gate, d_up
    back = lax.dot_general(d_gate, gate_w, turned, preferred_element_type=f32)
    back = back + lax.dot_general(d_up, up_w, turned, preferred_element_type=f32)
    back_ref[0] = back.astype(bf16)
    out = jnp.dot(act, down_w, preferred_element_type=f32) * weight_ref[0][:, :1]
    out_ref[0] = out.astype(bf16)


def expert_pass(rows, grads, weights, gate, up, down):
    experts, lanes, width = rows.shape
    hidden = gate.shape[2]

    def each(entry):
        return pl.BlockSpec((1,) + entry.shape[1:], lambda step: (step, 0, 0))

    inputs = (rows, grads, weights, gate, up, down)
    small = jax.ShapeDtypeStruct((experts, lanes, hidden), bf16)
    large = jax.ShapeDtypeStruct((experts, lanes, width), bf16)
    outputs = [small] * 3 + [large] * 2
    return pl.pallas_call(
        expert_kernel,
        grid=(experts,),
        in_specs=[each(entry) for entry in inputs],
        out_specs=[each(entry) for entry in outputs],
        out_shape=outputs,
        compiler_params=params(),
        cost_estimate=cost(20),
        name="expert_pass",
    )(*inputs)


def local(
    hidden_in,
    cotangent,
    routes,
    route_gates,
    lengths,
    in_proj,
    out_proj,
    conv_weight,
    conv_bias,
    norm_gain,
    mix_gain,
    ffn_gain,
    shared_gate,
    shared_up,
    shared_down,
    expert_gate,
    expert_up,
    expert_down,
    decay_log,
    step_bias,
    skip_gain,
):
    tokens, width = hidden_in.shape
    top = routes.shape[1]
    replicas = lax.axis_size("dp")
    groups = lax.axis_size("z") * 4
    devices = replicas * groups
    core = lax.axis_index("core")
    column = lax.axis_index("z") * 2 + lax.axis_index("y")
    place = column * 2 + core
    heads = HEADS // groups
    own = heads * HEAD_DIM
    half = groups // 2
    rows_in = in_proj.shape[0]
    hidden_units = shared_gate.shape[1]
    unit = hidden_units // devices
    units = hidden_units // groups
    local_experts = expert_gate.shape[0]
    capacity = 2 * tokens * top // (local_experts * groups)
    first_head = core * (HEADS // 2) + column * heads
    first_channel = first_head * HEAD_DIM

    small = (conv_weight.reshape(-1), conv_bias, norm_gain, mix_gain, ffn_gain)
    small_sizes = [entry.shape[0] for entry in small]
    small_lanes = -(-sum(small_sizes) // rows_in)
    small_flat = jnp.concatenate(small)
    small_flat = jnp.pad(small_flat, (0, small_lanes * rows_in - small_flat.shape[0]))

    bounds = jnp.cumsum(lengths[0])
    slot = jnp.arange(tokens, dtype=jnp.int32)
    runs = jnp.sum((slot[:, None] >= bounds[None, : SEQ_SLOTS - 1]).astype(jnp.int32), axis=1)
    live = (runs < SEQ_SLOTS - 1).astype(f32)[:, None]
    starts = jnp.concatenate([jnp.zeros((1,), jnp.int32), bounds[: SEQ_SLOTS - 1].astype(jnp.int32)])
    place_in_run = slot - jnp.sum(jnp.where(runs[:, None] == jnp.arange(SEQ_SLOTS), starts, 0), axis=1)
    beside = [runs.astype(bf16)[:, None], place_in_run.astype(bf16)[:, None], routes.astype(bf16)]
    beside = jnp.concatenate(beside + list(split_three(route_gates)), axis=1)
    beside = jnp.pad(beside, ((0, 0), (0, EXTRA - beside.shape[1])))
    spread = jnp.concatenate([in_proj[:, 2 * INNER :], small_flat.reshape(rows_in, small_lanes)], axis=1)
    spread = jnp.pad(spread, ((0, 0), (0, -spread.shape[1] % EXTRA)))
    spread = dp_gather_rows(spread[None], 0).reshape(replicas * rows_in, -1)
    spread = jnp.pad(spread, ((0, tokens - replicas * rows_in), (0, 0)))
    payload = jnp.concatenate([hidden_in, beside, spread], axis=1)

    def by_place(block):
        block = block.reshape(rows_in, 2, half, own).transpose(2, 1, 0, 3)
        return block.reshape(groups, rows_in, own)

    def by_unit(block):
        block = block.reshape(rows_in, replicas, groups, unit).transpose(2, 0, 1, 3)
        return block.reshape(groups, rows_in, units)

    pack = jnp.concatenate(
        [
            by_place(in_proj[:, :INNER]),
            by_place(in_proj[:, INNER : 2 * INNER]),
            by_unit(shared_gate),
            by_unit(shared_up),
        ],
        axis=2,
    )
    pack = lax.all_to_all(pack, GROUP, split_axis=0, concat_axis=0, tiled=True)

    if replicas == 2:
        both = swap(out_proj, "core")
        both = jnp.concatenate(
            [jnp.where(core == 0, out_proj, both), jnp.where(core == 0, both, out_proj)]
        )
        payload, both = tie(payload, both)
        w_out = jnp.where(lax.axis_index("dp") == core, both, swap(both, "dp"))
    else:
        w_out = lax.dynamic_slice_in_dim(
            lax.all_gather(out_proj, ALL, axis=0, tiled=True), first_channel, own, 0
        )
    def gather_tokens():
        size = lax.axis_size("z")
        block, blocks, pieces = payload, [], []
        arrived = None
        for step in range(size):
            following = ring(block) if step < size - 1 else ()
            near = swap(block, "y")
            if step == 0:
                work = (pack, w_out)
            elif replicas == 2 and step < 4:
                extent = arrived.shape[0] // 3
                work = swap(after(arrived[(step - 1) * extent : step * extent], block), "dp")
            else:
                work = ()
            following, near, work = tie(following, near, work)
            if step == 0:
                arrived = work[0].reshape(groups * rows_in, -1)
                found = work[1]
            elif replicas == 2 and step < 4:
                pieces.append(work)
            blocks += [block, near]
            block = following
        near = jnp.concatenate(blocks, axis=0)
        if replicas == 2:
            other = jnp.concatenate(pieces, axis=0)
            mine = lax.axis_index("dp") == 0
            everything = jnp.concatenate(
                [jnp.where(mine, arrived, other), jnp.where(mine, other, arrived)], axis=0
            )
        else:
            everything = lax.all_gather(arrived, "dp", axis=0, tiled=True)
        return near, swap(near, "core"), everything, found

    near, mate, pack, w_out = gather_tokens()
    w_shared_down = dp_gather_rows(shared_down[None], 0).reshape(units, width)
    w_gate, w_up, w_down = (
        lax.all_gather(entry, "dp", axis=1, tiled=True)
        for entry in (expert_gate, expert_up, expert_down)
    )

    table = jnp.concatenate([near[:, width : width + EXTRA], mate[:, width : width + EXTRA]], axis=0)
    routes_all = table[:, 2 : 2 + top].astype(jnp.int32)
    gates_all = join_three([table[:, 2 + k * top : 2 + (k + 1) * top] for k in (1, 2, 3)])
    number = jnp.arange(groups, dtype=jnp.int32)
    back_z = (lax.axis_index("z") - number // 4) % (groups // 4)
    other_y = (number // 2) % 2 != lax.axis_index("y")
    other_core = number % 2 != core
    order = other_core * half + back_z * 2 + other_y

    def blocks_of(entry):
        return entry[:, width + EXTRA :].reshape(half, tokens, -1)[:, : replicas * rows_in]

    spread = jnp.concatenate([blocks_of(near), blocks_of(mate)], axis=0)[order]
    spread = spread.reshape(groups, replicas, rows_in, -1).transpose(1, 0, 2, 3)
    spread = spread.reshape(devices, rows_in, -1)
    small_at = 2 * STATE + HEADS
    small_all = spread[:, :, small_at : small_at + small_lanes].reshape(devices, -1)
    pieces = []
    start = 0
    for size in small_sizes:
        pieces.append(small_all[:, start : start + size].reshape(-1).astype(f32))
        start += size
    conv_w_all = pieces[0].reshape(CONV_CH, KERNEL).T
    conv_b_all, norm_gain_all, mix_gain_all, ffn_gain_all = pieces[1:]
    spread = spread.reshape(devices * rows_in, -1)
    w_step = lax.dynamic_slice_in_dim(spread, 2 * STATE + first_head, heads, 1)
    w_step = jnp.pad(w_step, ((0, 0), (0, EXTRA - heads)))
    widen = ((0, 0), (0, WIDE - own))
    w_in = [spread[:, : 2 * STATE], jnp.pad(pack[:, own : 2 * own], widen), jnp.pad(pack[:, :own], widen), w_step]
    w_in = jnp.concatenate(w_in, axis=1)
    w_shared_gate = pack[:, 2 * own : 2 * own + units]
    w_shared_up = pack[:, 2 * own + units :]

    def own_channels(rows):
        return lax.dynamic_slice_in_dim(rows, first_channel, own, rows.ndim - 1)

    conv = jnp.concatenate([conv_w_all, conv_b_all[None]], axis=0)
    conv = jnp.concatenate([conv[:, INNER:], own_channels(conv)], axis=1)
    conv = jnp.pad(conv, ((0, 8 - conv.shape[0]), (0, CONV_LANES - conv.shape[1])))

    def own_heads(row):
        return lax.dynamic_slice_in_dim(row, first_head, heads, 0)

    def lanes_of(row):
        return jnp.pad(row, (0, WIDE - row.shape[0]))

    rate = -jnp.exp(own_heads(decay_log))
    head = [
        lanes_of(own_heads(step_bias)),
        lanes_of(rate),
        lanes_of(jnp.repeat(own_heads(skip_gain), HEAD_DIM)),
        lanes_of(own_channels(mix_gain_all)),
    ]
    head = jnp.pad(jnp.stack(head), ((0, 4), (0, 0)))
    rate_rows = jnp.broadcast_to(jnp.pad(rate, (0, 8 - heads))[:, None], (8, EXTRA))
    w_out = jnp.pad(w_out, ((0, WIDE - own), (0, 0)))

    input_rows = hidden_in.astype(f32)
    grad_out = cotangent.astype(f32)
    branch = after((grad_out * live).astype(bf16), near)

    pairs = groups // 2
    pair_tokens = 2 * tokens
    pair_slots = 2 * capacity
    numbers = place * local_experts + jnp.arange(local_experts, dtype=jnp.int32)
    named = routes_all[:, None, :] == numbers[None, :, None]
    member = jnp.any(named, axis=2).T.reshape(local_experts, pairs, pair_tokens)
    weight = jnp.sum(jnp.where(named, gates_all[:, None, :], 0.0), axis=2).T
    weight = weight.reshape(local_experts, pairs, pair_tokens)
    below = jnp.triu(jnp.ones((pair_tokens, pair_tokens), bf16))
    rank = matmul(member.astype(bf16), below)
    rank = jnp.where(member, rank.astype(jnp.int32) - 1, -1).transpose(1, 0, 2)
    rank = jnp.pad(rank, ((0, 0), (0, 8 - local_experts), (0, 0)), constant_values=-1)
    weight = jnp.pad(weight.transpose(1, 0, 2), ((0, 0), (0, 8 - local_experts), (0, 0)))
    half_pairs = pairs // 2

    def rows_out(values, first, shared, into=None):
        return dispatch(values, rank, weight, local_experts, pair_slots, first, shared, into)

    mixer = (norm_gain_all[None], w_in, w_out, conv, head)

    def forward(part):
        return lambda token: mixer_forward(after(part, token), width, tokens, *after(mixer, token))

    branch_near, branch_mate, ((mixer_set, w_gate), done_mate, done_near, _) = gather(
        branch, [(mixer, w_gate), forward(mate), forward(near)]
    )
    _, w_in, w_out, conv, head = mixer_set
    normed_mate, proj_mate, mixed_mate, scaled_mate = done_mate
    normed_near, proj_near, mixed_near, scaled_near = done_near
    pairs_sum = scatter_first(mixed_near, mixed_mate)
    d_row, slot_weight, act_grad_near = rows_out(branch_near, 0, (w_shared_down,))
    d_row, slot_weight, act_grad_mate = rows_out(
        branch_mate, half_pairs, (w_shared_down,), (d_row, slot_weight)
    )
    mixed_sum, (_, d_row, w_up, *_) = scatter_last(pairs_sum, [(), d_row, w_up])
    mix_rms = lax.rsqrt(jnp.sum(mixed_sum[:, width:], axis=1, keepdims=True) / INNER + epsilon)
    mixer_out = mixed_sum[:, :width] * mix_rms
    resid = input_rows + live * mixer_out
    ffn_rms = lax.rsqrt(jnp.mean(resid * resid, axis=1, keepdims=True) + epsilon)
    ffn_hat = resid * ffn_rms
    ffn_near, ffn_mate, _ = gather((ffn_hat * ffn_gain_all).astype(bf16))

    expert_in, shared_near, sg_near, su_near = rows_out(
        ffn_near, 0, (act_grad_near, w_shared_gate, w_shared_up)
    )
    expert_in, shared_mate, sg_mate, su_mate = rows_out(
        ffn_mate, half_pairs, (act_grad_mate, w_shared_gate, w_shared_up), (expert_in,)
    )
    act_low, g_low, u_low, d_in_row, expert_row = expert_pass(
        expert_in, d_row, slot_weight, w_gate, w_up, w_down
    )

    half_grad = (((1,), (1,)), ((0,), (0,)))
    grad_down = matmul(act_low, d_row, half_grad).astype(bf16)
    d_in_row, grad_down = tie(d_in_row, grad_down)

    def back_rows(sg, su, first):
        terms = ((sg, w_shared_gate), (su, w_shared_up))
        return combine(d_in_row, rank, terms, pair_slots, first, True)

    grad_ffn_mate = back_rows(sg_mate, su_mate, half_pairs)
    grad_ffn_near = back_rows(sg_near, su_near, 0)
    pairs_sum = scatter_first(grad_ffn_near, grad_ffn_mate)

    def leaving_of(part):
        return lambda token: matmul(after(expert_in, token), part, half_grad).astype(bf16)

    grad_ffn, leaving = scatter_last(pairs_sum, [leaving_of(g_low), leaving_of(u_low)])
    grad_down, grad_gate, grad_up = (
        lax.psum_scatter(entry, "dp", scatter_dimension=1, tiled=True)
        for entry in (grad_down, *leaving[:2])
    )

    grad_ffn_gain = jnp.sum(grad_ffn * ffn_hat, axis=0)
    scaled_ffn = grad_ffn * ffn_gain_all
    grad_resid = grad_out + ffn_rms * (
        scaled_ffn - ffn_hat * jnp.mean(scaled_ffn * ffn_hat, axis=1, keepdims=True)
    )
    d_mixer = (grad_resid * live).astype(bf16).astype(f32)
    inner_term = jnp.sum(d_mixer * mixer_out, axis=1, keepdims=True) * mix_rms * mix_rms / INNER
    inner_pack = jnp.pad(jnp.concatenate(split_three(inner_term), axis=1), ((0, 0), (0, EXTRA - 3)))
    d_mixer_pack = jnp.concatenate([(d_mixer * mix_rms).astype(bf16), inner_pack], axis=1)

    def out_rows(shared_act, first):
        def work(token):
            terms = ((shared_act, w_shared_down),)
            return combine(after(expert_row, token), rank, terms, pair_slots, first, False)

        return work

    turned = (((0,), (0,)), ((), ()))

    def of_halves(left, right):
        return matmul(left[0], right[0], turned) + matmul(left[1], right[1], turned)

    def shared_grads_of(token):
        halves = after(((branch_near, branch_mate), (ffn_near, ffn_mate)), token)
        return (
            of_halves((shared_near, shared_mate), halves[0]),
            of_halves(halves[1], (sg_near, sg_mate)),
            of_halves(halves[1], (su_near, su_mate)),
        )

    d_mixer_near, d_mixer_mate, (out_mate, out_near, shared_grads, grad_down) = gather(
        d_mixer_pack,
        [
            out_rows(shared_mate, half_pairs),
            out_rows(shared_near, 0),
            shared_grads_of,
            lambda token: after(grad_down, token).astype(f32),
        ],
    )
    grad_shared_down, grad_shared_g, grad_shared_u = shared_grads
    grad_shared_gu = dp_scatter_rows(jnp.concatenate([grad_shared_g, grad_shared_u], axis=1), 0)
    out_pairs = scatter_first(out_near, out_mate)
    (d_mixer_near, d_mixer_mate), out_pairs = tie((d_mixer_near, d_mixer_mate), out_pairs)

    def backward(grads, part, proj):
        return mixer_backward(grads, part, proj, width, tokens, w_in, w_out, conv, head, rate_rows)

    done_mate = backward(d_mixer_mate, mate, proj_mate)
    out_there = {step: swap(out_pairs[step][1], "y") for step in (1, 2)}
    d_mixer_near, out_pairs, out_there, done_mate = tie(d_mixer_near, out_pairs, out_there, done_mate)
    done_near = backward(d_mixer_near, near, proj_near)
    out_total = ring_step(add_low(out_pairs[1][0], out_there[1]), out_pairs, out_there, 1)
    out_there |= {step: swap(out_pairs[step][1], "y") for step in (3, 0)}
    moved = swap(done_mate[0], "core")
    done_near, out_total, out_there, moved = tie(done_near, out_total, out_there, moved)
    normed_grad_mate, proj_low_mate, conv_mate, head_mate = done_mate
    normed_grad_near, proj_low_near, conv_near, head_near = done_near
    pairs_sum = scatter_first(normed_grad_near, normed_grad_mate, moved)

    def to_owner(part):
        rows_part = jnp.zeros((part.shape[0], CONV_CH), f32)
        values = part[:, 2 * STATE : 2 * STATE + own]
        rows_part = lax.dynamic_update_slice_in_dim(rows_part, values, first_channel, 1)
        rows_part = lax.dynamic_update_slice_in_dim(rows_part, part[:, : 2 * STATE], INNER, 1)
        return rows_part.reshape(part.shape[0], devices, -1).transpose(1, 0, 2).reshape(devices, -1)

    def head_row(part):
        return lax.dynamic_update_slice_in_dim(jnp.zeros((HEADS,), f32), part, first_head, 0)

    def small_sums(conv_grads, head_grads):
        head_grads = jnp.sum(head_grads.reshape(3, 8, EXTRA)[:, :heads], axis=2)
        head_rows = [head_row(entry) for entry in (head_grads[0] * rate, *head_grads[1:])]
        return jnp.concatenate(
            [
                to_owner(conv_grads[: KERNEL + 1]),
                grad_ffn_gain.reshape(devices, -1),
                jnp.broadcast_to(jnp.concatenate(head_rows)[None], (devices, 3 * HEADS)),
            ],
            axis=1,
        )

    crossing = replicas == 2
    here = lax.axis_index("dp")
    normed_rows = width // 2 if crossing else width

    def input_grad(where, token):
        parts = after((normed_near, normed_mate), token)
        if crossing:
            parts = [lax.dynamic_slice_in_dim(part, where * normed_rows, normed_rows, 1) for part in parts]
        return of_halves(parts, (proj_low_near, proj_low_mate))

    def piece(array, index, token):
        extent = array.shape[0] // 3
        return swap(after(array[index * extent : (index + 1) * extent], token), "dp")

    pieces = []

    def window_one(token):
        return input_grad(1 - here, token).astype(bf16)

    def window_two(token):
        conv_parts, head_parts = after(((conv_mate, conv_near), (head_mate, head_near)), token)
        return small_sums(sum(conv_parts), sum(head_parts))

    def window_three(token):
        parts = after((scaled_near, scaled_mate), token)
        return of_halves(parts, (d_mixer_near[:, :width], d_mixer_mate[:, :width]))[:own]

    there = scatter_beside(pairs_sum)
    total = add_low(pairs_sum[1][0], there[1])
    total, leaving = tie(total, window_one(pairs_sum))
    works = (window_two, window_three, lambda token: input_grad(here, token))
    finished = []
    for index, work in enumerate(works):
        following = ring_step(total, pairs_sum, there, index + 1)
        across = piece(leaving, index, total) if crossing else ()
        if index < 2:
            out_total = ring_step(after(out_total, total), out_pairs, out_there, index + 2)
        result = work(total)
        total, across, out_total, result = tie(following, across, out_total, result)
        pieces.append(across)
        finished.append(result)
    grad_normed, branch_sum = total, out_total
    sums, grad_out_rows, grad_w_in = finished
    output = (resid + live * branch_sum).astype(bf16)
    grad_gate, grad_up = grad_gate.astype(f32), grad_up.astype(f32)

    if crossing:
        grad_w_in = grad_w_in + jnp.concatenate(pieces, axis=0).astype(f32)
    else:
        grad_w_in = lax.psum_scatter(leaving, "dp", scatter_dimension=0, tiled=True)
    grad_pack = jnp.concatenate([grad_w_in.astype(bf16), grad_shared_gu.astype(bf16)], axis=1)
    grad_pack = grad_pack.reshape(groups, rows_in, -1)
    grad_pack = lax.all_to_all(grad_pack, GROUP, split_axis=0, concat_axis=0, tiled=True).astype(f32)

    def from_place(block):
        block = block.reshape(half, 2, rows_in, block.shape[2]).transpose(2, 1, 0, 3)
        return block.reshape(rows_in, -1)

    def from_unit(block):
        block = block.reshape(groups, rows_in, replicas, unit).transpose(1, 2, 0, 3)
        return block.reshape(rows_in, hidden_units)

    value_at, gate_at, step_at = 2 * STATE, CONV_LANES, CONV_LANES + WIDE
    grad_in_proj = jnp.concatenate(
        [
            from_place(grad_pack[:, :, gate_at : gate_at + own]),
            from_place(grad_pack[:, :, value_at : value_at + own]),
            jnp.sum(grad_pack[:, :, : 2 * STATE], axis=0),
            from_place(grad_pack[:, :, step_at : step_at + heads]),
        ],
        axis=1,
    )
    grad_shared_gate = from_unit(grad_pack[:, :, PROJ_LANES : PROJ_LANES + units])
    grad_shared_up = from_unit(grad_pack[:, :, PROJ_LANES + units :])
    grad_shared_down = dp_scatter_rows(grad_shared_down.reshape(replicas, unit, width), 0)[0]
    if replicas == 2:
        mine = lax.axis_index("dp") == core
        received = swap(grad_out_rows.astype(bf16), "dp").astype(f32)
        total = (grad_out_rows + received).reshape(2, own // 2, width)
        passed = swap(lax.dynamic_index_in_dim(total, 1 - core, 0, keepdims=False), "core")
        grad_out_proj = jnp.where(mine, lax.dynamic_index_in_dim(total, core, 0, keepdims=False), passed)
    else:
        full = jnp.zeros((INNER, width), f32)
        full = lax.dynamic_update_slice_in_dim(full, grad_out_rows, first_channel, 0)
        grad_out_proj = lax.psum_scatter(full, ALL, scatter_dimension=0, tiled=True)
    grad_mix_gain = jnp.sum(grad_out_proj * out_proj.astype(f32), axis=1) / mix_gain.astype(f32)
    grad_norm_gain = jnp.sum(grad_in_proj * in_proj.astype(f32), axis=1) / norm_gain.astype(f32)

    sums = lax.all_to_all(sums, ALL, split_axis=0, concat_axis=0, tiled=True)
    sums = jnp.sum(sums, axis=0)
    channels = CONV_CH // devices
    grad_conv_weight = sums[: KERNEL * channels].reshape(KERNEL, channels).T
    grad_conv_bias = sums[KERNEL * channels : (KERNEL + 1) * channels]
    at = (KERNEL + 1) * channels
    grad_ffn_gain = sums[at : at + rows_in]
    at += rows_in
    grad_decay, grad_stepb, grad_skip = (sums[at + k * HEADS : at + (k + 1) * HEADS] for k in range(3))

    in_rms = lax.rsqrt(jnp.mean(input_rows * input_rows, axis=1, keepdims=True) + epsilon)
    in_hat = input_rows * in_rms
    scaled_in = grad_normed * norm_gain_all
    grad_input = grad_resid + in_rms * (
        scaled_in - in_hat * jnp.mean(scaled_in * in_hat, axis=1, keepdims=True)
    )
    return (
        output,
        grad_input,
        grad_in_proj,
        grad_out_proj,
        grad_conv_weight,
        grad_conv_bias,
        grad_norm_gain,
        grad_mix_gain,
        grad_ffn_gain,
        grad_shared_gate,
        grad_shared_up,
        grad_shared_down,
        grad_gate,
        grad_up,
        grad_down,
        grad_decay,
        grad_stepb,
        grad_skip,
    )


def solution(mesh):
    replicas, groups = mesh.shape["dp"], mesh.shape["expert"]
    inner = Mesh(mesh.devices.reshape(replicas, groups // 4, 2, 2), ALL)
    flat = P(ALL)
    expert = P(GROUP, "dp", None)
    return jax.shard_map(
        local,
        mesh=inner,
        in_specs=(flat,) * 15 + (expert,) * 3 + (P(),) * 3,
        out_specs=(flat,) * 12 + (expert,) * 3 + (P(),) * 3,
        check_vma=False,
    )
```

```python
import jax
import jax.numpy as jnp
from jax import lax
from jax.experimental import pallas as pl
from jax.experimental.pallas import tpu as pltpu
from jax.sharding import Mesh, PartitionSpec as P

HEADS = 48
HEAD_DIM = 64
STATE = 128
KERNEL = 4
SEQ_SLOTS = 3
INNER = 3072
CONV_CH = 3328
EXTRA = 128

epsilon = 1e-05
bf16 = jnp.bfloat16
f32 = jnp.float32
GROUP = ("z", "y", "core")
ALL = ("dp", "z", "y", "core")


def matmul(left, right, dims=None, precision=None):
    if dims is None:
        dims = (((left.ndim - 1,), (0,)), ((), ()))
    return lax.dot_general(left, right, dims, precision=precision, preferred_element_type=f32)


def swap(value, axis):
    return lax.ppermute(value, axis, [(0, 1), (1, 0)])


def ring(value):
    size = lax.axis_size("z")
    return lax.ppermute(value, "z", [(k, (k + 1) % size) for k in range(size)])


def after(value, *earlier):
    return lax.optimization_barrier((value, earlier))[0]


def split_three(value):
    high = lax.reduce_precision(value, 8, 7)
    rest = value - high
    middle = lax.reduce_precision(rest, 8, 7)
    return high.astype(bf16), middle.astype(bf16), (rest - middle).astype(bf16)


def join_three(parts):
    return parts[0].astype(f32) + parts[1].astype(f32) + parts[2].astype(f32)


def tie(value, *others):
    return lax.optimization_barrier((value, *others))


def work_of(entry, token):
    return entry(token) if callable(entry) else entry


def gather(block, beside_work=()):
    size = lax.axis_size("z")
    beside_work = (list(beside_work) + [()] * size)[:size]
    blocks = []
    for step in range(size):
        following = ring(block) if step < size - 1 else ()
        near = swap(block, "y")
        work = work_of(beside_work[step], block)
        following, near, beside_work[step] = tie(following, near, work)
        blocks += [block, near]
        block = following
    own = jnp.concatenate(blocks, axis=0)
    return own, swap(own, "core"), beside_work


def add_low(left, right):
    return (left.astype(f32) + right.astype(f32)).astype(bf16)


def scatter_first(near, mate, moved=None):
    size = lax.axis_size("z")
    shape = (size, 2, near.shape[0] // (2 * size), near.shape[1])
    there = (swap(mate, "core") if moved is None else moved).reshape(shape)
    near = near.reshape(shape)
    pairs = [add_low(near[step], there[step]) for step in range(size)]
    return pairs


def scatter_beside(pairs):
    size = len(pairs)
    order = list(range(1, size)) + [0]
    there = {step: swap(pairs[step][1], "y") for step in order}
    return [there[step] for step in range(size)]


def ring_step(total, pairs, there, step):
    at = (step + 1) % len(pairs)
    total = ring(total).astype(f32) + (pairs[at][0].astype(f32) + there[at].astype(f32))
    return total.astype(bf16) if at else total


def scatter_last(pairs, beside_work=(), there=None):
    size = len(pairs)
    beside_work = (list(beside_work) + [()] * size)[:size]
    there = there or scatter_beside(pairs)
    total = add_low(pairs[1][0], there[1])
    token = pairs
    for step in range(1, size):
        total, beside_work[step - 1] = tie(total, work_of(beside_work[step - 1], token))
        token = total
        total = ring_step(total, pairs, there, step)
    total, beside_work[-1] = tie(total, work_of(beside_work[-1], token))
    return total, beside_work


def dp_gather_rows(value, axis):
    if lax.axis_size("dp") != 2:
        return lax.all_gather(value, "dp", axis=axis, tiled=True)
    other = swap(value, "dp")
    first = lax.axis_index("dp") == 0
    return jnp.concatenate(
        [jnp.where(first, value, other), jnp.where(first, other, value)], axis=axis
    )


def dp_scatter_rows(value, axis, hold=()):
    count = lax.axis_size("dp")
    if count != 2:
        return lax.psum_scatter(value.astype(bf16), "dp", scatter_dimension=axis, tiled=True).astype(f32)
    place = lax.axis_index("dp")
    extent = value.shape[axis] // count
    sent = lax.dynamic_slice_in_dim(value, (1 - place) * extent, extent, axis).astype(bf16)
    kept = lax.dynamic_slice_in_dim(value, place * extent, extent, axis)
    received, kept, hold = tie(swap(sent, "dp"), kept, hold)
    return kept + received.astype(f32)


def params(steps=1):
    return pltpu.CompilerParams(
        dimension_semantics=("arbitrary",) * steps, vmem_limit_bytes=56 * 1024 * 1024
    )


def cost(micros):
    return pl.CostEstimate(
        flops=int(micros * 1.1e9), bytes_accessed=int(micros * 3.5e6), transcendentals=0
    )


def whole(array):
    return pl.BlockSpec(array.shape, lambda step: (0,) * array.ndim)


def sigmoid(value):
    return 1.0 / (1.0 + jnp.exp(-value))


def halves_of(value):
    high = value.astype(bf16)
    return high, (value - high.astype(f32)).astype(bf16)


def exact(left, right, dims):
    (left_high, left_low), (right_high, right_low) = halves_of(left), halves_of(right)

    def dot(one, other):
        return lax.dot_general(one, other, (dims, ((), ())), preferred_element_type=f32)

    return dot(left_high, right_high) + (dot(left_high, right_low) + dot(left_low, right_high))


def rows_of(array, index):
    return array[index : index + 1]


WIDE = 256
CONV_LANES = 2 * STATE + WIDE
PROJ_LANES = CONV_LANES + 2 * EXTRA


def triangle(count):
    row = lax.broadcasted_iota(jnp.int32, (count, count), 0)
    column = lax.broadcasted_iota(jnp.int32, (count, count), 1)
    return row - column


def block_scan(proj, place, conv, head):
    heads = HEADS // 16
    count = proj.shape[0]
    taps = [proj[:, :CONV_LANES]]
    total = rows_of(conv, KERNEL) + rows_of(conv, KERNEL - 1) * taps[0]
    for offset in range(1, KERNEL):
        inside = (place >= offset).astype(f32)
        taps.append(pltpu.roll(taps[0], offset, 0) * inside)
        total = total + rows_of(conv, KERNEL - 1 - offset) * taps[offset]
    conv_sig = sigmoid(total)
    conv_out = total * conv_sig
    b_part, c_part = conv_out[:, :STATE], conv_out[:, STATE : 2 * STATE]
    raw = proj[:, CONV_LANES + EXTRA :] + rows_of(head, 0)[:, :EXTRA]
    step = jnp.maximum(raw, 0.0) + jnp.log1p(jnp.exp(-jnp.abs(raw)))
    distance = triangle(count)
    lower = (distance >= 0).astype(f32)
    cumul = exact(lower, step * rows_of(head, 1)[:, :EXTRA], ((1,), (0,)))
    cumul_rows = cumul.T
    step_rows = step.T
    scores = exact(c_part, b_part, ((1,), (1,)))
    reach = jnp.logical_and(distance >= 0, distance.astype(f32) <= place)
    lane = lax.broadcasted_iota(jnp.int32, (1, 2 * HEAD_DIM), 1)
    decays, values, scan = [], [], [None] * (WIDE // EXTRA)
    for index in range(heads):
        tile = index // 2
        spread = cumul[:, index : index + 1] - rows_of(cumul_rows, index)
        decay = jnp.exp(jnp.where(reach, spread, -1e30))
        mine = (lane // HEAD_DIM == index % 2).astype(f32)
        at = 2 * STATE + tile * EXTRA
        value = conv_out[:, at : at + EXTRA] * mine
        mixing = decay * scores * rows_of(step_rows, index)
        part = exact(mixing, value, ((1,), (0,)))
        scan[tile] = part if scan[tile] is None else scan[tile] + part
        decays.append((decay, mixing))
        values.append((value, mine))
    scan = jnp.concatenate(scan, axis=1) + rows_of(head, 2) * conv_out[:, 2 * STATE :]
    turned = pltpu.roll(proj[:, CONV_LANES - EXTRA : CONV_LANES], HEAD_DIM, 1)
    turned = jnp.where(lane < HEAD_DIM, turned, 0.0)
    gate = jnp.concatenate([proj[:, CONV_LANES : CONV_LANES + EXTRA], turned], axis=1)
    gate_sig = sigmoid(gate)
    gated = scan * (gate * gate_sig)
    return dict(
        taps=taps, total=total, conv_sig=conv_sig, conv_out=conv_out, raw=raw, step_rows=step_rows,
        scores=scores, decays=decays, values=values, scan=scan, gate=gate, gate_sig=gate_sig,
        gated=gated, lower=lower,
    )


def mixer_forward_kernel(
    count, tokens_ref, beside_ref, gain_ref, w_in_ref, w_out_ref, conv_ref, head_ref,
    normed_ref, proj_ref, part_ref, scaled_ref,
):
    rows = tokens_ref[...].astype(f32)
    normed = rows * lax.rsqrt(jnp.mean(rows * rows, axis=1, keepdims=True) + epsilon) * gain_ref[...]
    normed = normed.astype(bf16)
    normed_ref[...] = normed
    proj_ref[...] = jnp.dot(normed, w_in_ref[...], preferred_element_type=f32)
    conv, head = conv_ref[...], head_ref[...]
    width = tokens_ref.shape[1]
    for index in range(tokens_ref.shape[0] // count):
        part = pl.ds(index * count, count)
        place = beside_ref[part, :].astype(f32)[:, 1:2]
        found = block_scan(proj_ref[part, :], place, conv, head)
        gated = found["gated"]
        scaled_ref[part, :] = (gated * rows_of(head, 3)).astype(bf16)
        square = gated * gated
        square = square[:, :EXTRA] + square[:, EXTRA:]
        part_ref[part, width:] = square.astype(bf16)
    part_ref[:, :width] = jnp.dot(
        scaled_ref[...], w_out_ref[...], preferred_element_type=f32
    ).astype(bf16)


def mixer_forward(gathered, width, count, gain, w_in, w_out, conv, head):
    total = gathered.shape[0]
    rows = 4 * count
    lanes = width // EXTRA

    def rows_spec(extent, column=0):
        return pl.BlockSpec((rows, extent), lambda step: (step, column))

    return pl.pallas_call(
        lambda *refs: mixer_forward_kernel(count, *refs),
        grid=(total // rows,),
        in_specs=[rows_spec(width), rows_spec(EXTRA, lanes)]
        + [whole(entry) for entry in (gain, w_in, w_out, conv, head)],
        out_specs=[rows_spec(width), rows_spec(PROJ_LANES), rows_spec(width + EXTRA), rows_spec(WIDE)],
        out_shape=[
            jax.ShapeDtypeStruct((total, width), bf16),
            jax.ShapeDtypeStruct((total, PROJ_LANES), f32),
            jax.ShapeDtypeStruct((total, width + EXTRA), bf16),
            jax.ShapeDtypeStruct((total, WIDE), bf16),
        ],
        compiler_params=params(),
        cost_estimate=cost(total / 80),
        name="mixer_forward",
    )(gathered, gathered, gain, w_in, w_out, conv, head)


def mixer_backward_kernel(
    count, grad_ref, inner_ref, beside_ref, proj_ref, w_in_ref, w_out_ref, conv_ref, head_ref, rate_ref,
    *refs,
):
    normed_ref, proj_grad_ref, conv_grad_ref, head_grad_ref = refs[-4:]
    heads = HEADS // 16
    conv, head = conv_ref[...], head_ref[...]

    @pl.when(pl.program_id(0) == 0)
    def _():
        conv_grad_ref[...] = jnp.zeros_like(conv_grad_ref)
        head_grad_ref[...] = jnp.zeros_like(head_grad_ref)

    grad_mixed = lax.dot_general(
        grad_ref[...], w_out_ref[...], (((1,), (1,)), ((), ())), preferred_element_type=f32
    )
    lane = lax.broadcasted_iota(jnp.int32, (1, EXTRA), 1)
    for index in range(grad_ref.shape[0] // count):
        part = pl.ds(index * count, count)
        place = beside_ref[part, :].astype(f32)[:, 1:2]
        found = block_scan(proj_ref[part, :], place, conv, head)
        inner = inner_ref[part, :].astype(f32)
        inner = inner[:, 0:1] + inner[:, 1:2] + inner[:, 2:3]
        gate, gate_sig, scan = found["gate"], found["gate_sig"], found["scan"]
        d_gated = grad_mixed[index * count : (index + 1) * count] * rows_of(head, 3) - found["gated"] * inner
        d_scan = d_gated * (gate * gate_sig)
        d_gate = d_gated * scan * (gate_sig * (1.0 + gate * (1.0 - gate_sig)))
        conv_out = found["conv_out"]
        d_values = [None] * (WIDE // EXTRA)
        d_scores = jnp.zeros((count, count), f32)
        column_sums = jnp.zeros((count, EXTRA), f32)
        direct, taken = [], []
        for number in range(heads):
            tile = number // 2
            decay, mixing = found["decays"][number]
            value, mine = found["values"][number]
            d_part = d_scan[:, tile * EXTRA : (tile + 1) * EXTRA]
            back = exact(mixing, d_part, ((0,), (0,))) * mine
            d_values[tile] = back if d_values[tile] is None else d_values[tile] + back
            d_mixing = exact(d_part, value, ((1,), (1,)))
            d_decayed = d_mixing * decay
            d_scores = d_scores + d_decayed * rows_of(found["step_rows"], number)
            d_spread = d_mixing * mixing
            direct.append(jnp.sum(d_decayed * found["scores"], axis=0, keepdims=True))
            taken.append(jnp.sum(d_spread, axis=0, keepdims=True))
            sums = jnp.sum(d_spread, axis=1, keepdims=True)
            column_sums = column_sums + jnp.where(lane == number, sums, 0.0)
            head_grad_ref[16 + number : 17 + number, :] += jnp.sum(d_part * value, axis=0, keepdims=True)
        d_values = jnp.concatenate(d_values, axis=1) + rows_of(head, 2) * d_scan
        empty = jnp.zeros((8 - heads, count), f32)
        d_cumul = column_sums.T[:8] - jnp.concatenate(taken + [empty], axis=0)
        d_rated = exact(d_cumul, found["lower"], ((1,), (0,)))
        step_rows = found["step_rows"][:8]
        d_step = jnp.concatenate(direct + [empty], axis=0) + d_rated * rate_ref[...]
        d_raw = d_step * sigmoid(found["raw"]).T[:8]
        head_grad_ref[0:8, :] += d_rated * step_rows
        head_grad_ref[8:16, :] += d_raw
        d_raw = jnp.concatenate([d_raw, jnp.zeros((EXTRA - 8, count), f32)], axis=0).T
        d_b = exact(d_scores, conv_out[:, STATE : 2 * STATE], ((0,), (0,)))
        d_c = exact(d_scores, conv_out[:, :STATE], ((1,), (0,)))
        d_out = jnp.concatenate([d_b, d_c, d_values], axis=1)
        conv_sig = found["conv_sig"]
        d_total = d_out * (conv_sig * (1.0 + found["total"] * (1.0 - conv_sig)))
        conv_grad_ref[KERNEL : KERNEL + 1, :] += jnp.sum(d_total, axis=0, keepdims=True)
        d_conv = rows_of(conv, KERNEL - 1) * d_total
        for offset in range(KERNEL):
            row = KERNEL - 1 - offset
            conv_grad_ref[row : row + 1, :] += jnp.sum(d_total * found["taps"][offset], axis=0, keepdims=True)
            if offset:
                kept = d_total * (place >= offset).astype(f32)
                d_conv = d_conv + rows_of(conv, row) * pltpu.roll(kept, count - offset, 0)
        shared_tile = d_conv[:, CONV_LANES - EXTRA :] + pltpu.roll(d_gate[:, EXTRA:], HEAD_DIM, 1)
        d_proj = [d_conv[:, : CONV_LANES - EXTRA], shared_tile, d_gate[:, :EXTRA], d_raw]
        proj_grad_ref[part, :] = jnp.concatenate(d_proj, axis=1).astype(bf16)
    normed_ref[...] = lax.dot_general(
        proj_grad_ref[...], w_in_ref[...], (((1,), (1,)), ((), ())), preferred_element_type=f32
    ).astype(bf16)


def mixer_backward(grads, gathered, proj, width, count, w_in, w_out, conv, head, rate, first, into=()):
    total = grads.shape[0]
    rows = 4 * count
    lanes = width // EXTRA

    def rows_spec(extent, column=0):
        return pl.BlockSpec((rows, extent), lambda step: (first + step, column))

    conv_shape = jax.ShapeDtypeStruct(conv.shape, f32)
    head_shape = jax.ShapeDtypeStruct((24, EXTRA), f32)
    in_specs = [rows_spec(width), rows_spec(EXTRA, lanes), rows_spec(EXTRA, lanes), rows_spec(PROJ_LANES)]
    in_specs += [whole(entry) for entry in (w_in, w_out, conv, head, rate)]
    aliases = {len(in_specs) + index: index for index in range(len(into))}
    in_specs += [pl.BlockSpec(memory_space=pl.ANY)] * len(into)
    return pl.pallas_call(
        lambda *refs: mixer_backward_kernel(count, *refs),
        grid=(1,),
        in_specs=in_specs,
        out_specs=[rows_spec(width), rows_spec(PROJ_LANES), whole(conv_shape), whole(head_shape)],
        out_shape=[
            jax.ShapeDtypeStruct((total, width), bf16),
            jax.ShapeDtypeStruct((total, PROJ_LANES), bf16),
            conv_shape,
            head_shape,
        ],
        input_output_aliases=aliases,
        compiler_params=params(),
        cost_estimate=cost(10),
        name="mixer_backward",
    )(grads, grads, gathered, proj, w_in, w_out, conv, head, rate, *into)


def selection(rank_ref, experts, slots):
    number = lax.broadcasted_iota(jnp.int32, (slots, rank_ref.shape[2]), 0)
    return [rank_ref[0, k : k + 1, :] == number for k in range(experts)]


def dispatch_kernel(experts, slots, grads, rank_ref, weight_ref, values_ref, *refs):
    chosen = selection(rank_ref, experts, slots)
    select = jnp.concatenate([entry.astype(f32) for entry in chosen], axis=0).astype(bf16)
    values = values_ref[...]
    rows = jnp.dot(select, values, preferred_element_type=f32)
    if grads:
        down_ref = refs[0]
        out_ref, weights_ref, act_grad_ref = refs[-3:]
        act_grad_ref[...] = lax.dot_general(
            values, down_ref[...], (((1,), (1,)), ((), ())), preferred_element_type=f32
        )
    else:
        act_grad_ref, gate_ref, up_ref = refs[:3]
        out_ref, act_ref, g_ref, u_ref = refs[-4:]
        gate = jnp.dot(values, gate_ref[...], preferred_element_type=f32)
        up = jnp.dot(values, up_ref[...], preferred_element_type=f32)
        sig = sigmoid(gate)
        silu = gate * sig
        d_act = act_grad_ref[...]
        act_ref[...] = (silu * up).astype(bf16)
        g_ref[...] = (d_act * up * (sig * (1.0 + gate * (1.0 - sig)))).astype(bf16)
        u_ref[...] = (d_act * silu).astype(bf16)
    for k in range(experts):
        part = rows[k * slots : (k + 1) * slots]
        if grads:
            own = jnp.where(chosen[k], weight_ref[0, k : k + 1, :], 0.0)
            own = jnp.sum(own, axis=1, keepdims=True)
            part = part * own
            weights_ref[k] = jnp.broadcast_to(own, (slots, EXTRA))
        out_ref[k] = part.astype(bf16)


def dispatch(values, rank, weight, experts, slots, first, shared, into=None):
    pairs, _, tokens = rank.shape
    count = values.shape[0] // tokens
    width = values.shape[1]
    grads = len(shared) == 1
    hidden = shared[0].shape[0] if grads else shared[0].shape[1]

    def slots_spec(extent):
        return pl.BlockSpec((experts, slots, extent), lambda step: (0, first + step, 0))

    def rows_spec(extent):
        return pl.BlockSpec((tokens, extent), lambda step: (step, 0))

    rank_spec = pl.BlockSpec((1,) + rank.shape[1:], lambda step: (first + step, 0, 0))
    in_specs = [rank_spec, rank_spec, rows_spec(width)]
    out_specs = [slots_spec(width)]
    shapes = [jax.ShapeDtypeStruct((experts, pairs * slots, width), bf16)]
    small = (values.shape[0], hidden)
    if grads:
        in_specs += [whole(shared[0])]
        out_specs += [slots_spec(EXTRA), rows_spec(hidden)]
        shapes += [
            jax.ShapeDtypeStruct((experts, pairs * slots, EXTRA), f32),
            jax.ShapeDtypeStruct(small, f32),
        ]
    else:
        in_specs += [rows_spec(hidden), whole(shared[1]), whole(shared[2])]
        out_specs += [rows_spec(hidden)] * 3
        shapes += [jax.ShapeDtypeStruct(small, bf16)] * 3
    aliases = {}
    into = () if into is None else tuple(into)
    for index, entry in enumerate(into):
        aliases[len(in_specs)] = index
        in_specs.append(pl.BlockSpec(memory_space=pl.ANY))
    return pl.pallas_call(
        lambda *refs: dispatch_kernel(experts, slots, grads, *refs),
        grid=(count,),
        in_specs=in_specs,
        out_specs=out_specs,
        out_shape=shapes,
        input_output_aliases=aliases,
        compiler_params=params(),
        cost_estimate=cost(5),
        name="dispatch",
    )(rank, weight, values, *shared, *into)


def combine_kernel(experts, slots, terms, turned, rank_ref, rows_ref, *refs):
    out_ref = refs[-1]
    chosen = selection(rank_ref, experts, slots)
    select = jnp.concatenate([entry.astype(f32) for entry in chosen], axis=0).astype(bf16)
    rows = jnp.concatenate([rows_ref[k] for k in range(experts)], axis=0)
    total = lax.dot_general(select, rows, (((0,), (0,)), ((), ())), preferred_element_type=f32)
    dims = ((1,), (1,)) if turned else ((1,), (0,))
    for k in range(terms):
        total = total + lax.dot_general(
            refs[2 * k][...], refs[2 * k + 1][...], (dims, ((), ())), preferred_element_type=f32
        )
    out_ref[...] = total.astype(bf16)


def combine(rows, rank, terms, slots, first, turned):
    pairs, _, tokens = rank.shape
    experts, _, width = rows.shape
    count = terms[0][0].shape[0] // tokens
    specs, operands = [], []
    for left, right in terms:
        specs += [pl.BlockSpec((tokens, left.shape[1]), lambda step: (step, 0)), whole(right)]
        operands += [left, right]
    return pl.pallas_call(
        lambda *refs: combine_kernel(experts, slots, len(terms), turned, *refs),
        grid=(count,),
        in_specs=[
            pl.BlockSpec((1,) + rank.shape[1:], lambda step: (first + step, 0, 0)),
            pl.BlockSpec((experts, slots, width), lambda step: (0, first + step, 0)),
        ]
        + specs,
        out_specs=pl.BlockSpec((tokens, width), lambda step: (step, 0)),
        out_shape=jax.ShapeDtypeStruct((count * tokens, width), bf16),
        compiler_params=params(),
        cost_estimate=cost(5),
        name="combine",
    )(rank, rows, *operands)


def expert_kernel(
    rows_ref, grad_ref, weight_ref, gate_ref, up_ref, down_ref, act_ref, g_ref, u_ref, back_ref, out_ref
):
    rows, gate_w, up_w, down_w = rows_ref[0], gate_ref[0], up_ref[0], down_ref[0]
    turned = (((1,), (1,)), ((), ()))
    gate = jnp.dot(rows, gate_w, preferred_element_type=f32)
    up = jnp.dot(rows, up_w, preferred_element_type=f32)
    sig = sigmoid(gate)
    silu = gate * sig
    act = (silu * up).astype(bf16)
    d_act = lax.dot_general(grad_ref[0], down_w, turned, preferred_element_type=f32)
    d_gate = (d_act * up * (sig * (1.0 + gate * (1.0 - sig)))).astype(bf16)
    d_up = (d_act * silu).astype(bf16)
    act_ref[0], g_ref[0], u_ref[0] = act, d_gate, d_up
    back = lax.dot_general(d_gate, gate_w, turned, preferred_element_type=f32)
    back = back + lax.dot_general(d_up, up_w, turned, preferred_element_type=f32)
    back_ref[0] = back.astype(bf16)
    out = jnp.dot(act, down_w, preferred_element_type=f32) * weight_ref[0][:, :1]
    out_ref[0] = out.astype(bf16)


def expert_pass(rows, grads, weights, gate, up, down):
    experts, lanes, width = rows.shape
    hidden = gate.shape[2]

    def each(entry):
        return pl.BlockSpec((1,) + entry.shape[1:], lambda step: (step, 0, 0))

    inputs = (rows, grads, weights, gate, up, down)
    small = jax.ShapeDtypeStruct((experts, lanes, hidden), bf16)
    large = jax.ShapeDtypeStruct((experts, lanes, width), bf16)
    outputs = [small] * 3 + [large] * 2
    return pl.pallas_call(
        expert_kernel,
        grid=(experts,),
        in_specs=[each(entry) for entry in inputs],
        out_specs=[each(entry) for entry in outputs],
        out_shape=outputs,
        compiler_params=params(),
        cost_estimate=cost(20),
        name="expert_pass",
    )(*inputs)


def unpack_kernel(half, own, heads, unit, pack_ref, weight_ref, grad_ref, gate_ref, up_ref, sums_ref):
    rows = weight_ref.shape[0]
    lane = lax.broadcasted_iota(jnp.int32, (1, EXTRA), 1)
    low = lane < HEAD_DIM
    groups = 2 * half
    sums = jnp.zeros((rows, EXTRA), f32)

    def tile(index, number):
        return pack_ref[index, :, number * EXTRA : (number + 1) * EXTRA].astype(f32)

    def put(start, value):
        grad_ref[:, start : start + EXTRA] = value
        return value * weight_ref[:, start : start + EXTRA].astype(f32)

    def turn(value, amount):
        amount %= EXTRA
        return pltpu.roll(value, amount, 1) if amount else value

    steps = jnp.zeros((rows, EXTRA), f32)
    shared_b = [jnp.zeros((rows, EXTRA), f32) for _ in range(2 * STATE // EXTRA)]
    for core in range(2):
        for column in range(0, half, 2):
            one, two = 2 * column + core, 2 * column + 2 + core
            values = (tile(one, 2), tile(one, 3), tile(two, 2), tile(two, 3))
            gates = (tile(one, 4), turn(values[1], HEAD_DIM), tile(two, 4), turn(values[3], HEAD_DIM))
            at = core * (INNER // 2) + column * own
            for start, (first, rest, other, other_rest) in ((at, gates), (INNER + at, values)):
                turned = turn(other, HEAD_DIM)
                sums = sums + put(start, first)
                sums = sums + put(start + EXTRA, jnp.where(low, rest, turned))
                sums = sums + put(start + 2 * EXTRA, jnp.where(low, turned, turn(other_rest, HEAD_DIM)))
            for index, place in ((one, column), (two, column + 1)):
                steps = steps + turn(tile(index, 5), core * (HEADS // 2) + place * heads)
                shared_b = [total + tile(index, k) for k, total in enumerate(shared_b)]
    for k, total in enumerate(shared_b):
        sums = sums + put(2 * INNER + k * EXTRA, total)
    at = INNER + CONV_CH
    steps = steps[:, :HEADS]
    grad_ref[:, at : at + HEADS] = steps
    rest = jnp.sum(steps * weight_ref[:, at : at + HEADS].astype(f32), axis=1, keepdims=True)
    sums_ref[...] = jnp.broadcast_to(jnp.sum(sums, axis=1, keepdims=True) + rest, (rows, EXTRA))
    per_tile = EXTRA // unit
    for replica in range(2):
        for start in range(0, groups, per_tile):
            for kind, out_ref in enumerate((gate_ref, up_ref)):
                begin = kind * 2 * unit + replica * unit
                mine = jnp.logical_and(lane >= begin, lane < begin + unit)
                total = jnp.zeros((rows, EXTRA), f32)
                for index in range(start, start + per_tile):
                    part = jnp.where(mine, tile(index, 6), 0.0)
                    total = total + turn(part, (index - start) * unit - begin)
                column = replica * groups * unit + start * unit
                out_ref[:, column : column + EXTRA] = total


def unpack(pack, weight, half, own, heads, unit, hidden_units):
    rows = weight.shape[0]
    shapes = [
        jax.ShapeDtypeStruct((rows, columns), f32)
        for columns in (weight.shape[1], hidden_units, hidden_units, EXTRA)
    ]
    return pl.pallas_call(
        lambda *refs: unpack_kernel(half, own, heads, unit, *refs),
        grid=(1,),
        in_specs=[whole(pack), whole(weight)],
        out_specs=[whole(shape) for shape in shapes],
        out_shape=shapes,
        compiler_params=params(),
        cost_estimate=cost(4),
        name="unpack",
    )(pack, weight)


def local(
    hidden_in,
    cotangent,
    routes,
    route_gates,
    lengths,
    in_proj,
    out_proj,
    conv_weight,
    conv_bias,
    norm_gain,
    mix_gain,
    ffn_gain,
    shared_gate,
    shared_up,
    shared_down,
    expert_gate,
    expert_up,
    expert_down,
    decay_log,
    step_bias,
    skip_gain,
):
    tokens, width = hidden_in.shape
    top = routes.shape[1]
    replicas = lax.axis_size("dp")
    groups = lax.axis_size("z") * 4
    devices = replicas * groups
    core = lax.axis_index("core")
    column = lax.axis_index("z") * 2 + lax.axis_index("y")
    place = column * 2 + core
    heads = HEADS // groups
    own = heads * HEAD_DIM
    half = groups // 2
    rows_in = in_proj.shape[0]
    hidden_units = shared_gate.shape[1]
    unit = hidden_units // devices
    units = hidden_units // groups
    local_experts = expert_gate.shape[0]
    capacity = 2 * tokens * top // (local_experts * groups)
    first_head = core * (HEADS // 2) + column * heads
    first_channel = first_head * HEAD_DIM

    small = (conv_weight.reshape(-1), conv_bias, norm_gain, mix_gain, ffn_gain)
    small_sizes = [entry.shape[0] for entry in small]
    small_lanes = -(-sum(small_sizes) // rows_in)
    small_flat = jnp.concatenate(small)
    small_flat = jnp.pad(small_flat, (0, small_lanes * rows_in - small_flat.shape[0]))

    bounds = jnp.cumsum(lengths[0])
    slot = jnp.arange(tokens, dtype=jnp.int32)
    runs = jnp.sum((slot[:, None] >= bounds[None, : SEQ_SLOTS - 1]).astype(jnp.int32), axis=1)
    live = (runs < SEQ_SLOTS - 1).astype(f32)[:, None]
    starts = jnp.concatenate([jnp.zeros((1,), jnp.int32), bounds[: SEQ_SLOTS - 1].astype(jnp.int32)])
    place_in_run = slot - jnp.sum(jnp.where(runs[:, None] == jnp.arange(SEQ_SLOTS), starts, 0), axis=1)
    beside = [runs.astype(bf16)[:, None], place_in_run.astype(bf16)[:, None], routes.astype(bf16)]
    beside = jnp.concatenate(beside + list(split_three(route_gates)), axis=1)
    beside = jnp.pad(beside, ((0, 0), (0, EXTRA - beside.shape[1])))
    spread = jnp.concatenate([in_proj[:, 2 * INNER :], small_flat.reshape(rows_in, small_lanes)], axis=1)
    spread = jnp.pad(spread, ((0, 0), (0, -spread.shape[1] % EXTRA)))
    spread = dp_gather_rows(spread[None], 0).reshape(replicas * rows_in, -1)
    spread = jnp.pad(spread, ((0, tokens - replicas * rows_in), (0, 0)))
    payload = jnp.concatenate([hidden_in, beside, spread], axis=1)

    def by_place(block):
        block = block.reshape(rows_in, 2, half, own).transpose(2, 1, 0, 3)
        return block.reshape(groups, rows_in, own)

    def by_unit(block):
        block = block.reshape(rows_in, replicas, groups, unit).transpose(2, 0, 1, 3)
        return block.reshape(groups, rows_in, units)

    pack = jnp.concatenate(
        [
            by_place(in_proj[:, :INNER]),
            by_place(in_proj[:, INNER : 2 * INNER]),
            by_unit(shared_gate),
            by_unit(shared_up),
        ],
        axis=2,
    )
    pack = lax.all_to_all(pack, GROUP, split_axis=0, concat_axis=0, tiled=True)

    if replicas == 2:
        both = swap(out_proj, "core")
        both = jnp.concatenate(
            [jnp.where(core == 0, out_proj, both), jnp.where(core == 0, both, out_proj)]
        )
        payload, both = tie(payload, both)
        w_out = jnp.where(lax.axis_index("dp") == core, both, swap(both, "dp"))
    else:
        w_out = lax.dynamic_slice_in_dim(
            lax.all_gather(out_proj, ALL, axis=0, tiled=True), first_channel, own, 0
        )
    def gather_tokens():
        size = lax.axis_size("z")
        block, blocks, pieces = payload, [], []
        arrived = None
        for step in range(size):
            following = ring(block) if step < size - 1 else ()
            near = swap(block, "y")
            if step == 0:
                work = (pack, w_out, w_shared_down)
            elif replicas == 2 and step < 4:
                extent = arrived.shape[0] // 3
                work = swap(after(arrived[(step - 1) * extent : step * extent], block), "dp")
            else:
                work = ()
            following, near, work = tie(following, near, work)
            if step == 0:
                arrived = work[0].reshape(groups * rows_in, -1)
                found = work[1:]
            elif replicas == 2 and step < 4:
                pieces.append(work)
            blocks += [block, near]
            block = following
        near = jnp.concatenate(blocks, axis=0)
        if replicas == 2:
            other = jnp.concatenate(pieces, axis=0)
            mine = lax.axis_index("dp") == 0
            everything = jnp.concatenate(
                [jnp.where(mine, arrived, other), jnp.where(mine, other, arrived)], axis=0
            )
        else:
            everything = lax.all_gather(arrived, "dp", axis=0, tiled=True)
        return near, swap(near, "core"), everything, found

    w_shared_down = dp_gather_rows(shared_down[None], 0).reshape(units, width)
    near, mate, pack, (w_out, w_shared_down) = gather_tokens()
    w_gate, w_up, w_down = (
        lax.all_gather(entry, "dp", axis=1, tiled=True)
        for entry in (expert_gate, expert_up, expert_down)
    )

    table = jnp.concatenate([near[:, width : width + EXTRA], mate[:, width : width + EXTRA]], axis=0)
    routes_all = table[:, 2 : 2 + top].astype(jnp.int32)
    gates_all = join_three([table[:, 2 + k * top : 2 + (k + 1) * top] for k in (1, 2, 3)])
    number = jnp.arange(groups, dtype=jnp.int32)
    back_z = (lax.axis_index("z") - number // 4) % (groups // 4)
    other_y = (number // 2) % 2 != lax.axis_index("y")
    other_core = number % 2 != core
    order = other_core * half + back_z * 2 + other_y

    def blocks_of(entry):
        return entry[:, width + EXTRA :].reshape(half, tokens, -1)[:, : replicas * rows_in]

    spread = jnp.concatenate([blocks_of(near), blocks_of(mate)], axis=0)[order]
    spread = spread.reshape(groups, replicas, rows_in, -1).transpose(1, 0, 2, 3)
    spread = spread.reshape(devices, rows_in, -1)
    small_at = 2 * STATE + HEADS
    small_all = spread[:, :, small_at : small_at + small_lanes].reshape(devices, -1)
    pieces = []
    start = 0
    for size in small_sizes:
        pieces.append(small_all[:, start : start + size].reshape(-1).astype(f32))
        start += size
    conv_w_all = pieces[0].reshape(CONV_CH, KERNEL).T
    conv_b_all, norm_gain_all, mix_gain_all, ffn_gain_all = pieces[1:]
    spread = spread.reshape(devices * rows_in, -1)
    w_step = lax.dynamic_slice_in_dim(spread, 2 * STATE + first_head, heads, 1)
    w_step = jnp.pad(w_step, ((0, 0), (0, EXTRA - heads)))
    w_in = [spread[:, : 2 * STATE], pack[:, own : 2 * own], pack[:, EXTRA:own], pack[:, :EXTRA], w_step]
    w_in = jnp.concatenate(w_in, axis=1)
    w_shared_gate = pack[:, 2 * own : 2 * own + units]
    w_shared_up = pack[:, 2 * own + units :]

    def own_channels(rows):
        return lax.dynamic_slice_in_dim(rows, first_channel, own, rows.ndim - 1)

    conv = jnp.concatenate([conv_w_all, conv_b_all[None]], axis=0)
    conv = jnp.concatenate([conv[:, INNER:], own_channels(conv)], axis=1)
    conv = jnp.pad(conv, ((0, 8 - conv.shape[0]), (0, CONV_LANES - conv.shape[1])))

    def own_heads(row):
        return lax.dynamic_slice_in_dim(row, first_head, heads, 0)

    def lanes_of(row):
        return jnp.pad(row, (0, WIDE - row.shape[0]))

    rate = -jnp.exp(own_heads(decay_log))
    head = [
        lanes_of(own_heads(step_bias)),
        lanes_of(rate),
        lanes_of(jnp.repeat(own_heads(skip_gain), HEAD_DIM)),
        lanes_of(own_channels(mix_gain_all)),
    ]
    head = jnp.pad(jnp.stack(head), ((0, 4), (0, 0)))
    rate_rows = jnp.broadcast_to(jnp.pad(rate, (0, 8 - heads))[:, None], (8, EXTRA))
    w_out = jnp.pad(w_out, ((0, WIDE - own), (0, 0)))

    input_rows = hidden_in.astype(f32)
    grad_out = cotangent.astype(f32)
    branch = after((grad_out * live).astype(bf16), near)

    pairs = groups // 2
    pair_tokens = 2 * tokens
    pair_slots = 2 * capacity
    numbers = place * local_experts + jnp.arange(local_experts, dtype=jnp.int32)
    named = routes_all[:, None, :] == numbers[None, :, None]
    member = jnp.any(named, axis=2).T.reshape(local_experts, pairs, pair_tokens)
    weight = jnp.sum(jnp.where(named, gates_all[:, None, :], 0.0), axis=2).T
    weight = weight.reshape(local_experts, pairs, pair_tokens)
    below = jnp.triu(jnp.ones((pair_tokens, pair_tokens), bf16))
    rank = matmul(member.astype(bf16), below)
    rank = jnp.where(member, rank.astype(jnp.int32) - 1, -1).transpose(1, 0, 2)
    rank = jnp.pad(rank, ((0, 0), (0, 8 - local_experts), (0, 0)), constant_values=-1)
    weight = jnp.pad(weight.transpose(1, 0, 2), ((0, 0), (0, 8 - local_experts), (0, 0)))
    half_pairs = pairs // 2

    def rows_out(values, first, shared, into=None):
        return dispatch(values, rank, weight, local_experts, pair_slots, first, shared, into)

    mixer = (norm_gain_all[None], w_in, w_out, conv, head)

    def forward(part):
        return lambda token: mixer_forward(after(part, token), width, tokens, *after(mixer, token))

    branch_near, branch_mate, ((mixer_set, w_gate), done_mate, done_near, _) = gather(
        branch, [(mixer, w_gate), forward(mate), forward(near)]
    )
    _, w_in, w_out, conv, head = mixer_set
    normed_mate, proj_mate, mixed_mate, scaled_mate = done_mate
    normed_near, proj_near, mixed_near, scaled_near = done_near
    pairs_sum = scatter_first(mixed_near, mixed_mate)
    mixed_sum, (_, _, w_up, *_) = scatter_last(pairs_sum, [(), (), w_up])
    mix_rms = lax.rsqrt(jnp.sum(mixed_sum[:, width:], axis=1, keepdims=True) / INNER + epsilon)
    mixer_out = mixed_sum[:, :width] * mix_rms
    resid = input_rows + live * mixer_out
    ffn_rms = lax.rsqrt(jnp.mean(resid * resid, axis=1, keepdims=True) + epsilon)
    ffn_hat = resid * ffn_rms

    def grads_near(token):
        return rows_out(after(branch_near, token), 0, (w_shared_down,))

    done_rows = []

    def grads_mate(token):
        return rows_out(after(branch_mate, token), half_pairs, (w_shared_down,), done_rows[0])

    def keep(work):
        def kept(token):
            found = work(token)
            done_rows.append(found[:2])
            return found

        return kept

    ffn_near, ffn_mate, ((_, _, act_grad_near), (d_row, slot_weight, act_grad_mate), *_) = gather(
        (ffn_hat * ffn_gain_all).astype(bf16), [keep(grads_near), grads_mate]
    )

    expert_in, shared_near, sg_near, su_near = rows_out(
        ffn_near, 0, (act_grad_near, w_shared_gate, w_shared_up)
    )
    expert_in, shared_mate, sg_mate, su_mate = rows_out(
        ffn_mate, half_pairs, (act_grad_mate, w_shared_gate, w_shared_up), (expert_in,)
    )
    act_low, g_low, u_low, d_in_row, expert_row = expert_pass(
        expert_in, d_row, slot_weight, w_gate, w_up, w_down
    )

    half_grad = (((1,), (1,)), ((0,), (0,)))
    grad_down = matmul(act_low, d_row, half_grad).astype(bf16)
    d_in_row, grad_down = tie(d_in_row, grad_down)

    def back_rows(sg, su, first):
        terms = ((sg, w_shared_gate), (su, w_shared_up))
        return combine(d_in_row, rank, terms, pair_slots, first, True)

    grad_ffn_mate = back_rows(sg_mate, su_mate, half_pairs)
    grad_ffn_near = back_rows(sg_near, su_near, 0)
    pairs_sum = scatter_first(grad_ffn_near, grad_ffn_mate)

    def leaving_of(part):
        return lambda token: matmul(after(expert_in, token), part, half_grad).astype(bf16)

    grad_ffn, leaving = scatter_last(pairs_sum, [leaving_of(g_low), leaving_of(u_low)])
    grad_down, grad_gate, grad_up = (
        lax.psum_scatter(entry, "dp", scatter_dimension=1, tiled=True)
        for entry in (grad_down, *leaving[:2])
    )

    grad_ffn_gain = jnp.sum(grad_ffn * ffn_hat, axis=0)
    scaled_ffn = grad_ffn * ffn_gain_all
    grad_resid = grad_out + ffn_rms * (
        scaled_ffn - ffn_hat * jnp.mean(scaled_ffn * ffn_hat, axis=1, keepdims=True)
    )
    d_mixer = (grad_resid * live).astype(bf16).astype(f32)
    inner_term = jnp.sum(d_mixer * mixer_out, axis=1, keepdims=True) * mix_rms * mix_rms / INNER
    inner_pack = jnp.pad(jnp.concatenate(split_three(inner_term), axis=1), ((0, 0), (0, EXTRA - 3)))
    d_mixer_pack = jnp.concatenate([(d_mixer * mix_rms).astype(bf16), inner_pack], axis=1)

    def out_rows(shared_act, first):
        def work(token):
            terms = ((shared_act, w_shared_down),)
            return combine(after(expert_row, token), rank, terms, pair_slots, first, False)

        return work

    turned = (((0,), (0,)), ((), ()))

    def of_halves(left, right):
        return matmul(left[0], right[0], turned) + matmul(left[1], right[1], turned)

    def shared_grads_of(token):
        halves = after(((branch_near, branch_mate), (ffn_near, ffn_mate)), token)
        return (
            of_halves((shared_near, shared_mate), halves[0]),
            of_halves(halves[1], (sg_near, sg_mate)),
            of_halves(halves[1], (su_near, su_mate)),
        )

    d_mixer_near, d_mixer_mate, (out_mate, out_near, shared_grads, grad_down) = gather(
        d_mixer_pack,
        [
            out_rows(shared_mate, half_pairs),
            out_rows(shared_near, 0),
            shared_grads_of,
            lambda token: after(grad_down, token).astype(f32),
        ],
    )
    grad_shared_down, grad_shared_g, grad_shared_u = shared_grads
    grad_shared_gu = jnp.concatenate([grad_shared_g, grad_shared_u], axis=1)
    grad_out_rows = of_halves(
        (scaled_near, scaled_mate), (d_mixer_near[:, :width], d_mixer_mate[:, :width])
    )[:own]
    out_rows_low = grad_out_rows.astype(bf16)
    out_pairs = scatter_first(out_near, out_mate)
    (d_mixer_near, d_mixer_mate), out_pairs, out_rows_low = tie(
        (d_mixer_near, d_mixer_mate), out_pairs, out_rows_low
    )

    def backward(grads, part, proj, first, into=()):
        return mixer_backward(
            grads, part, proj, width, tokens, w_in, w_out, conv, head, rate_rows, first, into
        )

    def towards(step):
        return swap(out_pairs[step][1], "y")

    def window(work, *others):
        return tie(work, *others)

    part_one = backward(d_mixer_mate, mate, proj_mate, 0)
    out_there = {1: towards(1), 2: towards(2)}
    part_one, out_there, out_pairs, d_mixer_mate = window(part_one, out_there, out_pairs, d_mixer_mate)
    done_mate = backward(d_mixer_mate, mate, proj_mate, 1, part_one[:2])
    out_total = ring_step(add_low(out_pairs[1][0], out_there[1]), out_pairs, out_there, 1)
    out_there[3] = towards(3)
    done_mate, out_total, out_there, out_pairs, d_mixer_near = window(
        done_mate, out_total, out_there, out_pairs, d_mixer_near
    )
    part_two = backward(d_mixer_near, near, proj_near, 0)
    moved = swap(done_mate[0], "core")
    out_total = ring_step(out_total, out_pairs, out_there, 2)
    out_there[0] = towards(0)
    part_two, moved, out_total, out_there, out_pairs, d_mixer_near = window(
        part_two, moved, out_total, out_there, out_pairs, d_mixer_near
    )
    out_rows_there = swap(after(out_rows_low, part_two[0]), "dp") if replicas == 2 else ()
    done_near = backward(d_mixer_near, near, proj_near, 1, part_two[:2])
    branch_sum = ring_step(out_total, out_pairs, out_there, 3)
    done_near, branch_sum = window(done_near, branch_sum)
    grad_shared_gu = dp_scatter_rows(grad_shared_gu, 0, done_near[0])
    grad_shared_down = dp_scatter_rows(grad_shared_down.reshape(replicas, unit, width), 0, done_near[0])[0]
    normed_grad_mate, proj_low_mate = done_mate[:2]
    normed_grad_near, proj_low_near = done_near[:2]
    conv_parts = [part_one[2], done_mate[2], part_two[2], done_near[2]]
    head_parts = [part_one[3], done_mate[3], part_two[3], done_near[3]]
    pairs_sum = scatter_first(normed_grad_near, normed_grad_mate, moved)

    def to_owner(part):
        rows_part = jnp.zeros((part.shape[0], CONV_CH), f32)
        values = part[:, 2 * STATE : 2 * STATE + own]
        rows_part = lax.dynamic_update_slice_in_dim(rows_part, values, first_channel, 1)
        rows_part = lax.dynamic_update_slice_in_dim(rows_part, part[:, : 2 * STATE], INNER, 1)
        return rows_part.reshape(part.shape[0], devices, -1).transpose(1, 0, 2).reshape(devices, -1)

    def head_row(part):
        return lax.dynamic_update_slice_in_dim(jnp.zeros((HEADS,), f32), part, first_head, 0)

    def small_sums(conv_grads, head_grads):
        head_grads = jnp.sum(head_grads.reshape(3, 8, EXTRA)[:, :heads], axis=2)
        head_rows = [head_row(entry) for entry in (head_grads[0] * rate, *head_grads[1:])]
        return jnp.concatenate(
            [
                to_owner(conv_grads[: KERNEL + 1]),
                grad_ffn_gain.reshape(devices, -1),
                jnp.broadcast_to(jnp.concatenate(head_rows)[None], (devices, 3 * HEADS)),
            ],
            axis=1,
        )

    crossing = replicas == 2
    here = lax.axis_index("dp")
    normed_rows = width // 2 if crossing else width

    def input_grad(where, token):
        parts = after((normed_near, normed_mate), token)
        if crossing:
            parts = [lax.dynamic_slice_in_dim(part, where * normed_rows, normed_rows, 1) for part in parts]
        return of_halves(parts, (proj_low_near, proj_low_mate))

    def piece(array, index, token):
        extent = array.shape[0] // 3
        return swap(after(array[index * extent : (index + 1) * extent], token), "dp")

    pieces = []

    def small_work(token):
        parts = after((conv_parts, head_parts), token)
        return small_sums(sum(parts[0]), sum(parts[1]))

    there = scatter_beside(pairs_sum)
    total = add_low(pairs_sum[1][0], there[1])
    total, leaving, out_rows_there = tie(
        total, input_grad(1 - here, pairs_sum).astype(bf16), out_rows_there
    )
    finished = []
    for index, work in enumerate((lambda token: input_grad(here, token), small_work, lambda token: ())):
        following = ring_step(total, pairs_sum, there, index + 1)
        across = piece(leaving, index, total) if crossing else ()
        total, across, result = tie(following, across, work(total))
        pieces.append(across)
        finished.append(result)
    grad_w_in, sums, _ = finished
    grad_normed = total
    output = (resid + live * branch_sum).astype(bf16)

    if crossing:
        grad_w_in = grad_w_in + jnp.concatenate(pieces, axis=0).astype(f32)
    else:
        grad_w_in = lax.psum_scatter(leaving, "dp", scatter_dimension=0, tiled=True)
    grad_pack = jnp.concatenate([grad_w_in.astype(bf16), grad_shared_gu.astype(bf16)], axis=1)
    grad_pack = grad_pack.reshape(groups, rows_in, -1)
    grad_gate, grad_up = (entry.astype(f32) for entry in after((grad_gate, grad_up), grad_pack))
    grad_pack = lax.all_to_all(grad_pack, GROUP, split_axis=0, concat_axis=0, tiled=True)

    def from_place(block):
        block = block.reshape(half, 2, rows_in, block.shape[2]).transpose(2, 1, 0, 3)
        return block.reshape(rows_in, -1)

    def from_unit(block):
        block = block.reshape(groups, rows_in, replicas, unit).transpose(1, 2, 0, 3)
        return block.reshape(rows_in, hidden_units)

    if replicas == 2:
        grad_in_proj, grad_shared_gate, grad_shared_up, gain_sums = unpack(
            grad_pack, in_proj, half, own, heads, unit, hidden_units
        )
        gain_sums = gain_sums[:, 0]
    else:
        grad_pack = grad_pack.astype(f32)
        value_at, gate_at, step_at = 2 * STATE, CONV_LANES, CONV_LANES + EXTRA
        gate_part = [grad_pack[:, :, gate_at : gate_at + EXTRA], grad_pack[:, :, value_at + own : gate_at]]
        grad_in_proj = jnp.concatenate(
            [
                from_place(jnp.concatenate(gate_part, axis=2)),
                from_place(grad_pack[:, :, value_at : value_at + own]),
                jnp.sum(grad_pack[:, :, : 2 * STATE], axis=0),
                from_place(grad_pack[:, :, step_at : step_at + heads]),
            ],
            axis=1,
        )
        grad_shared_gate = from_unit(grad_pack[:, :, PROJ_LANES : PROJ_LANES + units])
        grad_shared_up = from_unit(grad_pack[:, :, PROJ_LANES + units :])
        gain_sums = jnp.sum(grad_in_proj * in_proj.astype(f32), axis=1)
    if replicas == 2:
        mine = lax.axis_index("dp") == core
        total = (grad_out_rows + out_rows_there.astype(f32)).reshape(2, own // 2, width)
        passed = swap(lax.dynamic_index_in_dim(total, 1 - core, 0, keepdims=False), "core")
        grad_out_proj = jnp.where(mine, lax.dynamic_index_in_dim(total, core, 0, keepdims=False), passed)
    else:
        full = jnp.zeros((INNER, width), f32)
        full = lax.dynamic_update_slice_in_dim(full, grad_out_rows, first_channel, 0)
        grad_out_proj = lax.psum_scatter(full, ALL, scatter_dimension=0, tiled=True)
    grad_mix_gain = jnp.sum(grad_out_proj * out_proj.astype(f32), axis=1) / mix_gain.astype(f32)
    grad_norm_gain = gain_sums / norm_gain.astype(f32)

    sums = lax.all_to_all(sums, ALL, split_axis=0, concat_axis=0, tiled=True)
    sums = jnp.sum(sums, axis=0)
    channels = CONV_CH // devices
    grad_conv_weight = sums[: KERNEL * channels].reshape(KERNEL, channels).T
    grad_conv_bias = sums[KERNEL * channels : (KERNEL + 1) * channels]
    at = (KERNEL + 1) * channels
    grad_ffn_gain = sums[at : at + rows_in]
    at += rows_in
    grad_decay, grad_stepb, grad_skip = (sums[at + k * HEADS : at + (k + 1) * HEADS] for k in range(3))

    in_rms = lax.rsqrt(jnp.mean(input_rows * input_rows, axis=1, keepdims=True) + epsilon)
    in_hat = input_rows * in_rms
    scaled_in = grad_normed * norm_gain_all
    grad_input = grad_resid + in_rms * (
        scaled_in - in_hat * jnp.mean(scaled_in * in_hat, axis=1, keepdims=True)
    )
    return (
        output,
        grad_input,
        grad_in_proj,
        grad_out_proj,
        grad_conv_weight,
        grad_conv_bias,
        grad_norm_gain,
        grad_mix_gain,
        grad_ffn_gain,
        grad_shared_gate,
        grad_shared_up,
        grad_shared_down,
        grad_gate,
        grad_up,
        grad_down,
        grad_decay,
        grad_stepb,
        grad_skip,
    )


def solution(mesh):
    replicas, groups = mesh.shape["dp"], mesh.shape["expert"]
    inner = Mesh(mesh.devices.reshape(replicas, groups // 4, 2, 2), ALL)
    flat = P(ALL)
    expert = P(GROUP, "dp", None)
    return jax.shard_map(
        local,
        mesh=inner,
        in_specs=(flat,) * 15 + (expert,) * 3 + (P(),) * 3,
        out_specs=(flat,) * 12 + (expert,) * 3 + (P(),) * 3,
        check_vma=False,
    )
```

```python
import jax
import jax.numpy as jnp
from jax import lax
from jax.experimental import pallas as pl
from jax.experimental.pallas import tpu as pltpu
from jax.sharding import Mesh, PartitionSpec as P

HEADS = 48
HEAD_DIM = 64
STATE = 128
KERNEL = 4
SEQ_SLOTS = 3
INNER = 3072
CONV_CH = 3328
EXTRA = 128

epsilon = 1e-05
bf16 = jnp.bfloat16
f32 = jnp.float32
GROUP = ("z", "y", "core")
ALL = ("dp", "z", "y", "core")


def matmul(left, right, dims=None, precision=None):
    if dims is None:
        dims = (((left.ndim - 1,), (0,)), ((), ()))
    return lax.dot_general(left, right, dims, precision=precision, preferred_element_type=f32)


def swap(value, axis):
    return lax.ppermute(value, axis, [(0, 1), (1, 0)])


def ring(value):
    size = lax.axis_size("z")
    return lax.ppermute(value, "z", [(k, (k + 1) % size) for k in range(size)])


def after(value, *earlier):
    return lax.optimization_barrier((value, earlier))[0]


def split_three(value):
    high = lax.reduce_precision(value, 8, 7)
    rest = value - high
    middle = lax.reduce_precision(rest, 8, 7)
    return high.astype(bf16), middle.astype(bf16), (rest - middle).astype(bf16)


def join_three(parts):
    return parts[0].astype(f32) + parts[1].astype(f32) + parts[2].astype(f32)


def tie(value, *others):
    return lax.optimization_barrier((value, *others))


def work_of(entry, token):
    return entry(token) if callable(entry) else entry


def gather(block, beside_work=()):
    size = lax.axis_size("z")
    beside_work = (list(beside_work) + [()] * size)[:size]
    blocks = []
    for step in range(size):
        following = ring(block) if step < size - 1 else ()
        near = swap(block, "y")
        work = work_of(beside_work[step], block)
        following, near, beside_work[step] = tie(following, near, work)
        blocks += [block, near]
        block = following
    own = jnp.concatenate(blocks, axis=0)
    return own, swap(own, "core"), beside_work


def to_channels(value):
    return lax.ppermute(value, ("dp", "core"), [(0, 2), (3, 1)])


def from_channels(value):
    return lax.ppermute(value, ("dp", "core"), [(2, 0), (1, 3)])


def add_low(left, right):
    return (left.astype(f32) + right.astype(f32)).astype(bf16)


def scatter_first(near, mate, moved=None):
    size = lax.axis_size("z")
    shape = (size, 2, near.shape[0] // (2 * size), near.shape[1])
    there = (swap(mate, "core") if moved is None else moved).reshape(shape)
    near = near.reshape(shape)
    pairs = [add_low(near[step], there[step]) for step in range(size)]
    return pairs


def scatter_beside(pairs):
    size = len(pairs)
    order = list(range(1, size)) + [0]
    there = {step: swap(pairs[step][1], "y") for step in order}
    return [there[step] for step in range(size)]


def ring_step(total, pairs, there, step):
    at = (step + 1) % len(pairs)
    total = ring(total).astype(f32) + (pairs[at][0].astype(f32) + there[at].astype(f32))
    return total.astype(bf16) if at else total


def scatter_last(pairs, beside_work=(), there=None):
    size = len(pairs)
    beside_work = (list(beside_work) + [()] * size)[:size]
    there = there or scatter_beside(pairs)
    total = add_low(pairs[1][0], there[1])
    token = pairs
    for step in range(1, size):
        total, beside_work[step - 1] = tie(total, work_of(beside_work[step - 1], token))
        token = total
        total = ring_step(total, pairs, there, step)
    total, beside_work[-1] = tie(total, work_of(beside_work[-1], token))
    return total, beside_work


def dp_gather_rows(value, axis):
    if lax.axis_size("dp") != 2:
        return lax.all_gather(value, "dp", axis=axis, tiled=True)
    other = swap(value, "dp")
    first = lax.axis_index("dp") == 0
    return jnp.concatenate(
        [jnp.where(first, value, other), jnp.where(first, other, value)], axis=axis
    )


def dp_scatter_rows(value, axis, hold=()):
    count = lax.axis_size("dp")
    if count != 2:
        return lax.psum_scatter(value.astype(bf16), "dp", scatter_dimension=axis, tiled=True).astype(f32)
    place = lax.axis_index("dp")
    extent = value.shape[axis] // count
    sent = lax.dynamic_slice_in_dim(value, (1 - place) * extent, extent, axis).astype(bf16)
    kept = lax.dynamic_slice_in_dim(value, place * extent, extent, axis)
    received, kept, hold = tie(swap(sent, "dp"), kept, hold)
    return kept + received.astype(f32)


def params(steps=1):
    return pltpu.CompilerParams(
        dimension_semantics=("arbitrary",) * steps, vmem_limit_bytes=56 * 1024 * 1024
    )


def cost(micros):
    return pl.CostEstimate(
        flops=int(micros * 1.1e9), bytes_accessed=int(micros * 3.5e6), transcendentals=0
    )


def whole(array):
    return pl.BlockSpec(array.shape, lambda step: (0,) * array.ndim)


def sigmoid(value):
    return 1.0 / (1.0 + jnp.exp(-value))


def halves_of(value):
    high = value.astype(bf16)
    return high, (value - high.astype(f32)).astype(bf16)


def exact(left, right, dims):
    (left_high, left_low), (right_high, right_low) = halves_of(left), halves_of(right)

    def dot(one, other):
        return lax.dot_general(one, other, (dims, ((), ())), preferred_element_type=f32)

    return dot(left_high, right_high) + (dot(left_high, right_low) + dot(left_low, right_high))


def rows_of(array, index):
    return array[index : index + 1]


WIDE = 256
CONV_LANES = 2 * STATE + WIDE
PROJ_LANES = CONV_LANES + 2 * EXTRA


def triangle(count):
    row = lax.broadcasted_iota(jnp.int32, (count, count), 0)
    column = lax.broadcasted_iota(jnp.int32, (count, count), 1)
    return row - column


def block_scan(proj, place, conv, head):
    heads = HEADS // 16
    count = proj.shape[0]
    taps = [proj[:, :CONV_LANES]]
    total = rows_of(conv, KERNEL) + rows_of(conv, KERNEL - 1) * taps[0]
    for offset in range(1, KERNEL):
        inside = (place >= offset).astype(f32)
        taps.append(pltpu.roll(taps[0], offset, 0) * inside)
        total = total + rows_of(conv, KERNEL - 1 - offset) * taps[offset]
    conv_sig = sigmoid(total)
    conv_out = total * conv_sig
    b_part, c_part = conv_out[:, :STATE], conv_out[:, STATE : 2 * STATE]
    raw = proj[:, CONV_LANES + EXTRA :] + rows_of(head, 0)[:, :EXTRA]
    step = jnp.maximum(raw, 0.0) + jnp.log1p(jnp.exp(-jnp.abs(raw)))
    distance = triangle(count)
    lower = (distance >= 0).astype(f32)
    cumul = exact(lower, step * rows_of(head, 1)[:, :EXTRA], ((1,), (0,)))
    cumul_rows = cumul.T
    step_rows = step.T
    scores = exact(c_part, b_part, ((1,), (1,)))
    reach = jnp.logical_and(distance >= 0, distance.astype(f32) <= place)
    lane = lax.broadcasted_iota(jnp.int32, (1, 2 * HEAD_DIM), 1)
    decays, values, scan = [], [], [None] * (WIDE // EXTRA)
    for index in range(heads):
        tile = index // 2
        spread = cumul[:, index : index + 1] - rows_of(cumul_rows, index)
        decay = jnp.exp(jnp.where(reach, spread, -1e30))
        mine = (lane // HEAD_DIM == index % 2).astype(f32)
        at = 2 * STATE + tile * EXTRA
        value = conv_out[:, at : at + EXTRA] * mine
        mixing = decay * scores * rows_of(step_rows, index)
        part = exact(mixing, value, ((1,), (0,)))
        scan[tile] = part if scan[tile] is None else scan[tile] + part
        decays.append((decay, mixing))
        values.append((value, mine))
    scan = jnp.concatenate(scan, axis=1) + rows_of(head, 2) * conv_out[:, 2 * STATE :]
    turned = pltpu.roll(proj[:, CONV_LANES - EXTRA : CONV_LANES], HEAD_DIM, 1)
    turned = jnp.where(lane < HEAD_DIM, turned, 0.0)
    gate = jnp.concatenate([proj[:, CONV_LANES : CONV_LANES + EXTRA], turned], axis=1)
    gate_sig = sigmoid(gate)
    gated = scan * (gate * gate_sig)
    return dict(
        taps=taps, total=total, conv_sig=conv_sig, conv_out=conv_out, raw=raw, step_rows=step_rows,
        scores=scores, decays=decays, values=values, scan=scan, gate=gate, gate_sig=gate_sig,
        gated=gated, lower=lower,
    )


def mixer_forward_kernel(
    count, tokens_ref, beside_ref, gain_ref, w_in_ref, w_out_ref, conv_ref, head_ref,
    normed_ref, proj_ref, part_ref, scaled_ref,
):
    rows = tokens_ref[...].astype(f32)
    normed = rows * lax.rsqrt(jnp.mean(rows * rows, axis=1, keepdims=True) + epsilon) * gain_ref[...]
    normed = normed.astype(bf16)
    normed_ref[...] = normed
    proj_ref[...] = jnp.dot(normed, w_in_ref[...], preferred_element_type=f32)
    conv, head = conv_ref[...], head_ref[...]
    width = tokens_ref.shape[1]
    for index in range(tokens_ref.shape[0] // count):
        part = pl.ds(index * count, count)
        place = beside_ref[part, :].astype(f32)[:, 1:2]
        found = block_scan(proj_ref[part, :], place, conv, head)
        gated = found["gated"]
        scaled_ref[part, :] = (gated * rows_of(head, 3)).astype(bf16)
        square = gated * gated
        square = square[:, :EXTRA] + square[:, EXTRA:]
        part_ref[part, width:] = square.astype(bf16)
    part_ref[:, :width] = jnp.dot(
        scaled_ref[...], w_out_ref[...], preferred_element_type=f32
    ).astype(bf16)


def mixer_forward(gathered, width, count, gain, w_in, w_out, conv, head):
    total = gathered.shape[0]
    rows = 4 * count
    lanes = width // EXTRA

    def rows_spec(extent, column=0):
        return pl.BlockSpec((rows, extent), lambda step: (step, column))

    return pl.pallas_call(
        lambda *refs: mixer_forward_kernel(count, *refs),
        grid=(total // rows,),
        in_specs=[rows_spec(width), rows_spec(EXTRA, lanes)]
        + [whole(entry) for entry in (gain, w_in, w_out, conv, head)],
        out_specs=[rows_spec(width), rows_spec(PROJ_LANES), rows_spec(width + EXTRA), rows_spec(WIDE)],
        out_shape=[
            jax.ShapeDtypeStruct((total, width), bf16),
            jax.ShapeDtypeStruct((total, PROJ_LANES), f32),
            jax.ShapeDtypeStruct((total, width + EXTRA), bf16),
            jax.ShapeDtypeStruct((total, WIDE), bf16),
        ],
        compiler_params=params(),
        cost_estimate=cost(total / 80),
        name="mixer_forward",
    )(gathered, gathered, gain, w_in, w_out, conv, head)


def mixer_backward_kernel(
    count, grad_ref, inner_ref, beside_ref, proj_ref, w_in_ref, w_out_ref, conv_ref, head_ref, rate_ref,
    *refs,
):
    normed_ref, proj_grad_ref, conv_grad_ref, head_grad_ref = refs[-4:]
    heads = HEADS // 16
    conv, head = conv_ref[...], head_ref[...]

    @pl.when(pl.program_id(0) == 0)
    def _():
        conv_grad_ref[...] = jnp.zeros_like(conv_grad_ref)
        head_grad_ref[...] = jnp.zeros_like(head_grad_ref)

    grad_mixed = lax.dot_general(
        grad_ref[...], w_out_ref[...], (((1,), (1,)), ((), ())), preferred_element_type=f32
    )
    lane = lax.broadcasted_iota(jnp.int32, (1, EXTRA), 1)
    for index in range(grad_ref.shape[0] // count):
        part = pl.ds(index * count, count)
        place = beside_ref[part, :].astype(f32)[:, 1:2]
        found = block_scan(proj_ref[part, :], place, conv, head)
        inner = inner_ref[part, :].astype(f32)
        inner = inner[:, 0:1] + inner[:, 1:2] + inner[:, 2:3]
        gate, gate_sig, scan = found["gate"], found["gate_sig"], found["scan"]
        d_gated = grad_mixed[index * count : (index + 1) * count] * rows_of(head, 3) - found["gated"] * inner
        d_scan = d_gated * (gate * gate_sig)
        d_gate = d_gated * scan * (gate_sig * (1.0 + gate * (1.0 - gate_sig)))
        conv_out = found["conv_out"]
        d_values = [None] * (WIDE // EXTRA)
        d_scores = jnp.zeros((count, count), f32)
        column_sums = jnp.zeros((count, EXTRA), f32)
        direct, taken = [], []
        for number in range(heads):
            tile = number // 2
            decay, mixing = found["decays"][number]
            value, mine = found["values"][number]
            d_part = d_scan[:, tile * EXTRA : (tile + 1) * EXTRA]
            back = exact(mixing, d_part, ((0,), (0,))) * mine
            d_values[tile] = back if d_values[tile] is None else d_values[tile] + back
            d_mixing = exact(d_part, value, ((1,), (1,)))
            d_decayed = d_mixing * decay
            d_scores = d_scores + d_decayed * rows_of(found["step_rows"], number)
            d_spread = d_mixing * mixing
            direct.append(jnp.sum(d_decayed * found["scores"], axis=0, keepdims=True))
            taken.append(jnp.sum(d_spread, axis=0, keepdims=True))
            sums = jnp.sum(d_spread, axis=1, keepdims=True)
            column_sums = column_sums + jnp.where(lane == number, sums, 0.0)
            head_grad_ref[16 + number : 17 + number, :] += jnp.sum(d_part * value, axis=0, keepdims=True)
        d_values = jnp.concatenate(d_values, axis=1) + rows_of(head, 2) * d_scan
        empty = jnp.zeros((8 - heads, count), f32)
        d_cumul = column_sums.T[:8] - jnp.concatenate(taken + [empty], axis=0)
        d_rated = exact(d_cumul, found["lower"], ((1,), (0,)))
        step_rows = found["step_rows"][:8]
        d_step = jnp.concatenate(direct + [empty], axis=0) + d_rated * rate_ref[...]
        d_raw = d_step * sigmoid(found["raw"]).T[:8]
        head_grad_ref[0:8, :] += d_rated * step_rows
        head_grad_ref[8:16, :] += d_raw
        d_raw = jnp.concatenate([d_raw, jnp.zeros((EXTRA - 8, count), f32)], axis=0).T
        d_b = exact(d_scores, conv_out[:, STATE : 2 * STATE], ((0,), (0,)))
        d_c = exact(d_scores, conv_out[:, :STATE], ((1,), (0,)))
        d_out = jnp.concatenate([d_b, d_c, d_values], axis=1)
        conv_sig = found["conv_sig"]
        d_total = d_out * (conv_sig * (1.0 + found["total"] * (1.0 - conv_sig)))
        conv_grad_ref[KERNEL : KERNEL + 1, :] += jnp.sum(d_total, axis=0, keepdims=True)
        d_conv = rows_of(conv, KERNEL - 1) * d_total
        for offset in range(KERNEL):
            row = KERNEL - 1 - offset
            conv_grad_ref[row : row + 1, :] += jnp.sum(d_total * found["taps"][offset], axis=0, keepdims=True)
            if offset:
                kept = d_total * (place >= offset).astype(f32)
                d_conv = d_conv + rows_of(conv, row) * pltpu.roll(kept, count - offset, 0)
        shared_tile = d_conv[:, CONV_LANES - EXTRA :] + pltpu.roll(d_gate[:, EXTRA:], HEAD_DIM, 1)
        d_proj = [d_conv[:, : CONV_LANES - EXTRA], shared_tile, d_gate[:, :EXTRA], d_raw]
        proj_grad_ref[part, :] = jnp.concatenate(d_proj, axis=1).astype(bf16)
    normed_ref[...] = lax.dot_general(
        proj_grad_ref[...], w_in_ref[...], (((1,), (1,)), ((), ())), preferred_element_type=f32
    ).astype(bf16)


def mixer_backward(grads, gathered, proj, width, count, w_in, w_out, conv, head, rate, first, into=()):
    total = grads.shape[0]
    rows = 4 * count
    lanes = width // EXTRA

    def rows_spec(extent, column=0):
        return pl.BlockSpec((rows, extent), lambda step: (first + step, column))

    conv_shape = jax.ShapeDtypeStruct(conv.shape, f32)
    head_shape = jax.ShapeDtypeStruct((24, EXTRA), f32)
    in_specs = [rows_spec(width), rows_spec(EXTRA, lanes), rows_spec(EXTRA, lanes), rows_spec(PROJ_LANES)]
    in_specs += [whole(entry) for entry in (w_in, w_out, conv, head, rate)]
    aliases = {len(in_specs) + index: index for index in range(len(into))}
    in_specs += [pl.BlockSpec(memory_space=pl.ANY)] * len(into)
    return pl.pallas_call(
        lambda *refs: mixer_backward_kernel(count, *refs),
        grid=(1,),
        in_specs=in_specs,
        out_specs=[rows_spec(width), rows_spec(PROJ_LANES), whole(conv_shape), whole(head_shape)],
        out_shape=[
            jax.ShapeDtypeStruct((total, width), bf16),
            jax.ShapeDtypeStruct((total, PROJ_LANES), bf16),
            conv_shape,
            head_shape,
        ],
        input_output_aliases=aliases,
        compiler_params=params(),
        cost_estimate=cost(10),
        name="mixer_backward",
    )(grads, grads, gathered, proj, w_in, w_out, conv, head, rate, *into)


def selection(rank_ref, experts, slots):
    number = lax.broadcasted_iota(jnp.int32, (slots, rank_ref.shape[2]), 0)
    return [rank_ref[0, k : k + 1, :] == number for k in range(experts)]


def dispatch_kernel(experts, slots, grads, rank_ref, weight_ref, values_ref, *refs):
    chosen = selection(rank_ref, experts, slots)
    select = jnp.concatenate([entry.astype(f32) for entry in chosen], axis=0).astype(bf16)
    values = values_ref[...]
    rows = jnp.dot(select, values, preferred_element_type=f32)
    if grads:
        down_ref = refs[0]
        out_ref, weights_ref, act_grad_ref = refs[-3:]
        act_grad_ref[...] = lax.dot_general(
            values, down_ref[...], (((1,), (1,)), ((), ())), preferred_element_type=f32
        )
    else:
        act_grad_ref, gate_ref, up_ref = refs[:3]
        out_ref, act_ref, g_ref, u_ref = refs[-4:]
        gate = jnp.dot(values, gate_ref[...], preferred_element_type=f32)
        up = jnp.dot(values, up_ref[...], preferred_element_type=f32)
        sig = sigmoid(gate)
        silu = gate * sig
        d_act = act_grad_ref[...]
        act_ref[...] = (silu * up).astype(bf16)
        g_ref[...] = (d_act * up * (sig * (1.0 + gate * (1.0 - sig)))).astype(bf16)
        u_ref[...] = (d_act * silu).astype(bf16)
    for k in range(experts):
        part = rows[k * slots : (k + 1) * slots]
        if grads:
            own = jnp.where(chosen[k], weight_ref[0, k : k + 1, :], 0.0)
            own = jnp.sum(own, axis=1, keepdims=True)
            part = part * own
            weights_ref[k] = jnp.broadcast_to(own, (slots, EXTRA))
        out_ref[k] = part.astype(bf16)


def dispatch(values, rank, weight, experts, slots, first, shared, into=None):
    pairs, _, tokens = rank.shape
    count = values.shape[0] // tokens
    width = values.shape[1]
    grads = len(shared) == 1
    hidden = shared[0].shape[0] if grads else shared[0].shape[1]

    def slots_spec(extent):
        return pl.BlockSpec((experts, slots, extent), lambda step: (0, first + step, 0))

    def rows_spec(extent):
        return pl.BlockSpec((tokens, extent), lambda step: (step, 0))

    rank_spec = pl.BlockSpec((1,) + rank.shape[1:], lambda step: (first + step, 0, 0))
    in_specs = [rank_spec, rank_spec, rows_spec(width)]
    out_specs = [slots_spec(width)]
    shapes = [jax.ShapeDtypeStruct((experts, pairs * slots, width), bf16)]
    small = (values.shape[0], hidden)
    if grads:
        in_specs += [whole(shared[0])]
        out_specs += [slots_spec(EXTRA), rows_spec(hidden)]
        shapes += [
            jax.ShapeDtypeStruct((experts, pairs * slots, EXTRA), f32),
            jax.ShapeDtypeStruct(small, f32),
        ]
    else:
        in_specs += [rows_spec(hidden), whole(shared[1]), whole(shared[2])]
        out_specs += [rows_spec(hidden)] * 3
        shapes += [jax.ShapeDtypeStruct(small, bf16)] * 3
    aliases = {}
    into = () if into is None else tuple(into)
    for index, entry in enumerate(into):
        aliases[len(in_specs)] = index
        in_specs.append(pl.BlockSpec(memory_space=pl.ANY))
    return pl.pallas_call(
        lambda *refs: dispatch_kernel(experts, slots, grads, *refs),
        grid=(count,),
        in_specs=in_specs,
        out_specs=out_specs,
        out_shape=shapes,
        input_output_aliases=aliases,
        compiler_params=params(),
        cost_estimate=cost(5),
        name="dispatch",
    )(rank, weight, values, *shared, *into)


def combine_kernel(experts, slots, terms, turned, rank_ref, rows_ref, *refs):
    out_ref = refs[-1]
    chosen = selection(rank_ref, experts, slots)
    select = jnp.concatenate([entry.astype(f32) for entry in chosen], axis=0).astype(bf16)
    rows = jnp.concatenate([rows_ref[k] for k in range(experts)], axis=0)
    total = lax.dot_general(select, rows, (((0,), (0,)), ((), ())), preferred_element_type=f32)
    dims = ((1,), (1,)) if turned else ((1,), (0,))
    for k in range(terms):
        total = total + lax.dot_general(
            refs[2 * k][...], refs[2 * k + 1][...], (dims, ((), ())), preferred_element_type=f32
        )
    out_ref[...] = total.astype(bf16)


def combine(rows, rank, terms, slots, first, turned):
    pairs, _, tokens = rank.shape
    experts, _, width = rows.shape
    count = terms[0][0].shape[0] // tokens
    specs, operands = [], []
    for left, right in terms:
        specs += [pl.BlockSpec((tokens, left.shape[1]), lambda step: (step, 0)), whole(right)]
        operands += [left, right]
    return pl.pallas_call(
        lambda *refs: combine_kernel(experts, slots, len(terms), turned, *refs),
        grid=(count,),
        in_specs=[
            pl.BlockSpec((1,) + rank.shape[1:], lambda step: (first + step, 0, 0)),
            pl.BlockSpec((experts, slots, width), lambda step: (0, first + step, 0)),
        ]
        + specs,
        out_specs=pl.BlockSpec((tokens, width), lambda step: (step, 0)),
        out_shape=jax.ShapeDtypeStruct((count * tokens, width), bf16),
        compiler_params=params(),
        cost_estimate=cost(5),
        name="combine",
    )(rank, rows, *operands)


def expert_kernel(
    rows_ref, grad_ref, weight_ref, gate_ref, up_ref, down_ref, act_ref, g_ref, u_ref, back_ref, out_ref
):
    rows, gate_w, up_w, down_w = rows_ref[0], gate_ref[0], up_ref[0], down_ref[0]
    turned = (((1,), (1,)), ((), ()))
    gate = jnp.dot(rows, gate_w, preferred_element_type=f32)
    up = jnp.dot(rows, up_w, preferred_element_type=f32)
    sig = sigmoid(gate)
    silu = gate * sig
    act = (silu * up).astype(bf16)
    d_act = lax.dot_general(grad_ref[0], down_w, turned, preferred_element_type=f32)
    d_gate = (d_act * up * (sig * (1.0 + gate * (1.0 - sig)))).astype(bf16)
    d_up = (d_act * silu).astype(bf16)
    act_ref[0], g_ref[0], u_ref[0] = act, d_gate, d_up
    back = lax.dot_general(d_gate, gate_w, turned, preferred_element_type=f32)
    back = back + lax.dot_general(d_up, up_w, turned, preferred_element_type=f32)
    back_ref[0] = back.astype(bf16)
    out = jnp.dot(act, down_w, preferred_element_type=f32) * weight_ref[0][:, :1]
    out_ref[0] = out.astype(bf16)


def expert_pass(rows, grads, weights, gate, up, down):
    experts, lanes, width = rows.shape
    hidden = gate.shape[2]

    def each(entry):
        return pl.BlockSpec((1,) + entry.shape[1:], lambda step: (step, 0, 0))

    inputs = (rows, grads, weights, gate, up, down)
    small = jax.ShapeDtypeStruct((experts, lanes, hidden), bf16)
    large = jax.ShapeDtypeStruct((experts, lanes, width), bf16)
    outputs = [small] * 3 + [large] * 2
    return pl.pallas_call(
        expert_kernel,
        grid=(experts,),
        in_specs=[each(entry) for entry in inputs],
        out_specs=[each(entry) for entry in outputs],
        out_shape=outputs,
        compiler_params=params(),
        cost_estimate=cost(20),
        name="expert_pass",
    )(*inputs)


def unpack_kernel(half, own, heads, unit, pack_ref, weight_ref, grad_ref, gate_ref, up_ref, sums_ref):
    rows = weight_ref.shape[0]
    lane = lax.broadcasted_iota(jnp.int32, (1, EXTRA), 1)
    low = lane < HEAD_DIM
    groups = 2 * half
    sums = jnp.zeros((rows, EXTRA), f32)

    def tile(index, number):
        return pack_ref[index, :, number * EXTRA : (number + 1) * EXTRA].astype(f32)

    def put(start, value):
        grad_ref[:, start : start + EXTRA] = value
        return value * weight_ref[:, start : start + EXTRA].astype(f32)

    def turn(value, amount):
        amount %= EXTRA
        return pltpu.roll(value, amount, 1) if amount else value

    steps = jnp.zeros((rows, EXTRA), f32)
    shared_b = [jnp.zeros((rows, EXTRA), f32) for _ in range(2 * STATE // EXTRA)]
    for core in range(2):
        for column in range(0, half, 2):
            one, two = 2 * column + core, 2 * column + 2 + core
            values = (tile(one, 2), tile(one, 3), tile(two, 2), tile(two, 3))
            gates = (tile(one, 4), turn(values[1], HEAD_DIM), tile(two, 4), turn(values[3], HEAD_DIM))
            at = core * (INNER // 2) + column * own
            for start, (first, rest, other, other_rest) in ((at, gates), (INNER + at, values)):
                turned = turn(other, HEAD_DIM)
                sums = sums + put(start, first)
                sums = sums + put(start + EXTRA, jnp.where(low, rest, turned))
                sums = sums + put(start + 2 * EXTRA, jnp.where(low, turned, turn(other_rest, HEAD_DIM)))
            for index, place in ((one, column), (two, column + 1)):
                steps = steps + turn(tile(index, 5), core * (HEADS // 2) + place * heads)
                shared_b = [total + tile(index, k) for k, total in enumerate(shared_b)]
    for k, total in enumerate(shared_b):
        sums = sums + put(2 * INNER + k * EXTRA, total)
    at = INNER + CONV_CH
    steps = steps[:, :HEADS]
    grad_ref[:, at : at + HEADS] = steps
    rest = jnp.sum(steps * weight_ref[:, at : at + HEADS].astype(f32), axis=1, keepdims=True)
    sums_ref[...] = jnp.broadcast_to(jnp.sum(sums, axis=1, keepdims=True) + rest, (rows, EXTRA))
    per_tile = EXTRA // unit
    for replica in range(2):
        for start in range(0, groups, per_tile):
            for kind, out_ref in enumerate((gate_ref, up_ref)):
                begin = kind * 2 * unit + replica * unit
                mine = jnp.logical_and(lane >= begin, lane < begin + unit)
                total = jnp.zeros((rows, EXTRA), f32)
                for index in range(start, start + per_tile):
                    part = jnp.where(mine, tile(index, 6), 0.0)
                    total = total + turn(part, (index - start) * unit - begin)
                column = replica * groups * unit + start * unit
                out_ref[:, column : column + EXTRA] = total


def unpack(pack, weight, half, own, heads, unit, hidden_units):
    rows = weight.shape[0]
    shapes = [
        jax.ShapeDtypeStruct((rows, columns), f32)
        for columns in (weight.shape[1], hidden_units, hidden_units, EXTRA)
    ]
    return pl.pallas_call(
        lambda *refs: unpack_kernel(half, own, heads, unit, *refs),
        grid=(1,),
        in_specs=[whole(pack), whole(weight)],
        out_specs=[whole(shape) for shape in shapes],
        out_shape=shapes,
        compiler_params=params(),
        cost_estimate=cost(4),
        name="unpack",
    )(pack, weight)


def local(
    hidden_in,
    cotangent,
    routes,
    route_gates,
    lengths,
    in_proj,
    out_proj,
    conv_weight,
    conv_bias,
    norm_gain,
    mix_gain,
    ffn_gain,
    shared_gate,
    shared_up,
    shared_down,
    expert_gate,
    expert_up,
    expert_down,
    decay_log,
    step_bias,
    skip_gain,
):
    tokens, width = hidden_in.shape
    top = routes.shape[1]
    replicas = lax.axis_size("dp")
    groups = lax.axis_size("z") * 4
    devices = replicas * groups
    core = lax.axis_index("core")
    column = lax.axis_index("z") * 2 + lax.axis_index("y")
    place = column * 2 + core
    heads = HEADS // groups
    own = heads * HEAD_DIM
    half = groups // 2
    rows_in = in_proj.shape[0]
    hidden_units = shared_gate.shape[1]
    unit = hidden_units // devices
    units = hidden_units // groups
    local_experts = expert_gate.shape[0]
    capacity = 2 * tokens * top // (local_experts * groups)
    first_head = core * (HEADS // 2) + column * heads
    first_channel = first_head * HEAD_DIM

    small = (conv_weight.reshape(-1), conv_bias, norm_gain, mix_gain, ffn_gain)
    small_sizes = [entry.shape[0] for entry in small]
    small_lanes = -(-sum(small_sizes) // rows_in)
    small_flat = jnp.concatenate(small)
    small_flat = jnp.pad(small_flat, (0, small_lanes * rows_in - small_flat.shape[0]))

    bounds = jnp.cumsum(lengths[0])
    slot = jnp.arange(tokens, dtype=jnp.int32)
    runs = jnp.sum((slot[:, None] >= bounds[None, : SEQ_SLOTS - 1]).astype(jnp.int32), axis=1)
    live = (runs < SEQ_SLOTS - 1).astype(f32)[:, None]
    starts = jnp.concatenate([jnp.zeros((1,), jnp.int32), bounds[: SEQ_SLOTS - 1].astype(jnp.int32)])
    place_in_run = slot - jnp.sum(jnp.where(runs[:, None] == jnp.arange(SEQ_SLOTS), starts, 0), axis=1)
    beside = [runs.astype(bf16)[:, None], place_in_run.astype(bf16)[:, None], routes.astype(bf16)]
    beside = jnp.concatenate(beside + list(split_three(route_gates)), axis=1)
    beside = jnp.pad(beside, ((0, 0), (0, EXTRA - beside.shape[1])))
    spread = jnp.concatenate([in_proj[:, 2 * INNER :], small_flat.reshape(rows_in, small_lanes)], axis=1)
    spread = jnp.pad(spread, ((0, 0), (0, -spread.shape[1] % EXTRA)))
    spread = dp_gather_rows(spread[None], 0).reshape(replicas * rows_in, -1)
    spread = jnp.pad(spread, ((0, tokens - replicas * rows_in), (0, 0)))
    payload = jnp.concatenate([hidden_in, beside, spread], axis=1)

    def by_place(block):
        block = block.reshape(rows_in, 2, half, own).transpose(2, 1, 0, 3)
        return block.reshape(groups, rows_in, own)

    def by_unit(block):
        block = block.reshape(rows_in, replicas, groups, unit).transpose(2, 0, 1, 3)
        return block.reshape(groups, rows_in, units)

    pack = jnp.concatenate(
        [
            by_place(in_proj[:, :INNER]),
            by_place(in_proj[:, INNER : 2 * INNER]),
            by_unit(shared_gate),
            by_unit(shared_up),
        ],
        axis=2,
    )
    pack = lax.all_to_all(pack, GROUP, split_axis=0, concat_axis=0, tiled=True)

    if replicas == 2:
        both = swap(out_proj, "core")
        both = jnp.concatenate(
            [jnp.where(core == 0, out_proj, both), jnp.where(core == 0, both, out_proj)]
        )
        payload, both = tie(payload, both)
        w_out = jnp.where(lax.axis_index("dp") == core, both, to_channels(both))
    else:
        w_out = lax.dynamic_slice_in_dim(
            lax.all_gather(out_proj, ALL, axis=0, tiled=True), first_channel, own, 0
        )
    def gather_tokens():
        size = lax.axis_size("z")
        block, blocks, pieces = payload, [], []
        arrived = None
        for step in range(size):
            following = ring(block) if step < size - 1 else ()
            near = swap(block, "y")
            if step == 0:
                work = (pack, w_out, w_shared_down)
            elif replicas == 2 and step < 4:
                extent = arrived.shape[0] // 3
                work = swap(after(arrived[(step - 1) * extent : step * extent], block), "dp")
            else:
                work = ()
            following, near, work = tie(following, near, work)
            if step == 0:
                arrived = work[0].reshape(groups * rows_in, -1)
                found = work[1:]
            elif replicas == 2 and step < 4:
                pieces.append(work)
            blocks += [block, near]
            block = following
        near = jnp.concatenate(blocks, axis=0)
        if replicas == 2:
            other = jnp.concatenate(pieces, axis=0)
            mine = lax.axis_index("dp") == 0
            everything = jnp.concatenate(
                [jnp.where(mine, arrived, other), jnp.where(mine, other, arrived)], axis=0
            )
        else:
            everything = lax.all_gather(arrived, "dp", axis=0, tiled=True)
        return near, swap(near, "core"), everything, found

    w_shared_down = dp_gather_rows(shared_down[None], 0).reshape(units, width)
    near, mate, pack, (w_out, w_shared_down) = gather_tokens()
    w_gate, w_up, w_down = (
        lax.all_gather(entry, "dp", axis=1, tiled=True)
        for entry in (expert_gate, expert_up, expert_down)
    )

    table = jnp.concatenate([near[:, width : width + EXTRA], mate[:, width : width + EXTRA]], axis=0)
    routes_all = table[:, 2 : 2 + top].astype(jnp.int32)
    gates_all = join_three([table[:, 2 + k * top : 2 + (k + 1) * top] for k in (1, 2, 3)])
    number = jnp.arange(groups, dtype=jnp.int32)
    back_z = (lax.axis_index("z") - number // 4) % (groups // 4)
    other_y = (number // 2) % 2 != lax.axis_index("y")
    other_core = number % 2 != core
    order = other_core * half + back_z * 2 + other_y

    def blocks_of(entry):
        return entry[:, width + EXTRA :].reshape(half, tokens, -1)[:, : replicas * rows_in]

    spread = jnp.concatenate([blocks_of(near), blocks_of(mate)], axis=0)[order]
    spread, w_gate = tie(spread, w_gate)
    spread = spread.reshape(groups, replicas, rows_in, -1).transpose(1, 0, 2, 3)
    spread = spread.reshape(devices, rows_in, -1)
    small_at = 2 * STATE + HEADS
    small_all = spread[:, :, small_at : small_at + small_lanes].reshape(devices, -1)
    pieces = []
    start = 0
    for size in small_sizes:
        pieces.append(small_all[:, start : start + size].reshape(-1).astype(f32))
        start += size
    conv_w_all = pieces[0].reshape(CONV_CH, KERNEL).T
    conv_b_all, norm_gain_all, mix_gain_all, ffn_gain_all = pieces[1:]
    spread = spread.reshape(devices * rows_in, -1)
    w_step = lax.dynamic_slice_in_dim(spread, 2 * STATE + first_head, heads, 1)
    w_step = jnp.pad(w_step, ((0, 0), (0, EXTRA - heads)))
    w_in = [spread[:, : 2 * STATE], pack[:, own : 2 * own], pack[:, EXTRA:own], pack[:, :EXTRA], w_step]
    w_in = jnp.concatenate(w_in, axis=1)
    w_shared_gate = pack[:, 2 * own : 2 * own + units]
    w_shared_up = pack[:, 2 * own + units :]

    def own_channels(rows):
        return lax.dynamic_slice_in_dim(rows, first_channel, own, rows.ndim - 1)

    conv = jnp.concatenate([conv_w_all, conv_b_all[None]], axis=0)
    conv = jnp.concatenate([conv[:, INNER:], own_channels(conv)], axis=1)
    conv = jnp.pad(conv, ((0, 8 - conv.shape[0]), (0, CONV_LANES - conv.shape[1])))

    def own_heads(row):
        return lax.dynamic_slice_in_dim(row, first_head, heads, 0)

    def lanes_of(row):
        return jnp.pad(row, (0, WIDE - row.shape[0]))

    rate = -jnp.exp(own_heads(decay_log))
    head = [
        lanes_of(own_heads(step_bias)),
        lanes_of(rate),
        lanes_of(jnp.repeat(own_heads(skip_gain), HEAD_DIM)),
        lanes_of(own_channels(mix_gain_all)),
    ]
    head = jnp.pad(jnp.stack(head), ((0, 4), (0, 0)))
    rate_rows = jnp.broadcast_to(jnp.pad(rate, (0, 8 - heads))[:, None], (8, EXTRA))
    w_out = jnp.pad(w_out, ((0, WIDE - own), (0, 0)))

    input_rows = hidden_in.astype(f32)
    grad_out = cotangent.astype(f32)
    branch = after((grad_out * live).astype(bf16), near)

    pairs = groups // 2
    pair_tokens = 2 * tokens
    pair_slots = 2 * capacity
    numbers = place * local_experts + jnp.arange(local_experts, dtype=jnp.int32)
    named = routes_all[:, None, :] == numbers[None, :, None]
    member = jnp.any(named, axis=2).T.reshape(local_experts, pairs, pair_tokens)
    weight = jnp.sum(jnp.where(named, gates_all[:, None, :], 0.0), axis=2).T
    weight = weight.reshape(local_experts, pairs, pair_tokens)
    below = jnp.triu(jnp.ones((pair_tokens, pair_tokens), bf16))
    rank = matmul(member.astype(bf16), below)
    rank = jnp.where(member, rank.astype(jnp.int32) - 1, -1).transpose(1, 0, 2)
    rank = jnp.pad(rank, ((0, 0), (0, 8 - local_experts), (0, 0)), constant_values=-1)
    weight = jnp.pad(weight.transpose(1, 0, 2), ((0, 0), (0, 8 - local_experts), (0, 0)))
    half_pairs = pairs // 2

    def rows_out(values, first, shared, into=None):
        return dispatch(values, rank, weight, local_experts, pair_slots, first, shared, into)

    mixer = (norm_gain_all[None], w_in, w_out, conv, head)

    def forward(part):
        return lambda token: mixer_forward(after(part, token), width, tokens, *after(mixer, token))

    branch_near, branch_mate, (mixer_set, done_mate, done_near, _) = gather(
        branch, [mixer, forward(mate), forward(near)]
    )
    _, w_in, w_out, conv, head = mixer_set
    normed_mate, proj_mate, mixed_mate, scaled_mate = done_mate
    normed_near, proj_near, mixed_near, scaled_near = done_near
    pairs_sum = scatter_first(mixed_near, mixed_mate)
    mixed_sum, (_, _, w_up, *_) = scatter_last(pairs_sum, [(), (), w_up])
    mix_rms = lax.rsqrt(jnp.sum(mixed_sum[:, width:], axis=1, keepdims=True) / INNER + epsilon)
    mixer_out = mixed_sum[:, :width] * mix_rms
    resid = input_rows + live * mixer_out
    ffn_rms = lax.rsqrt(jnp.mean(resid * resid, axis=1, keepdims=True) + epsilon)
    ffn_hat = resid * ffn_rms

    def grads_near(token):
        return rows_out(after(branch_near, token), 0, (w_shared_down,))

    done_rows = []

    def grads_mate(token):
        return rows_out(after(branch_mate, token), half_pairs, (w_shared_down,), done_rows[0])

    def keep(work):
        def kept(token):
            found = work(token)
            done_rows.append(found[:2])
            return found

        return kept

    ffn_near, ffn_mate, ((_, _, act_grad_near), (d_row, slot_weight, act_grad_mate), *_) = gather(
        (ffn_hat * ffn_gain_all).astype(bf16), [keep(grads_near), grads_mate]
    )

    expert_in, shared_near, sg_near, su_near = rows_out(
        ffn_near, 0, (act_grad_near, w_shared_gate, w_shared_up)
    )
    expert_in, shared_mate, sg_mate, su_mate = rows_out(
        ffn_mate, half_pairs, (act_grad_mate, w_shared_gate, w_shared_up), (expert_in,)
    )
    act_low, g_low, u_low, d_in_row, expert_row = expert_pass(
        expert_in, d_row, slot_weight, w_gate, w_up, w_down
    )

    half_grad = (((1,), (1,)), ((0,), (0,)))
    grad_down = matmul(act_low, d_row, half_grad).astype(bf16)
    d_in_row, grad_down = tie(d_in_row, grad_down)

    def back_rows(sg, su, first):
        terms = ((sg, w_shared_gate), (su, w_shared_up))
        return combine(d_in_row, rank, terms, pair_slots, first, True)

    grad_ffn_mate = back_rows(sg_mate, su_mate, half_pairs)
    grad_ffn_near = back_rows(sg_near, su_near, 0)
    pairs_sum = scatter_first(grad_ffn_near, grad_ffn_mate)

    def leaving_of(part):
        return lambda token: matmul(after(expert_in, token), part, half_grad).astype(bf16)

    grad_ffn, leaving = scatter_last(pairs_sum, [leaving_of(g_low), leaving_of(u_low)])
    grad_down, grad_gate, grad_up = (
        lax.psum_scatter(entry, "dp", scatter_dimension=1, tiled=True)
        for entry in (grad_down, *leaving[:2])
    )

    grad_ffn_gain = jnp.sum(grad_ffn * ffn_hat, axis=0)
    scaled_ffn = grad_ffn * ffn_gain_all
    grad_resid = grad_out + ffn_rms * (
        scaled_ffn - ffn_hat * jnp.mean(scaled_ffn * ffn_hat, axis=1, keepdims=True)
    )
    d_mixer = (grad_resid * live).astype(bf16).astype(f32)
    inner_term = jnp.sum(d_mixer * mixer_out, axis=1, keepdims=True) * mix_rms * mix_rms / INNER
    inner_pack = jnp.pad(jnp.concatenate(split_three(inner_term), axis=1), ((0, 0), (0, EXTRA - 3)))
    d_mixer_pack = jnp.concatenate([(d_mixer * mix_rms).astype(bf16), inner_pack], axis=1)

    def out_rows(shared_act, first):
        def work(token):
            terms = ((shared_act, w_shared_down),)
            return combine(after(expert_row, token), rank, terms, pair_slots, first, False)

        return work

    turned = (((0,), (0,)), ((), ()))

    def of_halves(left, right):
        return matmul(left[0], right[0], turned) + matmul(left[1], right[1], turned)

    def shared_grads_of(token):
        halves = after(((branch_near, branch_mate), (ffn_near, ffn_mate)), token)
        return (
            of_halves((shared_near, shared_mate), halves[0]),
            of_halves(halves[1], (sg_near, sg_mate)),
            of_halves(halves[1], (su_near, su_mate)),
        )

    d_mixer_near, d_mixer_mate, (out_mate, out_near, shared_grads, grad_down) = gather(
        d_mixer_pack,
        [
            out_rows(shared_mate, half_pairs),
            out_rows(shared_near, 0),
            shared_grads_of,
            lambda token: after(grad_down, token).astype(f32),
        ],
    )
    grad_shared_down, grad_shared_g, grad_shared_u = shared_grads
    grad_shared_gu = jnp.concatenate([grad_shared_g, grad_shared_u], axis=1)
    grad_out_rows = of_halves(
        (scaled_near, scaled_mate), (d_mixer_near[:, :width], d_mixer_mate[:, :width])
    )[:own]
    out_rows_low = grad_out_rows.astype(bf16)
    out_pairs = scatter_first(out_near, out_mate)
    (d_mixer_near, d_mixer_mate), out_pairs, out_rows_low = tie(
        (d_mixer_near, d_mixer_mate), out_pairs, out_rows_low
    )

    def backward(grads, part, proj, first, into=()):
        return mixer_backward(
            grads, part, proj, width, tokens, w_in, w_out, conv, head, rate_rows, first, into
        )

    def towards(step):
        return swap(out_pairs[step][1], "y")

    def window(work, *others):
        return tie(work, *others)

    part_one = backward(d_mixer_mate, mate, proj_mate, 0)
    out_there = {1: towards(1), 2: towards(2)}
    part_one, out_there, out_pairs, d_mixer_mate = window(part_one, out_there, out_pairs, d_mixer_mate)
    done_mate = backward(d_mixer_mate, mate, proj_mate, 1, part_one[:2])
    out_total = ring_step(add_low(out_pairs[1][0], out_there[1]), out_pairs, out_there, 1)
    out_there[3] = towards(3)
    done_mate, out_total, out_there, out_pairs, d_mixer_near = window(
        done_mate, out_total, out_there, out_pairs, d_mixer_near
    )
    part_two = backward(d_mixer_near, near, proj_near, 0)
    moved = swap(done_mate[0], "core")
    out_total = ring_step(out_total, out_pairs, out_there, 2)
    out_there[0] = towards(0)
    part_two, moved, out_total, out_there, out_pairs, d_mixer_near = window(
        part_two, moved, out_total, out_there, out_pairs, d_mixer_near
    )
    out_rows_there = from_channels(after(out_rows_low, part_two[0])) if replicas == 2 else ()
    done_near = backward(d_mixer_near, near, proj_near, 1, part_two[:2])
    branch_sum = ring_step(out_total, out_pairs, out_there, 3)
    done_near, branch_sum, grad_gate = window(done_near, branch_sum, grad_gate)
    grad_shared_gu = dp_scatter_rows(grad_shared_gu, 0, done_near[0])
    grad_shared_down = dp_scatter_rows(grad_shared_down.reshape(replicas, unit, width), 0, done_near[0])[0]
    normed_grad_mate, proj_low_mate = done_mate[:2]
    normed_grad_near, proj_low_near = done_near[:2]
    conv_parts = [part_one[2], done_mate[2], part_two[2], done_near[2]]
    head_parts = [part_one[3], done_mate[3], part_two[3], done_near[3]]
    pairs_sum = scatter_first(normed_grad_near, normed_grad_mate, moved)

    def to_owner(part):
        rows_part = jnp.zeros((part.shape[0], CONV_CH), f32)
        values = part[:, 2 * STATE : 2 * STATE + own]
        rows_part = lax.dynamic_update_slice_in_dim(rows_part, values, first_channel, 1)
        rows_part = lax.dynamic_update_slice_in_dim(rows_part, part[:, : 2 * STATE], INNER, 1)
        return rows_part.reshape(part.shape[0], devices, -1).transpose(1, 0, 2).reshape(devices, -1)

    def head_row(part):
        return lax.dynamic_update_slice_in_dim(jnp.zeros((HEADS,), f32), part, first_head, 0)

    def small_sums(conv_grads, head_grads):
        head_grads = jnp.sum(head_grads.reshape(3, 8, EXTRA)[:, :heads], axis=2)
        head_rows = [head_row(entry) for entry in (head_grads[0] * rate, *head_grads[1:])]
        return jnp.concatenate(
            [
                to_owner(conv_grads[: KERNEL + 1]),
                grad_ffn_gain.reshape(devices, -1),
                jnp.broadcast_to(jnp.concatenate(head_rows)[None], (devices, 3 * HEADS)),
            ],
            axis=1,
        )

    crossing = replicas == 2
    here = lax.axis_index("dp")
    normed_rows = width // 2 if crossing else width

    def input_grad(where, token):
        parts = after((normed_near, normed_mate), token)
        if crossing:
            parts = [lax.dynamic_slice_in_dim(part, where * normed_rows, normed_rows, 1) for part in parts]
        return of_halves(parts, (proj_low_near, proj_low_mate))

    def piece(array, index, token):
        extent = array.shape[0] // 3
        return swap(after(array[index * extent : (index + 1) * extent], token), "dp")

    pieces = []

    def small_work(token):
        parts = after((conv_parts, head_parts), token)
        return small_sums(sum(parts[0]), sum(parts[1]))

    there = scatter_beside(pairs_sum)
    total = add_low(pairs_sum[1][0], there[1])
    total, leaving, out_rows_there = tie(
        total, input_grad(1 - here, pairs_sum).astype(bf16), out_rows_there
    )
    finished = []
    works = (lambda token: input_grad(here, token), small_work, lambda token: grad_up)
    for index, work in enumerate(works):
        following = ring_step(total, pairs_sum, there, index + 1)
        across = piece(leaving, index, total) if crossing else ()
        total, across, result = tie(following, across, work(total))
        pieces.append(across)
        finished.append(result)
    grad_w_in, sums, grad_up = finished
    grad_normed = total
    output = (resid + live * branch_sum).astype(bf16)

    if crossing:
        grad_w_in = grad_w_in + jnp.concatenate(pieces, axis=0).astype(f32)
    else:
        grad_w_in = lax.psum_scatter(leaving, "dp", scatter_dimension=0, tiled=True)
    grad_pack = jnp.concatenate([grad_w_in.astype(bf16), grad_shared_gu.astype(bf16)], axis=1)
    grad_pack = grad_pack.reshape(groups, rows_in, -1)
    grad_gate, grad_up = (entry.astype(f32) for entry in after((grad_gate, grad_up), grad_pack))
    grad_pack = lax.all_to_all(grad_pack, GROUP, split_axis=0, concat_axis=0, tiled=True)

    def from_place(block):
        block = block.reshape(half, 2, rows_in, block.shape[2]).transpose(2, 1, 0, 3)
        return block.reshape(rows_in, -1)

    def from_unit(block):
        block = block.reshape(groups, rows_in, replicas, unit).transpose(1, 2, 0, 3)
        return block.reshape(rows_in, hidden_units)

    if replicas == 2:
        grad_in_proj, grad_shared_gate, grad_shared_up, gain_sums = unpack(
            grad_pack, in_proj, half, own, heads, unit, hidden_units
        )
        gain_sums = gain_sums[:, 0]
    else:
        grad_pack = grad_pack.astype(f32)
        value_at, gate_at, step_at = 2 * STATE, CONV_LANES, CONV_LANES + EXTRA
        gate_part = [grad_pack[:, :, gate_at : gate_at + EXTRA], grad_pack[:, :, value_at + own : gate_at]]
        grad_in_proj = jnp.concatenate(
            [
                from_place(jnp.concatenate(gate_part, axis=2)),
                from_place(grad_pack[:, :, value_at : value_at + own]),
                jnp.sum(grad_pack[:, :, : 2 * STATE], axis=0),
                from_place(grad_pack[:, :, step_at : step_at + heads]),
            ],
            axis=1,
        )
        grad_shared_gate = from_unit(grad_pack[:, :, PROJ_LANES : PROJ_LANES + units])
        grad_shared_up = from_unit(grad_pack[:, :, PROJ_LANES + units :])
        gain_sums = jnp.sum(grad_in_proj * in_proj.astype(f32), axis=1)
    if replicas == 2:
        mine = lax.axis_index("dp") == core
        total = (grad_out_rows + out_rows_there.astype(f32)).reshape(2, own // 2, width)
        passed = swap(lax.dynamic_index_in_dim(total, 1 - core, 0, keepdims=False), "core")
        grad_out_proj = jnp.where(mine, lax.dynamic_index_in_dim(total, core, 0, keepdims=False), passed)
    else:
        full = jnp.zeros((INNER, width), f32)
        full = lax.dynamic_update_slice_in_dim(full, grad_out_rows, first_channel, 0)
        grad_out_proj = lax.psum_scatter(full, ALL, scatter_dimension=0, tiled=True)
    grad_mix_gain = jnp.sum(grad_out_proj * out_proj.astype(f32), axis=1) / mix_gain.astype(f32)
    grad_norm_gain = gain_sums / norm_gain.astype(f32)

    sums = lax.all_to_all(sums, ALL, split_axis=0, concat_axis=0, tiled=True)
    sums = jnp.sum(sums, axis=0)
    channels = CONV_CH // devices
    grad_conv_weight = sums[: KERNEL * channels].reshape(KERNEL, channels).T
    grad_conv_bias = sums[KERNEL * channels : (KERNEL + 1) * channels]
    at = (KERNEL + 1) * channels
    grad_ffn_gain = sums[at : at + rows_in]
    at += rows_in
    grad_decay, grad_stepb, grad_skip = (sums[at + k * HEADS : at + (k + 1) * HEADS] for k in range(3))

    in_rms = lax.rsqrt(jnp.mean(input_rows * input_rows, axis=1, keepdims=True) + epsilon)
    in_hat = input_rows * in_rms
    scaled_in = grad_normed * norm_gain_all
    grad_input = grad_resid + in_rms * (
        scaled_in - in_hat * jnp.mean(scaled_in * in_hat, axis=1, keepdims=True)
    )
    return (
        output,
        grad_input,
        grad_in_proj,
        grad_out_proj,
        grad_conv_weight,
        grad_conv_bias,
        grad_norm_gain,
        grad_mix_gain,
        grad_ffn_gain,
        grad_shared_gate,
        grad_shared_up,
        grad_shared_down,
        grad_gate,
        grad_up,
        grad_down,
        grad_decay,
        grad_stepb,
        grad_skip,
    )


def solution(mesh):
    replicas, groups = mesh.shape["dp"], mesh.shape["expert"]
    inner = Mesh(mesh.devices.reshape(replicas, groups // 4, 2, 2), ALL)
    flat = P(ALL)
    expert = P(GROUP, "dp", None)
    return jax.shard_map(
        local,
        mesh=inner,
        in_specs=(flat,) * 15 + (expert,) * 3 + (P(),) * 3,
        out_specs=(flat,) * 12 + (expert,) * 3 + (P(),) * 3,
        check_vma=False,
    )
```

```python
import jax
import jax.numpy as jnp
from jax import lax
from jax.experimental import pallas as pl
from jax.experimental.pallas import tpu as pltpu
from jax.sharding import Mesh, PartitionSpec as P

HEADS = 48
HEAD_DIM = 64
STATE = 128
KERNEL = 4
SEQ_SLOTS = 3
INNER = 3072
CONV_CH = 3328
EXTRA = 128

epsilon = 1e-05
bf16 = jnp.bfloat16
f32 = jnp.float32
GROUP = ("z", "y", "core")
ALL = ("dp", "z", "y", "core")


def matmul(left, right, dims=None, precision=None):
    if dims is None:
        dims = (((left.ndim - 1,), (0,)), ((), ()))
    return lax.dot_general(left, right, dims, precision=precision, preferred_element_type=f32)


def swap(value, axis):
    return lax.ppermute(value, axis, [(0, 1), (1, 0)])


def ring(value):
    size = lax.axis_size("z")
    return lax.ppermute(value, "z", [(k, (k + 1) % size) for k in range(size)])


def after(value, *earlier):
    return lax.optimization_barrier((value, earlier))[0]


def split_three(value):
    high = lax.reduce_precision(value, 8, 7)
    rest = value - high
    middle = lax.reduce_precision(rest, 8, 7)
    return high.astype(bf16), middle.astype(bf16), (rest - middle).astype(bf16)


def join_three(parts):
    return parts[0].astype(f32) + parts[1].astype(f32) + parts[2].astype(f32)


def tie(value, *others):
    return lax.optimization_barrier((value, *others))


def work_of(entry, token):
    return entry(token) if callable(entry) else entry


def gather(block, beside_work=()):
    size = lax.axis_size("z")
    beside_work = (list(beside_work) + [()] * size)[:size]
    blocks = []
    for step in range(size):
        following = ring(block) if step < size - 1 else ()
        near = swap(block, "y")
        work = work_of(beside_work[step], block)
        following, near, beside_work[step] = tie(following, near, work)
        blocks += [block, near]
        block = following
    own = jnp.concatenate(blocks, axis=0)
    return own, swap(own, "core"), beside_work


def to_channels(value):
    return lax.ppermute(value, ("dp", "core"), [(0, 2), (3, 1)])


def from_channels(value):
    return lax.ppermute(value, ("dp", "core"), [(2, 0), (1, 3)])


def add_low(left, right):
    return (left.astype(f32) + right.astype(f32)).astype(bf16)


def scatter_first(near, mate, moved=None):
    size = lax.axis_size("z")
    shape = (size, 2, near.shape[0] // (2 * size), near.shape[1])
    there = (swap(mate, "core") if moved is None else moved).reshape(shape)
    near = near.reshape(shape)
    pairs = [add_low(near[step], there[step]) for step in range(size)]
    return pairs


def scatter_beside(pairs):
    size = len(pairs)
    order = list(range(1, size)) + [0]
    there = {step: swap(pairs[step][1], "y") for step in order}
    return [there[step] for step in range(size)]


def ring_step(total, pairs, there, step):
    at = (step + 1) % len(pairs)
    total = ring(total).astype(f32) + (pairs[at][0].astype(f32) + there[at].astype(f32))
    return total.astype(bf16) if at else total


def scatter_last(pairs, beside_work=(), there=None):
    size = len(pairs)
    beside_work = (list(beside_work) + [()] * size)[:size]
    there = there or scatter_beside(pairs)
    total = add_low(pairs[1][0], there[1])
    token = pairs
    for step in range(1, size):
        total, beside_work[step - 1] = tie(total, work_of(beside_work[step - 1], token))
        token = total
        total = ring_step(total, pairs, there, step)
    total, beside_work[-1] = tie(total, work_of(beside_work[-1], token))
    return total, beside_work


def dp_gather_rows(value, axis):
    if lax.axis_size("dp") != 2:
        return lax.all_gather(value, "dp", axis=axis, tiled=True)
    other = swap(value, "dp")
    first = lax.axis_index("dp") == 0
    return jnp.concatenate(
        [jnp.where(first, value, other), jnp.where(first, other, value)], axis=axis
    )


def dp_scatter_rows(value, axis, hold=()):
    count = lax.axis_size("dp")
    if count != 2:
        return lax.psum_scatter(value.astype(bf16), "dp", scatter_dimension=axis, tiled=True).astype(f32)
    place = lax.axis_index("dp")
    extent = value.shape[axis] // count
    sent = lax.dynamic_slice_in_dim(value, (1 - place) * extent, extent, axis).astype(bf16)
    kept = lax.dynamic_slice_in_dim(value, place * extent, extent, axis)
    received, kept, hold = tie(swap(sent, "dp"), kept, hold)
    return kept + received.astype(f32)


def params(steps=1):
    return pltpu.CompilerParams(
        dimension_semantics=("arbitrary",) * steps, vmem_limit_bytes=56 * 1024 * 1024
    )


def cost(micros):
    return pl.CostEstimate(
        flops=int(micros * 1.1e9), bytes_accessed=int(micros * 3.5e6), transcendentals=0
    )


def whole(array):
    return pl.BlockSpec(array.shape, lambda step: (0,) * array.ndim)


def sigmoid(value):
    return 1.0 / (1.0 + jnp.exp(-value))


def halves_of(value):
    high = value.astype(bf16)
    return high, (value - high.astype(f32)).astype(bf16)


def exact(left, right, dims):
    (left_high, left_low), (right_high, right_low) = halves_of(left), halves_of(right)

    def dot(one, other):
        return lax.dot_general(one, other, (dims, ((), ())), preferred_element_type=f32)

    return dot(left_high, right_high) + (dot(left_high, right_low) + dot(left_low, right_high))


def rows_of(array, index):
    return array[index : index + 1]


WIDE = 256
CONV_LANES = 2 * STATE + WIDE
PROJ_LANES = CONV_LANES + 2 * EXTRA


def triangle(count):
    row = lax.broadcasted_iota(jnp.int32, (count, count), 0)
    column = lax.broadcasted_iota(jnp.int32, (count, count), 1)
    return row - column


def block_scan(proj, place, conv, head):
    heads = HEADS // 16
    count = proj.shape[0]
    taps = [proj[:, :CONV_LANES]]
    total = rows_of(conv, KERNEL) + rows_of(conv, KERNEL - 1) * taps[0]
    for offset in range(1, KERNEL):
        inside = (place >= offset).astype(f32)
        taps.append(pltpu.roll(taps[0], offset, 0) * inside)
        total = total + rows_of(conv, KERNEL - 1 - offset) * taps[offset]
    conv_sig = sigmoid(total)
    conv_out = total * conv_sig
    b_part, c_part = conv_out[:, :STATE], conv_out[:, STATE : 2 * STATE]
    raw = proj[:, CONV_LANES + EXTRA :] + rows_of(head, 0)[:, :EXTRA]
    step = jnp.maximum(raw, 0.0) + jnp.log1p(jnp.exp(-jnp.abs(raw)))
    distance = triangle(count)
    lower = (distance >= 0).astype(f32)
    cumul = exact(lower, step * rows_of(head, 1)[:, :EXTRA], ((1,), (0,)))
    cumul_rows = cumul.T
    step_rows = step.T
    scores = exact(c_part, b_part, ((1,), (1,)))
    reach = jnp.logical_and(distance >= 0, distance.astype(f32) <= place)
    lane = lax.broadcasted_iota(jnp.int32, (1, 2 * HEAD_DIM), 1)
    decays, values, scan = [], [], [None] * (WIDE // EXTRA)
    for index in range(heads):
        tile = index // 2
        spread = cumul[:, index : index + 1] - rows_of(cumul_rows, index)
        decay = jnp.exp(jnp.where(reach, spread, -1e30))
        mine = (lane // HEAD_DIM == index % 2).astype(f32)
        at = 2 * STATE + tile * EXTRA
        value = conv_out[:, at : at + EXTRA] * mine
        mixing = decay * scores * rows_of(step_rows, index)
        part = exact(mixing, value, ((1,), (0,)))
        scan[tile] = part if scan[tile] is None else scan[tile] + part
        decays.append((decay, mixing))
        values.append((value, mine))
    scan = jnp.concatenate(scan, axis=1) + rows_of(head, 2) * conv_out[:, 2 * STATE :]
    turned = pltpu.roll(proj[:, CONV_LANES - EXTRA : CONV_LANES], HEAD_DIM, 1)
    turned = jnp.where(lane < HEAD_DIM, turned, 0.0)
    gate = jnp.concatenate([proj[:, CONV_LANES : CONV_LANES + EXTRA], turned], axis=1)
    gate_sig = sigmoid(gate)
    gated = scan * (gate * gate_sig)
    return dict(
        taps=taps, total=total, conv_sig=conv_sig, conv_out=conv_out, raw=raw, step_rows=step_rows,
        scores=scores, decays=decays, values=values, scan=scan, gate=gate, gate_sig=gate_sig,
        gated=gated, lower=lower,
    )


def mixer_forward_kernel(
    count, tokens_ref, beside_ref, gain_ref, w_in_ref, w_out_ref, conv_ref, head_ref,
    normed_ref, proj_ref, part_ref, scaled_ref,
):
    rows = tokens_ref[...].astype(f32)
    normed = rows * lax.rsqrt(jnp.mean(rows * rows, axis=1, keepdims=True) + epsilon) * gain_ref[...]
    normed = normed.astype(bf16)
    normed_ref[...] = normed
    proj_ref[...] = jnp.dot(normed, w_in_ref[...], preferred_element_type=f32)
    conv, head = conv_ref[...], head_ref[...]
    width = tokens_ref.shape[1]
    for index in range(tokens_ref.shape[0] // count):
        part = pl.ds(index * count, count)
        place = beside_ref[part, :].astype(f32)[:, 1:2]
        found = block_scan(proj_ref[part, :], place, conv, head)
        gated = found["gated"]
        scaled_ref[part, :] = (gated * rows_of(head, 3)).astype(bf16)
        square = gated * gated
        square = square[:, :EXTRA] + square[:, EXTRA:]
        part_ref[part, width:] = square.astype(bf16)
    part_ref[:, :width] = jnp.dot(
        scaled_ref[...], w_out_ref[...], preferred_element_type=f32
    ).astype(bf16)


def mixer_forward(gathered, width, count, gain, w_in, w_out, conv, head):
    total = gathered.shape[0]
    rows = 4 * count
    lanes = width // EXTRA

    def rows_spec(extent, column=0):
        return pl.BlockSpec((rows, extent), lambda step: (step, column))

    return pl.pallas_call(
        lambda *refs: mixer_forward_kernel(count, *refs),
        grid=(total // rows,),
        in_specs=[rows_spec(width), rows_spec(EXTRA, lanes)]
        + [whole(entry) for entry in (gain, w_in, w_out, conv, head)],
        out_specs=[rows_spec(width), rows_spec(PROJ_LANES), rows_spec(width + EXTRA), rows_spec(WIDE)],
        out_shape=[
            jax.ShapeDtypeStruct((total, width), bf16),
            jax.ShapeDtypeStruct((total, PROJ_LANES), f32),
            jax.ShapeDtypeStruct((total, width + EXTRA), bf16),
            jax.ShapeDtypeStruct((total, WIDE), bf16),
        ],
        compiler_params=params(),
        cost_estimate=cost(total / 80),
        name="mixer_forward",
    )(gathered, gathered, gain, w_in, w_out, conv, head)


def mixer_backward_kernel(
    count, grad_ref, inner_ref, beside_ref, proj_ref, w_in_ref, w_out_ref, conv_ref, head_ref, rate_ref,
    *refs,
):
    normed_ref, proj_grad_ref, conv_grad_ref, head_grad_ref = refs[-4:]
    heads = HEADS // 16
    conv, head = conv_ref[...], head_ref[...]

    @pl.when(pl.program_id(0) == 0)
    def _():
        conv_grad_ref[...] = jnp.zeros_like(conv_grad_ref)
        head_grad_ref[...] = jnp.zeros_like(head_grad_ref)

    grad_mixed = lax.dot_general(
        grad_ref[...], w_out_ref[...], (((1,), (1,)), ((), ())), preferred_element_type=f32
    )
    lane = lax.broadcasted_iota(jnp.int32, (1, EXTRA), 1)
    for index in range(grad_ref.shape[0] // count):
        part = pl.ds(index * count, count)
        place = beside_ref[part, :].astype(f32)[:, 1:2]
        found = block_scan(proj_ref[part, :], place, conv, head)
        inner = inner_ref[part, :].astype(f32)
        inner = inner[:, 0:1] + inner[:, 1:2] + inner[:, 2:3]
        gate, gate_sig, scan = found["gate"], found["gate_sig"], found["scan"]
        d_gated = grad_mixed[index * count : (index + 1) * count] * rows_of(head, 3) - found["gated"] * inner
        d_scan = d_gated * (gate * gate_sig)
        d_gate = d_gated * scan * (gate_sig * (1.0 + gate * (1.0 - gate_sig)))
        conv_out = found["conv_out"]
        d_values = [None] * (WIDE // EXTRA)
        d_scores = jnp.zeros((count, count), f32)
        column_sums = jnp.zeros((count, EXTRA), f32)
        direct, taken = [], []
        for number in range(heads):
            tile = number // 2
            decay, mixing = found["decays"][number]
            value, mine = found["values"][number]
            d_part = d_scan[:, tile * EXTRA : (tile + 1) * EXTRA]
            back = exact(mixing, d_part, ((0,), (0,))) * mine
            d_values[tile] = back if d_values[tile] is None else d_values[tile] + back
            d_mixing = exact(d_part, value, ((1,), (1,)))
            d_decayed = d_mixing * decay
            d_scores = d_scores + d_decayed * rows_of(found["step_rows"], number)
            d_spread = d_mixing * mixing
            direct.append(jnp.sum(d_decayed * found["scores"], axis=0, keepdims=True))
            taken.append(jnp.sum(d_spread, axis=0, keepdims=True))
            sums = jnp.sum(d_spread, axis=1, keepdims=True)
            column_sums = column_sums + jnp.where(lane == number, sums, 0.0)
            head_grad_ref[16 + number : 17 + number, :] += jnp.sum(d_part * value, axis=0, keepdims=True)
        d_values = jnp.concatenate(d_values, axis=1) + rows_of(head, 2) * d_scan
        empty = jnp.zeros((8 - heads, count), f32)
        d_cumul = column_sums.T[:8] - jnp.concatenate(taken + [empty], axis=0)
        d_rated = exact(d_cumul, found["lower"], ((1,), (0,)))
        step_rows = found["step_rows"][:8]
        d_step = jnp.concatenate(direct + [empty], axis=0) + d_rated * rate_ref[...]
        d_raw = d_step * sigmoid(found["raw"]).T[:8]
        head_grad_ref[0:8, :] += d_rated * step_rows
        head_grad_ref[8:16, :] += d_raw
        d_raw = jnp.concatenate([d_raw, jnp.zeros((EXTRA - 8, count), f32)], axis=0).T
        d_b = exact(d_scores, conv_out[:, STATE : 2 * STATE], ((0,), (0,)))
        d_c = exact(d_scores, conv_out[:, :STATE], ((1,), (0,)))
        d_out = jnp.concatenate([d_b, d_c, d_values], axis=1)
        conv_sig = found["conv_sig"]
        d_total = d_out * (conv_sig * (1.0 + found["total"] * (1.0 - conv_sig)))
        conv_grad_ref[KERNEL : KERNEL + 1, :] += jnp.sum(d_total, axis=0, keepdims=True)
        d_conv = rows_of(conv, KERNEL - 1) * d_total
        for offset in range(KERNEL):
            row = KERNEL - 1 - offset
            conv_grad_ref[row : row + 1, :] += jnp.sum(d_total * found["taps"][offset], axis=0, keepdims=True)
            if offset:
                kept = d_total * (place >= offset).astype(f32)
                d_conv = d_conv + rows_of(conv, row) * pltpu.roll(kept, count - offset, 0)
        shared_tile = d_conv[:, CONV_LANES - EXTRA :] + pltpu.roll(d_gate[:, EXTRA:], HEAD_DIM, 1)
        d_proj = [d_conv[:, : CONV_LANES - EXTRA], shared_tile, d_gate[:, :EXTRA], d_raw]
        proj_grad_ref[part, :] = jnp.concatenate(d_proj, axis=1).astype(bf16)
    normed_ref[...] = lax.dot_general(
        proj_grad_ref[...], w_in_ref[...], (((1,), (1,)), ((), ())), preferred_element_type=f32
    ).astype(bf16)


def mixer_backward(grads, gathered, proj, width, count, w_in, w_out, conv, head, rate, first, into=()):
    total = grads.shape[0]
    rows = 4 * count
    lanes = width // EXTRA

    def rows_spec(extent, column=0):
        return pl.BlockSpec((rows, extent), lambda step: (first + step, column))

    conv_shape = jax.ShapeDtypeStruct(conv.shape, f32)
    head_shape = jax.ShapeDtypeStruct((24, EXTRA), f32)
    in_specs = [rows_spec(width), rows_spec(EXTRA, lanes), rows_spec(EXTRA, lanes), rows_spec(PROJ_LANES)]
    in_specs += [whole(entry) for entry in (w_in, w_out, conv, head, rate)]
    aliases = {len(in_specs) + index: index for index in range(len(into))}
    in_specs += [pl.BlockSpec(memory_space=pl.ANY)] * len(into)
    return pl.pallas_call(
        lambda *refs: mixer_backward_kernel(count, *refs),
        grid=(1,),
        in_specs=in_specs,
        out_specs=[rows_spec(width), rows_spec(PROJ_LANES), whole(conv_shape), whole(head_shape)],
        out_shape=[
            jax.ShapeDtypeStruct((total, width), bf16),
            jax.ShapeDtypeStruct((total, PROJ_LANES), bf16),
            conv_shape,
            head_shape,
        ],
        input_output_aliases=aliases,
        compiler_params=params(),
        cost_estimate=cost(10),
        name="mixer_backward",
    )(grads, grads, gathered, proj, w_in, w_out, conv, head, rate, *into)


def selection(rank_ref, experts, slots):
    number = lax.broadcasted_iota(jnp.int32, (slots, rank_ref.shape[2]), 0)
    return [rank_ref[0, k : k + 1, :] == number for k in range(experts)]


def dispatch_kernel(experts, slots, grads, rank_ref, weight_ref, values_ref, *refs):
    chosen = selection(rank_ref, experts, slots)
    select = jnp.concatenate([entry.astype(f32) for entry in chosen], axis=0).astype(bf16)
    values = values_ref[...]
    rows = jnp.dot(select, values, preferred_element_type=f32)
    if grads:
        down_ref = refs[0]
        out_ref, weights_ref, act_grad_ref = refs[-3:]
        act_grad_ref[...] = lax.dot_general(
            values, down_ref[...], (((1,), (1,)), ((), ())), preferred_element_type=f32
        )
    else:
        act_grad_ref, weights_in_ref = refs[:2]
        out_ref, act_ref, gu_ref = refs[-3:]
        gate = jnp.dot(values, weights_in_ref[...], preferred_element_type=f32)
        hidden = act_ref.shape[1]
        up = pltpu.roll(gate, hidden, 1)
        sig = sigmoid(gate)
        silu = gate * sig
        d_act = act_grad_ref[...]
        act_ref[...] = (silu * up)[:, :hidden].astype(bf16)
        d_gate = d_act * up * (sig * (1.0 + gate * (1.0 - sig)))
        d_up = pltpu.roll(d_act * silu, hidden, 1)
        lane = lax.broadcasted_iota(jnp.int32, (1, 2 * hidden), 1)
        gu_ref[...] = jnp.where(lane < hidden, d_gate, d_up).astype(bf16)
    for k in range(experts):
        part = rows[k * slots : (k + 1) * slots]
        if grads:
            own = jnp.where(chosen[k], weight_ref[0, k : k + 1, :], 0.0)
            own = jnp.sum(own, axis=1, keepdims=True)
            part = part * own
            weights_ref[k] = jnp.broadcast_to(own, (slots, EXTRA))
        out_ref[k] = part.astype(bf16)


def dispatch(values, rank, weight, experts, slots, first, shared, into=None):
    pairs, _, tokens = rank.shape
    count = values.shape[0] // tokens
    width = values.shape[1]
    grads = len(shared) == 1
    hidden = shared[0].shape[0] if grads else shared[1].shape[1]

    def slots_spec(extent):
        return pl.BlockSpec((experts, slots, extent), lambda step: (0, first + step, 0))

    def rows_spec(extent):
        return pl.BlockSpec((tokens, extent), lambda step: (step, 0))

    rank_spec = pl.BlockSpec((1,) + rank.shape[1:], lambda step: (first + step, 0, 0))
    in_specs = [rank_spec, rank_spec, rows_spec(width)]
    out_specs = [slots_spec(width)]
    shapes = [jax.ShapeDtypeStruct((experts, pairs * slots, width), bf16)]
    small = (values.shape[0], hidden)
    if grads:
        in_specs += [whole(shared[0])]
        out_specs += [slots_spec(EXTRA), rows_spec(hidden)]
        shapes += [
            jax.ShapeDtypeStruct((experts, pairs * slots, EXTRA), f32),
            jax.ShapeDtypeStruct(small, f32),
        ]
    else:
        in_specs += [rows_spec(hidden), whole(shared[1])]
        out_specs += [rows_spec(hidden // 2), rows_spec(hidden)]
        shapes += [jax.ShapeDtypeStruct((small[0], extent), bf16) for extent in (hidden // 2, hidden)]
    aliases = {}
    into = () if into is None else tuple(into)
    for index, entry in enumerate(into):
        aliases[len(in_specs)] = index
        in_specs.append(pl.BlockSpec(memory_space=pl.ANY))
    return pl.pallas_call(
        lambda *refs: dispatch_kernel(experts, slots, grads, *refs),
        grid=(count,),
        in_specs=in_specs,
        out_specs=out_specs,
        out_shape=shapes,
        input_output_aliases=aliases,
        compiler_params=params(),
        cost_estimate=cost(5),
        name="dispatch",
    )(rank, weight, values, *shared, *into)


def combine_kernel(experts, slots, terms, turned, rank_ref, rows_ref, *refs):
    out_ref = refs[-1]
    chosen = selection(rank_ref, experts, slots)
    select = jnp.concatenate([entry.astype(f32) for entry in chosen], axis=0).astype(bf16)
    rows = jnp.concatenate([rows_ref[k] for k in range(experts)], axis=0)
    total = lax.dot_general(select, rows, (((0,), (0,)), ((), ())), preferred_element_type=f32)
    dims = ((1,), (1,)) if turned else ((1,), (0,))
    for k in range(terms):
        total = total + lax.dot_general(
            refs[2 * k][...], refs[2 * k + 1][...], (dims, ((), ())), preferred_element_type=f32
        )
    out_ref[...] = total.astype(bf16)


def combine(rows, rank, terms, slots, first, turned):
    pairs, _, tokens = rank.shape
    experts, _, width = rows.shape
    count = terms[0][0].shape[0] // tokens
    specs, operands = [], []
    for left, right in terms:
        specs += [pl.BlockSpec((tokens, left.shape[1]), lambda step: (step, 0)), whole(right)]
        operands += [left, right]
    return pl.pallas_call(
        lambda *refs: combine_kernel(experts, slots, len(terms), turned, *refs),
        grid=(count,),
        in_specs=[
            pl.BlockSpec((1,) + rank.shape[1:], lambda step: (first + step, 0, 0)),
            pl.BlockSpec((experts, slots, width), lambda step: (0, first + step, 0)),
        ]
        + specs,
        out_specs=pl.BlockSpec((tokens, width), lambda step: (step, 0)),
        out_shape=jax.ShapeDtypeStruct((count * tokens, width), bf16),
        compiler_params=params(),
        cost_estimate=cost(5),
        name="combine",
    )(rank, rows, *operands)


def expert_kernel(
    rows_ref, grad_ref, weight_ref, gate_ref, up_ref, down_ref, act_ref, g_ref, u_ref, back_ref, out_ref
):
    rows, gate_w, up_w, down_w = rows_ref[0], gate_ref[0], up_ref[0], down_ref[0]
    turned = (((1,), (1,)), ((), ()))
    gate = jnp.dot(rows, gate_w, preferred_element_type=f32)
    up = jnp.dot(rows, up_w, preferred_element_type=f32)
    sig = sigmoid(gate)
    silu = gate * sig
    act = (silu * up).astype(bf16)
    d_act = lax.dot_general(grad_ref[0], down_w, turned, preferred_element_type=f32)
    d_gate = (d_act * up * (sig * (1.0 + gate * (1.0 - sig)))).astype(bf16)
    d_up = (d_act * silu).astype(bf16)
    act_ref[0], g_ref[0], u_ref[0] = act, d_gate, d_up
    back = lax.dot_general(d_gate, gate_w, turned, preferred_element_type=f32)
    back = back + lax.dot_general(d_up, up_w, turned, preferred_element_type=f32)
    back_ref[0] = back.astype(bf16)
    out = jnp.dot(act, down_w, preferred_element_type=f32) * weight_ref[0][:, :1]
    out_ref[0] = out.astype(bf16)


def expert_pass(rows, grads, weights, gate, up, down):
    experts, lanes, width = rows.shape
    hidden = gate.shape[2]

    def each(entry):
        return pl.BlockSpec((1,) + entry.shape[1:], lambda step: (step, 0, 0))

    inputs = (rows, grads, weights, gate, up, down)
    small = jax.ShapeDtypeStruct((experts, lanes, hidden), bf16)
    large = jax.ShapeDtypeStruct((experts, lanes, width), bf16)
    outputs = [small] * 3 + [large] * 2
    return pl.pallas_call(
        expert_kernel,
        grid=(experts,),
        in_specs=[each(entry) for entry in inputs],
        out_specs=[each(entry) for entry in outputs],
        out_shape=outputs,
        compiler_params=params(),
        cost_estimate=cost(20),
        name="expert_pass",
    )(*inputs)


def unpack_kernel(half, own, heads, unit, pack_ref, weight_ref, grad_ref, gate_ref, up_ref, sums_ref):
    rows = weight_ref.shape[0]
    lane = lax.broadcasted_iota(jnp.int32, (1, EXTRA), 1)
    low = lane < HEAD_DIM
    groups = 2 * half
    sums = jnp.zeros((rows, EXTRA), f32)

    def tile(index, number):
        return pack_ref[index, :, number * EXTRA : (number + 1) * EXTRA].astype(f32)

    def put(start, value):
        grad_ref[:, start : start + EXTRA] = value
        return value * weight_ref[:, start : start + EXTRA].astype(f32)

    def turn(value, amount):
        amount %= EXTRA
        return pltpu.roll(value, amount, 1) if amount else value

    steps = jnp.zeros((rows, EXTRA), f32)
    shared_b = [jnp.zeros((rows, EXTRA), f32) for _ in range(2 * STATE // EXTRA)]
    for core in range(2):
        for column in range(0, half, 2):
            one, two = 2 * column + core, 2 * column + 2 + core
            values = (tile(one, 2), tile(one, 3), tile(two, 2), tile(two, 3))
            gates = (tile(one, 4), turn(values[1], HEAD_DIM), tile(two, 4), turn(values[3], HEAD_DIM))
            at = core * (INNER // 2) + column * own
            for start, (first, rest, other, other_rest) in ((at, gates), (INNER + at, values)):
                turned = turn(other, HEAD_DIM)
                sums = sums + put(start, first)
                sums = sums + put(start + EXTRA, jnp.where(low, rest, turned))
                sums = sums + put(start + 2 * EXTRA, jnp.where(low, turned, turn(other_rest, HEAD_DIM)))
            for index, place in ((one, column), (two, column + 1)):
                steps = steps + turn(tile(index, 5), core * (HEADS // 2) + place * heads)
                shared_b = [total + tile(index, k) for k, total in enumerate(shared_b)]
    for k, total in enumerate(shared_b):
        sums = sums + put(2 * INNER + k * EXTRA, total)
    at = INNER + CONV_CH
    steps = steps[:, :HEADS]
    grad_ref[:, at : at + HEADS] = steps
    rest = jnp.sum(steps * weight_ref[:, at : at + HEADS].astype(f32), axis=1, keepdims=True)
    sums_ref[...] = jnp.broadcast_to(jnp.sum(sums, axis=1, keepdims=True) + rest, (rows, EXTRA))
    per_tile = EXTRA // unit
    for replica in range(2):
        for start in range(0, groups, per_tile):
            for kind, out_ref in enumerate((gate_ref, up_ref)):
                begin = kind * 2 * unit + replica * unit
                mine = jnp.logical_and(lane >= begin, lane < begin + unit)
                total = jnp.zeros((rows, EXTRA), f32)
                for index in range(start, start + per_tile):
                    part = jnp.where(mine, tile(index, 6), 0.0)
                    total = total + turn(part, (index - start) * unit - begin)
                column = replica * groups * unit + start * unit
                out_ref[:, column : column + EXTRA] = total


def unpack(pack, weight, half, own, heads, unit, hidden_units):
    rows = weight.shape[0]
    shapes = [
        jax.ShapeDtypeStruct((rows, columns), f32)
        for columns in (weight.shape[1], hidden_units, hidden_units, EXTRA)
    ]
    return pl.pallas_call(
        lambda *refs: unpack_kernel(half, own, heads, unit, *refs),
        grid=(1,),
        in_specs=[whole(pack), whole(weight)],
        out_specs=[whole(shape) for shape in shapes],
        out_shape=shapes,
        compiler_params=params(),
        cost_estimate=cost(4),
        name="unpack",
    )(pack, weight)


def local(
    hidden_in,
    cotangent,
    routes,
    route_gates,
    lengths,
    in_proj,
    out_proj,
    conv_weight,
    conv_bias,
    norm_gain,
    mix_gain,
    ffn_gain,
    shared_gate,
    shared_up,
    shared_down,
    expert_gate,
    expert_up,
    expert_down,
    decay_log,
    step_bias,
    skip_gain,
):
    tokens, width = hidden_in.shape
    top = routes.shape[1]
    replicas = lax.axis_size("dp")
    groups = lax.axis_size("z") * 4
    devices = replicas * groups
    core = lax.axis_index("core")
    column = lax.axis_index("z") * 2 + lax.axis_index("y")
    place = column * 2 + core
    heads = HEADS // groups
    own = heads * HEAD_DIM
    half = groups // 2
    rows_in = in_proj.shape[0]
    hidden_units = shared_gate.shape[1]
    unit = hidden_units // devices
    units = hidden_units // groups
    local_experts = expert_gate.shape[0]
    capacity = 2 * tokens * top // (local_experts * groups)
    first_head = core * (HEADS // 2) + column * heads
    first_channel = first_head * HEAD_DIM

    small = (conv_weight.reshape(-1), conv_bias, norm_gain, mix_gain, ffn_gain)
    small_sizes = [entry.shape[0] for entry in small]
    small_lanes = -(-sum(small_sizes) // rows_in)
    small_flat = jnp.concatenate(small)
    small_flat = jnp.pad(small_flat, (0, small_lanes * rows_in - small_flat.shape[0]))

    bounds = jnp.cumsum(lengths[0])
    slot = jnp.arange(tokens, dtype=jnp.int32)
    runs = jnp.sum((slot[:, None] >= bounds[None, : SEQ_SLOTS - 1]).astype(jnp.int32), axis=1)
    live = (runs < SEQ_SLOTS - 1).astype(f32)[:, None]
    starts = jnp.concatenate([jnp.zeros((1,), jnp.int32), bounds[: SEQ_SLOTS - 1].astype(jnp.int32)])
    place_in_run = slot - jnp.sum(jnp.where(runs[:, None] == jnp.arange(SEQ_SLOTS), starts, 0), axis=1)
    beside = [runs.astype(bf16)[:, None], place_in_run.astype(bf16)[:, None], routes.astype(bf16)]
    beside = jnp.concatenate(beside + list(split_three(route_gates)), axis=1)
    beside = jnp.pad(beside, ((0, 0), (0, EXTRA - beside.shape[1])))
    spread = jnp.concatenate([in_proj[:, 2 * INNER :], small_flat.reshape(rows_in, small_lanes)], axis=1)
    spread = jnp.pad(spread, ((0, 0), (0, -spread.shape[1] % EXTRA)))
    spread = dp_gather_rows(spread[None], 0).reshape(replicas * rows_in, -1)
    spread = jnp.pad(spread, ((0, tokens - replicas * rows_in), (0, 0)))
    payload = jnp.concatenate([hidden_in, beside, spread], axis=1)

    def by_place(block):
        block = block.reshape(rows_in, 2, half, own).transpose(2, 1, 0, 3)
        return block.reshape(groups, rows_in, own)

    def by_unit(block):
        block = block.reshape(rows_in, replicas, groups, unit).transpose(2, 0, 1, 3)
        return block.reshape(groups, rows_in, units)

    pack = jnp.concatenate(
        [
            by_place(in_proj[:, :INNER]),
            by_place(in_proj[:, INNER : 2 * INNER]),
            by_unit(shared_gate),
            by_unit(shared_up),
        ],
        axis=2,
    )
    pack = lax.all_to_all(pack, GROUP, split_axis=0, concat_axis=0, tiled=True)

    if replicas == 2:
        both = swap(out_proj, "core")
        both = jnp.concatenate(
            [jnp.where(core == 0, out_proj, both), jnp.where(core == 0, both, out_proj)]
        )
        payload, both = tie(payload, both)
        w_out = jnp.where(lax.axis_index("dp") == core, both, to_channels(both))
    else:
        w_out = lax.dynamic_slice_in_dim(
            lax.all_gather(out_proj, ALL, axis=0, tiled=True), first_channel, own, 0
        )
    def gather_tokens():
        size = lax.axis_size("z")
        block, blocks, pieces = payload, [], []
        arrived = None
        for step in range(size):
            following = ring(block) if step < size - 1 else ()
            near = swap(block, "y")
            if step == 0:
                work = (pack, w_out, w_shared_down)
            elif replicas == 2 and step < 4:
                extent = arrived.shape[0] // 3
                work = swap(after(arrived[(step - 1) * extent : step * extent], block), "dp")
            else:
                work = ()
            following, near, work = tie(following, near, work)
            if step == 0:
                arrived = work[0].reshape(groups * rows_in, -1)
                found = work[1:]
            elif replicas == 2 and step < 4:
                pieces.append(work)
            blocks += [block, near]
            block = following
        near = jnp.concatenate(blocks, axis=0)
        if replicas == 2:
            other = jnp.concatenate(pieces, axis=0)
            mine = lax.axis_index("dp") == 0
            everything = jnp.concatenate(
                [jnp.where(mine, arrived, other), jnp.where(mine, other, arrived)], axis=0
            )
        else:
            everything = lax.all_gather(arrived, "dp", axis=0, tiled=True)
        return near, swap(near, "core"), everything, found

    w_shared_down = dp_gather_rows(shared_down[None], 0).reshape(units, width)
    near, mate, pack, (w_out, w_shared_down) = gather_tokens()
    w_gate, w_up, w_down = (
        lax.all_gather(entry, "dp", axis=1, tiled=True)
        for entry in (expert_gate, expert_up, expert_down)
    )

    table = jnp.concatenate([near[:, width : width + EXTRA], mate[:, width : width + EXTRA]], axis=0)
    routes_all = table[:, 2 : 2 + top].astype(jnp.int32)
    gates_all = join_three([table[:, 2 + k * top : 2 + (k + 1) * top] for k in (1, 2, 3)])
    number = jnp.arange(groups, dtype=jnp.int32)
    back_z = (lax.axis_index("z") - number // 4) % (groups // 4)
    other_y = (number // 2) % 2 != lax.axis_index("y")
    other_core = number % 2 != core
    order = other_core * half + back_z * 2 + other_y

    def blocks_of(entry):
        return entry[:, width + EXTRA :].reshape(half, tokens, -1)[:, : replicas * rows_in]

    spread = jnp.concatenate([blocks_of(near), blocks_of(mate)], axis=0)[order]
    spread, w_gate = tie(spread, w_gate)
    spread = spread.reshape(groups, replicas, rows_in, -1).transpose(1, 0, 2, 3)
    spread = spread.reshape(devices, rows_in, -1)
    small_at = 2 * STATE + HEADS
    small_all = spread[:, :, small_at : small_at + small_lanes].reshape(devices, -1)
    pieces = []
    start = 0
    for size in small_sizes:
        pieces.append(small_all[:, start : start + size].reshape(-1).astype(f32))
        start += size
    conv_w_all = pieces[0].reshape(CONV_CH, KERNEL).T
    conv_b_all, norm_gain_all, mix_gain_all, ffn_gain_all = pieces[1:]
    spread = spread.reshape(devices * rows_in, -1)
    w_step = lax.dynamic_slice_in_dim(spread, 2 * STATE + first_head, heads, 1)
    w_step = jnp.pad(w_step, ((0, 0), (0, EXTRA - heads)))
    w_in = [spread[:, : 2 * STATE], pack[:, own : 2 * own], pack[:, EXTRA:own], pack[:, :EXTRA], w_step]
    w_in = jnp.concatenate(w_in, axis=1)
    w_shared = pack[:, 2 * own :]
    w_shared_wide = jnp.pad(w_shared_down, ((0, units), (0, 0)))

    def own_channels(rows):
        return lax.dynamic_slice_in_dim(rows, first_channel, own, rows.ndim - 1)

    conv = jnp.concatenate([conv_w_all, conv_b_all[None]], axis=0)
    conv = jnp.concatenate([conv[:, INNER:], own_channels(conv)], axis=1)
    conv = jnp.pad(conv, ((0, 8 - conv.shape[0]), (0, CONV_LANES - conv.shape[1])))

    def own_heads(row):
        return lax.dynamic_slice_in_dim(row, first_head, heads, 0)

    def lanes_of(row):
        return jnp.pad(row, (0, WIDE - row.shape[0]))

    rate = -jnp.exp(own_heads(decay_log))
    head = [
        lanes_of(own_heads(step_bias)),
        lanes_of(rate),
        lanes_of(jnp.repeat(own_heads(skip_gain), HEAD_DIM)),
        lanes_of(own_channels(mix_gain_all)),
    ]
    head = jnp.pad(jnp.stack(head), ((0, 4), (0, 0)))
    rate_rows = jnp.broadcast_to(jnp.pad(rate, (0, 8 - heads))[:, None], (8, EXTRA))
    w_out = jnp.pad(w_out, ((0, WIDE - own), (0, 0)))

    input_rows = hidden_in.astype(f32)
    grad_out = cotangent.astype(f32)
    branch = after((grad_out * live).astype(bf16), near)

    pairs = groups // 2
    pair_tokens = 2 * tokens
    pair_slots = 2 * capacity
    numbers = place * local_experts + jnp.arange(local_experts, dtype=jnp.int32)
    named = routes_all[:, None, :] == numbers[None, :, None]
    member = jnp.any(named, axis=2).T.reshape(local_experts, pairs, pair_tokens)
    weight = jnp.sum(jnp.where(named, gates_all[:, None, :], 0.0), axis=2).T
    weight = weight.reshape(local_experts, pairs, pair_tokens)
    below = jnp.triu(jnp.ones((pair_tokens, pair_tokens), bf16))
    rank = matmul(member.astype(bf16), below)
    rank = jnp.where(member, rank.astype(jnp.int32) - 1, -1).transpose(1, 0, 2)
    rank = jnp.pad(rank, ((0, 0), (0, 8 - local_experts), (0, 0)), constant_values=-1)
    weight = jnp.pad(weight.transpose(1, 0, 2), ((0, 0), (0, 8 - local_experts), (0, 0)))
    half_pairs = pairs // 2

    def rows_out(values, first, shared, into=None):
        return dispatch(values, rank, weight, local_experts, pair_slots, first, shared, into)

    mixer = (norm_gain_all[None], w_in, w_out, conv, head)

    def forward(part):
        return lambda token: mixer_forward(after(part, token), width, tokens, *after(mixer, token))

    branch_near, branch_mate, (mixer_set, done_mate, done_near, _) = gather(
        branch, [mixer, forward(mate), forward(near)]
    )
    _, w_in, w_out, conv, head = mixer_set
    normed_mate, proj_mate, mixed_mate, scaled_mate = done_mate
    normed_near, proj_near, mixed_near, scaled_near = done_near
    pairs_sum = scatter_first(mixed_near, mixed_mate)
    mixed_sum, (_, _, w_up, *_) = scatter_last(pairs_sum, [(), (), w_up])
    mix_rms = lax.rsqrt(jnp.sum(mixed_sum[:, width:], axis=1, keepdims=True) / INNER + epsilon)
    mixer_out = mixed_sum[:, :width] * mix_rms
    resid = input_rows + live * mixer_out
    ffn_rms = lax.rsqrt(jnp.mean(resid * resid, axis=1, keepdims=True) + epsilon)
    ffn_hat = resid * ffn_rms

    def grads_near(token):
        return rows_out(after(branch_near, token), 0, (w_shared_wide,))

    done_rows = []

    def grads_mate(token):
        return rows_out(after(branch_mate, token), half_pairs, (w_shared_wide,), done_rows[0])

    def keep(work):
        def kept(token):
            found = work(token)
            done_rows.append(found[:2])
            return found

        return kept

    ffn_near, ffn_mate, ((_, _, act_grad_near), (d_row, slot_weight, act_grad_mate), *_) = gather(
        (ffn_hat * ffn_gain_all).astype(bf16), [keep(grads_near), grads_mate]
    )

    expert_in, shared_near, gu_near = rows_out(ffn_near, 0, (act_grad_near, w_shared))
    expert_in, shared_mate, gu_mate = rows_out(
        ffn_mate, half_pairs, (act_grad_mate, w_shared), (expert_in,)
    )
    act_low, g_low, u_low, d_in_row, expert_row = expert_pass(
        expert_in, d_row, slot_weight, w_gate, w_up, w_down
    )

    half_grad = (((1,), (1,)), ((0,), (0,)))
    grad_down = matmul(act_low, d_row, half_grad).astype(bf16)
    d_in_row, grad_down = tie(d_in_row, grad_down)

    def back_rows(gu, first):
        return combine(d_in_row, rank, ((gu, w_shared),), pair_slots, first, True)

    grad_ffn_mate = back_rows(gu_mate, half_pairs)
    grad_ffn_near = back_rows(gu_near, 0)
    pairs_sum = scatter_first(grad_ffn_near, grad_ffn_mate)

    def leaving_of(part):
        return lambda token: matmul(after(expert_in, token), part, half_grad).astype(bf16)

    grad_ffn, leaving = scatter_last(pairs_sum, [leaving_of(g_low), leaving_of(u_low)])
    grad_down, grad_gate, grad_up = (
        lax.psum_scatter(entry, "dp", scatter_dimension=1, tiled=True)
        for entry in (grad_down, *leaving[:2])
    )

    grad_ffn_gain = jnp.sum(grad_ffn * ffn_hat, axis=0)
    scaled_ffn = grad_ffn * ffn_gain_all
    grad_resid = grad_out + ffn_rms * (
        scaled_ffn - ffn_hat * jnp.mean(scaled_ffn * ffn_hat, axis=1, keepdims=True)
    )
    d_mixer = (grad_resid * live).astype(bf16).astype(f32)
    inner_term = jnp.sum(d_mixer * mixer_out, axis=1, keepdims=True) * mix_rms * mix_rms / INNER
    inner_pack = jnp.pad(jnp.concatenate(split_three(inner_term), axis=1), ((0, 0), (0, EXTRA - 3)))
    d_mixer_pack = jnp.concatenate([(d_mixer * mix_rms).astype(bf16), inner_pack], axis=1)

    def out_rows(shared_act, first):
        def work(token):
            terms = ((shared_act, w_shared_down),)
            return combine(after(expert_row, token), rank, terms, pair_slots, first, False)

        return work

    turned = (((0,), (0,)), ((), ()))

    def of_halves(left, right):
        return matmul(left[0], right[0], turned) + matmul(left[1], right[1], turned)

    def shared_grads_of(token):
        halves = after(((branch_near, branch_mate), (ffn_near, ffn_mate)), token)
        return (
            of_halves((shared_near, shared_mate), halves[0]),
            of_halves(halves[1], (gu_near, gu_mate)),
        )

    d_mixer_near, d_mixer_mate, (out_mate, out_near, shared_grads, grad_down) = gather(
        d_mixer_pack,
        [
            out_rows(shared_mate, half_pairs),
            out_rows(shared_near, 0),
            shared_grads_of,
            lambda token: after(grad_down, token).astype(f32),
        ],
    )
    grad_shared_down, grad_shared_gu = shared_grads
    grad_out_rows = of_halves(
        (scaled_near, scaled_mate), (d_mixer_near[:, :width], d_mixer_mate[:, :width])
    )[:own]
    out_rows_low = grad_out_rows.astype(bf16)
    out_pairs = scatter_first(out_near, out_mate)
    (d_mixer_near, d_mixer_mate), out_pairs, out_rows_low = tie(
        (d_mixer_near, d_mixer_mate), out_pairs, out_rows_low
    )

    def backward(grads, part, proj, first, into=()):
        return mixer_backward(
            grads, part, proj, width, tokens, w_in, w_out, conv, head, rate_rows, first, into
        )

    def towards(step):
        return swap(out_pairs[step][1], "y")

    def window(work, *others):
        return tie(work, *others)

    part_one = backward(d_mixer_mate, mate, proj_mate, 0)
    out_there = {1: towards(1), 2: towards(2)}
    part_one, out_there, out_pairs, d_mixer_mate = window(part_one, out_there, out_pairs, d_mixer_mate)
    done_mate = backward(d_mixer_mate, mate, proj_mate, 1, part_one[:2])
    out_total = ring_step(add_low(out_pairs[1][0], out_there[1]), out_pairs, out_there, 1)
    out_there[3] = towards(3)
    done_mate, out_total, out_there, out_pairs, d_mixer_near = window(
        done_mate, out_total, out_there, out_pairs, d_mixer_near
    )
    part_two = backward(d_mixer_near, near, proj_near, 0)
    moved = swap(done_mate[0], "core")
    out_total = ring_step(out_total, out_pairs, out_there, 2)
    out_there[0] = towards(0)
    part_two, moved, out_total, out_there, out_pairs, d_mixer_near = window(
        part_two, moved, out_total, out_there, out_pairs, d_mixer_near
    )
    out_rows_there = from_channels(after(out_rows_low, part_two[0])) if replicas == 2 else ()
    done_near = backward(d_mixer_near, near, proj_near, 1, part_two[:2])
    branch_sum = ring_step(out_total, out_pairs, out_there, 3)
    done_near, branch_sum, grad_gate = window(done_near, branch_sum, grad_gate)
    grad_shared_gu = dp_scatter_rows(grad_shared_gu, 0, done_near[0])
    grad_shared_down = dp_scatter_rows(grad_shared_down.reshape(replicas, unit, width), 0, done_near[0])[0]
    normed_grad_mate, proj_low_mate = done_mate[:2]
    normed_grad_near, proj_low_near = done_near[:2]
    conv_parts = [part_one[2], done_mate[2], part_two[2], done_near[2]]
    head_parts = [part_one[3], done_mate[3], part_two[3], done_near[3]]
    pairs_sum = scatter_first(normed_grad_near, normed_grad_mate, moved)

    def to_owner(part):
        rows_part = jnp.zeros((part.shape[0], CONV_CH), f32)
        values = part[:, 2 * STATE : 2 * STATE + own]
        rows_part = lax.dynamic_update_slice_in_dim(rows_part, values, first_channel, 1)
        rows_part = lax.dynamic_update_slice_in_dim(rows_part, part[:, : 2 * STATE], INNER, 1)
        return rows_part.reshape(part.shape[0], devices, -1).transpose(1, 0, 2).reshape(devices, -1)

    def head_row(part):
        return lax.dynamic_update_slice_in_dim(jnp.zeros((HEADS,), f32), part, first_head, 0)

    def small_sums(conv_grads, head_grads):
        head_grads = jnp.sum(head_grads.reshape(3, 8, EXTRA)[:, :heads], axis=2)
        head_rows = [head_row(entry) for entry in (head_grads[0] * rate, *head_grads[1:])]
        return jnp.concatenate(
            [
                to_owner(conv_grads[: KERNEL + 1]),
                grad_ffn_gain.reshape(devices, -1),
                jnp.broadcast_to(jnp.concatenate(head_rows)[None], (devices, 3 * HEADS)),
            ],
            axis=1,
        )

    crossing = replicas == 2
    here = lax.axis_index("dp")
    normed_rows = width // 2 if crossing else width

    def input_grad(where, token):
        parts = after((normed_near, normed_mate), token)
        if crossing:
            parts = [lax.dynamic_slice_in_dim(part, where * normed_rows, normed_rows, 1) for part in parts]
        return of_halves(parts, (proj_low_near, proj_low_mate))

    def piece(array, index, token):
        extent = array.shape[0] // 2
        return swap(after(array[index * extent : (index + 1) * extent], token), "dp")

    pieces = []

    def small_work(token):
        parts = after((conv_parts, head_parts), token)
        return small_sums(sum(parts[0]), sum(parts[1]))

    there = scatter_beside(pairs_sum)
    total = add_low(pairs_sum[1][0], there[1])
    total, leaving, out_rows_there = tie(
        total, input_grad(1 - here, pairs_sum).astype(bf16), out_rows_there
    )
    finished = []
    works = (lambda token: input_grad(here, token), small_work, lambda token: grad_up)
    for index, work in enumerate(works):
        following = ring_step(total, pairs_sum, there, index + 1)
        if crossing and index < 2:
            pieces.append(piece(leaving, index, total))
        last = index == len(works) - 1
        total, arrived, result = tie(following, tuple(pieces) if last else (), work(total))
        finished.append(result)
    grad_w_in, sums, grad_up = finished
    pieces = list(arrived)
    grad_normed = total
    output = (resid + live * branch_sum).astype(bf16)

    if crossing:
        grad_w_in = grad_w_in + jnp.concatenate(pieces, axis=0).astype(f32)
    else:
        grad_w_in = lax.psum_scatter(leaving, "dp", scatter_dimension=0, tiled=True)
    grad_pack = jnp.concatenate([grad_w_in.astype(bf16), grad_shared_gu.astype(bf16)], axis=1)
    grad_pack = grad_pack.reshape(groups, rows_in, -1)
    grad_gate, grad_up = (entry.astype(f32) for entry in after((grad_gate, grad_up), grad_pack))
    grad_pack = lax.all_to_all(grad_pack, GROUP, split_axis=0, concat_axis=0, tiled=True)

    def from_place(block):
        block = block.reshape(half, 2, rows_in, block.shape[2]).transpose(2, 1, 0, 3)
        return block.reshape(rows_in, -1)

    def from_unit(block):
        block = block.reshape(groups, rows_in, replicas, unit).transpose(1, 2, 0, 3)
        return block.reshape(rows_in, hidden_units)

    if replicas == 2:
        grad_in_proj, grad_shared_gate, grad_shared_up, gain_sums = unpack(
            grad_pack, in_proj, half, own, heads, unit, hidden_units
        )
        gain_sums = gain_sums[:, 0]
    else:
        grad_pack = grad_pack.astype(f32)
        value_at, gate_at, step_at = 2 * STATE, CONV_LANES, CONV_LANES + EXTRA
        gate_part = [grad_pack[:, :, gate_at : gate_at + EXTRA], grad_pack[:, :, value_at + own : gate_at]]
        grad_in_proj = jnp.concatenate(
            [
                from_place(jnp.concatenate(gate_part, axis=2)),
                from_place(grad_pack[:, :, value_at : value_at + own]),
                jnp.sum(grad_pack[:, :, : 2 * STATE], axis=0),
                from_place(grad_pack[:, :, step_at : step_at + heads]),
            ],
            axis=1,
        )
        grad_shared_gate = from_unit(grad_pack[:, :, PROJ_LANES : PROJ_LANES + units])
        grad_shared_up = from_unit(grad_pack[:, :, PROJ_LANES + units :])
        gain_sums = jnp.sum(grad_in_proj * in_proj.astype(f32), axis=1)
    if replicas == 2:
        mine = lax.axis_index("dp") == core
        total = (grad_out_rows + out_rows_there.astype(f32)).reshape(2, own // 2, width)
        passed = swap(lax.dynamic_index_in_dim(total, 1 - core, 0, keepdims=False), "core")
        grad_out_proj = jnp.where(mine, lax.dynamic_index_in_dim(total, core, 0, keepdims=False), passed)
    else:
        full = jnp.zeros((INNER, width), f32)
        full = lax.dynamic_update_slice_in_dim(full, grad_out_rows, first_channel, 0)
        grad_out_proj = lax.psum_scatter(full, ALL, scatter_dimension=0, tiled=True)
    grad_mix_gain = jnp.sum(grad_out_proj * out_proj.astype(f32), axis=1) / mix_gain.astype(f32)
    grad_norm_gain = gain_sums / norm_gain.astype(f32)

    sums = lax.all_to_all(sums, ALL, split_axis=0, concat_axis=0, tiled=True)
    sums = jnp.sum(sums, axis=0)
    channels = CONV_CH // devices
    grad_conv_weight = sums[: KERNEL * channels].reshape(KERNEL, channels).T
    grad_conv_bias = sums[KERNEL * channels : (KERNEL + 1) * channels]
    at = (KERNEL + 1) * channels
    grad_ffn_gain = sums[at : at + rows_in]
    at += rows_in
    grad_decay, grad_stepb, grad_skip = (sums[at + k * HEADS : at + (k + 1) * HEADS] for k in range(3))

    in_rms = lax.rsqrt(jnp.mean(input_rows * input_rows, axis=1, keepdims=True) + epsilon)
    in_hat = input_rows * in_rms
    scaled_in = grad_normed * norm_gain_all
    grad_input = grad_resid + in_rms * (
        scaled_in - in_hat * jnp.mean(scaled_in * in_hat, axis=1, keepdims=True)
    )
    return (
        output,
        grad_input,
        grad_in_proj,
        grad_out_proj,
        grad_conv_weight,
        grad_conv_bias,
        grad_norm_gain,
        grad_mix_gain,
        grad_ffn_gain,
        grad_shared_gate,
        grad_shared_up,
        grad_shared_down,
        grad_gate,
        grad_up,
        grad_down,
        grad_decay,
        grad_stepb,
        grad_skip,
    )


def solution(mesh):
    replicas, groups = mesh.shape["dp"], mesh.shape["expert"]
    inner = Mesh(mesh.devices.reshape(replicas, groups // 4, 2, 2), ALL)
    flat = P(ALL)
    expert = P(GROUP, "dp", None)
    return jax.shard_map(
        local,
        mesh=inner,
        in_specs=(flat,) * 15 + (expert,) * 3 + (P(),) * 3,
        out_specs=(flat,) * 12 + (expert,) * 3 + (P(),) * 3,
        check_vma=False,
    )
```
